32 devices in a mesh: dp: 4 (over y, x), seq: 8 (over z, core).
Axes of the slice: x: 2, y: 2, z: 4, core: 2. Of those that a mesh axis runs over, the one named last changes fastest.
Arguments:
- series: bfloat16 [4, 4096, 128], P('dp', 'seq'), may hold values from -6 to 6
- cotangent: bfloat16 [4, 4096, 128], P('dp', 'seq'), may hold values from -6 to 6
- w_in: bfloat16 [128, 384], replicated, may hold values from -0.5 to 0.5
- w_out: bfloat16 [128, 128], replicated, may hold values from -0.5 to 0.5
- taps: float32 [3, 384], replicated, may hold values from -3 to 3
- skip_one: float32 [128], replicated, may hold values from 0.5 to 1.5
- skip_two: float32 [128], replicated, may hold values from 0.5 to 1.5
- filter_one: float32 [8, 4096], P(None, 'seq'), may hold values from -0.09375 to 0.09375
- filter_two: float32 [8, 4096], P(None, 'seq'), may hold values from -0.09375 to 0.09375
Outputs:
- output: bfloat16 [4, 4096, 128], P('dp', 'seq')
- d_series: bfloat16 [4, 4096, 128], P('dp', 'seq')
- grad_w_in: float32 [128, 384], replicated
- grad_w_out: float32 [128, 128], replicated
- grad_taps: float32 [3, 384], replicated
- grad_skip_one: float32 [128], replicated
- grad_skip_two: float32 [128], replicated
- grad_filter_one: float32 [8, 4096], P(None, 'seq')
- grad_filter_two: float32 [8, 4096], P(None, 'seq')
The draws below stay inside these ranges and needn't reach their ends.
All inputs are finite; a program needn't handle non-finite values.
Results may differ from the reference program's by a relative error of at most 0.015.
Values may be sent and summed in bfloat16 or wider, within the bound.
No kernel may reach another device: no remote copies, remote signals or barrier semaphores. Data moves between devices by JAX's collectives and lax.ppermute only.
A program may use at most 128 MiB of HBM per device.

```python
import jax
import jax.numpy as jnp
from jax import lax

D = 128
FILTERS = 8
L = 4096
SERIES = 4


def level_of(stream_key, extent, pieces, smallest, largest):
    def one(dim, shards_of):
        draws = jax.random.uniform(jax.random.fold_in(jax.random.fold_in(stream_key, 6), dim), (shards_of,), jnp.float32, smallest / len(pieces), largest / len(pieces))
        return jnp.repeat(jnp.exp(draws), extent[dim] // shards_of).reshape((-1,) + (1,) * (len(extent) - dim - 1))

    gain = one(*pieces[0])
    for cut in pieces[1:]:
        gain = gain * one(*cut)
    return gain


def bell_draw(rng, shape, spread, bound, cuts=(), held_as=jnp.bfloat16):
    values = spread * jax.random.normal(rng, shape, jnp.float32)
    if cuts:
        values = values * level_of(rng, shape, cuts, -0.22, 0.18)
    return jnp.clip(values, -bound, bound).astype(held_as)


def setup_inputs(seed: int = 0) -> dict:
    seeds = jax.random.split(jax.random.key(seed), 10)
    return {
        "series": bell_draw(seeds[0], (SERIES, L, D), 1.0, 6.0, ((0, 4), (1, 8))),
        "cotangent": bell_draw(seeds[1], (SERIES, L, D), 1.0, 6.0, ((0, 4), (1, 8))),
        "w_in": bell_draw(seeds[2], (D, 3 * D), D ** -0.5, 0.5),
        "w_out": bell_draw(seeds[3], (D, D), D ** -0.5, 0.5),
        "taps": bell_draw(seeds[4], (3, 3 * D), 0.6, 3.0, (), jnp.float32),
        "skip_one": jnp.clip(jax.random.uniform(seeds[5], (D,), jnp.float32, 0.5, 1.5), 0.5, 1.5),
        "skip_two": jnp.clip(jax.random.uniform(seeds[6], (D,), jnp.float32, 0.5, 1.5), 0.5, 1.5),
        "filter_one": bell_draw(seeds[7], (FILTERS, L), L ** -0.5, 0.09375, ((1, 8),), jnp.float32),
        "filter_two": bell_draw(seeds[8], (FILTERS, L), L ** -0.5, 0.09375, ((1, 8),), jnp.float32),
    }


def filter_spectrum(filter_rows, channels, length):
    spectral = jnp.fft.rfft(filter_rows, n=2 * length, axis=1)
    return jnp.repeat(spectral.T, channels // filter_rows.shape[0], axis=1)[None]

def causal_conv(filter_rows, field, length):
    spectral = jnp.fft.rfft(field, n=2 * length, axis=1) * filter_spectrum(filter_rows, field.shape[2], length)
    return jnp.fft.irfft(spectral, n=2 * length, axis=1)[:, :length]

def anticausal_conv(filter_rows, field, length):
    spectral = jnp.fft.rfft(field, n=2 * length, axis=1) * jnp.conj(filter_spectrum(filter_rows, field.shape[2], length))
    return jnp.fft.irfft(spectral, n=2 * length, axis=1)[:, :length]

def filter_gradient(grad_field, field, filters, length):
    spectral = jnp.fft.rfft(grad_field, n=2 * length, axis=1) * jnp.conj(jnp.fft.rfft(field, n=2 * length, axis=1))
    series_count, bins, channels = spectral.shape
    spectral = lax.optimization_barrier(jnp.sum(spectral.reshape(series_count, bins, filters, channels // filters), axis=(0, 3)))
    return jnp.fft.irfft(spectral, n=2 * length, axis=0)[:length].T

def reference(series, cotangent, w_in, w_out, taps, skip_one, skip_two, filter_one, filter_two):
    highest = lax.Precision.HIGHEST
    width_d = series.shape[2]
    filters = filter_one.shape[0]
    series_wide = series.astype(jnp.float32)
    cot_wide = cotangent.astype(jnp.float32)
    projected = jnp.einsum('etd,dc->etc', series_wide, w_in.astype(jnp.float32), precision=highest)
    padded = jnp.pad(projected, ((0, 0), (2, 0), (0, 0)))
    convolved = taps[0] * padded[:, 2:] + taps[1] * padded[:, 1:-1] + taps[2] * padded[:, :-2]
    value_part = convolved[..., :width_d]
    gate_one = convolved[..., width_d:2 * width_d]
    gate_two = convolved[..., 2 * width_d:]
    y_one = causal_conv(filter_one, value_part, L) + skip_one * value_part
    gated_mid = gate_one * y_one
    y_two = causal_conv(filter_two, gated_mid, L) + skip_two * gated_mid
    product = (gate_two * y_two).astype(jnp.bfloat16)
    output = jnp.einsum('etc,cd->etd', product.astype(jnp.float32), w_out.astype(jnp.float32), precision=highest).astype(jnp.bfloat16)
    d_product = jnp.einsum('etd,cd->etc', cot_wide, w_out.astype(jnp.float32), precision=highest)
    grad_two = d_product * gate_two
    d_gate_two = d_product * y_two
    d_mid = anticausal_conv(filter_two, grad_two, L) + skip_two * grad_two
    grad_one = d_mid * gate_one
    d_gate_one = d_mid * y_one
    d_value = anticausal_conv(filter_one, grad_one, L) + skip_one * grad_one
    d_convolved = jnp.concatenate([d_value, d_gate_one, d_gate_two], axis=2)
    padded_back = jnp.pad(d_convolved, ((0, 0), (0, 2), (0, 0)))
    d_projected = (taps[0] * padded_back[:, :-2] + taps[1] * padded_back[:, 1:-1] + taps[2] * padded_back[:, 2:]).astype(jnp.bfloat16)
    d_series = jnp.einsum('etc,dc->etd', d_projected.astype(jnp.float32), w_in.astype(jnp.float32), precision=highest).astype(jnp.bfloat16)
    grad_scale = 1.0 / jnp.sqrt(jnp.float32(SERIES * L))
    grad_w_in = grad_scale * jnp.einsum('etd,etc->dc', series_wide, d_projected.astype(jnp.float32), precision=highest)
    grad_w_out = grad_scale * jnp.einsum('etc,etd->cd', product.astype(jnp.float32), cot_wide, precision=highest)
    grad_taps = grad_scale * jnp.stack([lax.optimization_barrier(jnp.sum(d_convolved * padded[:, 2 - offset:2 - offset + L], axis=(0, 1))) for offset in range(3)])
    grad_skip_one = grad_scale * lax.optimization_barrier(jnp.sum(grad_one * value_part, axis=(0, 1)))
    grad_skip_two = grad_scale * lax.optimization_barrier(jnp.sum(grad_two * gated_mid, axis=(0, 1)))
    grad_filter_one = grad_scale * filter_gradient(grad_one, value_part, filters, L)
    grad_filter_two = grad_scale * filter_gradient(grad_two, gated_mid, filters, L)
    return (output, d_series, grad_w_in, grad_w_out, grad_taps, grad_skip_one, grad_skip_two, grad_filter_one, grad_filter_two)
```

```python
import functools
import math

import jax
import jax.numpy as jnp
from jax import lax
from jax.experimental import pallas as pl
from jax.experimental.pallas import tpu as pltpu
from jax.sharding import PartitionSpec as P

W = 256
F32 = jnp.float32
BF16 = jnp.bfloat16
NT = (((1,), (1,)), ((), ()))
VMEM_LIMIT = 56 * 1024 * 1024


def call(body, out_shape, scratch=(), flops=0, moved=0):
    return pl.pallas_call(
        body,
        out_shape=out_shape,
        scratch_shapes=list(scratch),
        compiler_params=pltpu.CompilerParams(vmem_limit_bytes=VMEM_LIMIT),
        cost_estimate=pl.CostEstimate(flops=flops, bytes_accessed=moved, transcendentals=0),
    )


def dot(a, b):
    return jnp.dot(a, b, preferred_element_type=F32)


def dot_nt(a, b):
    return lax.dot_general(a, b, NT, preferred_element_type=F32)


def project_kernel(units, series_ref, cot_ref, w_in_ref, w_out_ref, out_ref):
    count, block, width = series_ref.shape
    group = width // units
    parts = block // W
    w_in_t = w_in_ref[...].T
    w_out = w_out_ref[...]
    for e in range(count):
        for part in range(parts):
            rows = pl.ds(part * W, W)
            proj = dot_nt(w_in_t, series_ref[e, rows, :]).astype(BF16)
            d_prod = dot_nt(w_out, cot_ref[e, rows, :]).astype(BF16)
            for kind in range(4):
                field = proj[kind * width : (kind + 1) * width] if kind < 3 else d_prod
                out_ref[
                    e * units : (e + 1) * units,
                    (kind * parts + part) * group : (kind * parts + part + 1) * group,
                    :,
                ] = field.reshape(units, group, W)


def toeplitz_kernel(taps_ref, out_ref, base_ref):
    sources, chunk_rows, lanes = taps_ref.shape
    chunks = chunk_rows // 2
    length = sources * chunks * lanes
    blocks = length // W
    row = lax.broadcasted_iota(jnp.int32, (8, length), 0)
    for m in range(2):
        for s in range(sources):
            for q in range(chunks):
                at = (s * chunks + q) * lanes
                base_ref[:, at : at + lanes] = jnp.broadcast_to(
                    taps_ref[s, m * chunks + q : m * chunks + q + 1, :], (8, lanes)
                )
        base = base_ref[...]
        for bit in (1, 2, 4):
            base = jnp.where((row & bit) != 0, pltpu.roll(base, bit, 1), base)

        def step(q, base, m=m):
            start = pl.multiple_of(q * 16, 16)
            both = jnp.concatenate([base, pltpu.roll(base, 8, 1)], axis=0)
            b = lax.broadcasted_iota(jnp.int32, (16, W), 0) + start
            r = lax.broadcasted_iota(jnp.int32, (16, W), 1)
            first = jnp.where(r >= b, both[:, :W], 0.0)
            out_ref[m, 0, pl.ds(start, 16), :] = first.astype(BF16)
            for d in range(1, blocks):
                out_ref[m, d, pl.ds(start, 16), :] = both[:, d * W : (d + 1) * W].astype(BF16)
            return pltpu.roll(base, 16, 1)

        lax.fori_loop(0, W // 16, step, base)


def earlier(field, j, group):
    if j == 0:
        return field
    turned = pltpu.roll(field, j, 1)
    above = jnp.concatenate([jnp.zeros((group, W), F32), turned[:-group]], axis=0)
    lane = lax.broadcasted_iota(jnp.int32, field.shape, 1)
    return jnp.where(lane < j, above, turned)


def later(field, j, group):
    if j == 0:
        return field
    turned = pltpu.roll(field, W - j, 1)
    below = jnp.concatenate([turned[group:], jnp.zeros((group, W), F32)], axis=0)
    lane = lax.broadcasted_iota(jnp.int32, field.shape, 1)
    return jnp.where(lane >= W - j, below, turned)


def own_lanes(f, group, width):
    lane = lax.broadcasted_iota(jnp.int32, (group, width), 1)
    channel = lax.broadcasted_iota(jnp.int32, (group, width), 0)
    return lane == f * group + channel


def pick(ref, kind, received):
    rows = received // 4
    field = ref[:, kind * rows : (kind + 1) * rows, :]
    return field.reshape(field.shape[0] * rows, W).astype(F32)


def operator_kernel(
    units, fields_ref, toep_ref, taps_ref, skip_one_ref, skip_two_ref, out_ref, kept_ref, pad_ref
):
    sources, received, _ = fields_ref.shape
    width = taps_ref.shape[1] // 3
    group = width // units
    rows = sources * received // 4
    blocks = rows // group
    f = lax.rem(lax.axis_index("seq"), units)
    mine = own_lanes(f, group, width)

    def column(values):
        col = jnp.sum(jnp.where(mine, values, 0.0), axis=1, keepdims=True)
        return jnp.broadcast_to(col, (group, W))

    def scaled(field, col):
        return (field.reshape(blocks, group, W) * col[None]).reshape(rows, W)

    zeros = jnp.zeros((rows, W), BF16)
    pad_ref[0:rows, :] = zeros
    pad_ref[2 * rows : 3 * rows, :] = zeros

    def causal(m, field):
        pad_ref[rows : 2 * rows, :] = field
        left = jnp.concatenate(
            [pad_ref[rows - group * d : 2 * rows - group * d, :] for d in range(blocks)], axis=1
        )
        return dot(left, toep_ref[m].reshape(blocks * W, W))

    def anticausal(m, field):
        pad_ref[rows : 2 * rows, :] = field
        left = jnp.concatenate(
            [pad_ref[rows + group * d : 2 * rows + group * d, :] for d in range(blocks)], axis=1
        )
        right = jnp.concatenate([toep_ref[m, d] for d in range(blocks)], axis=1)
        return dot_nt(left, right)

    tap = [
        [
            column(taps_ref[j : j + 1, kind * width : (kind + 1) * width])
            for j in range(3)
        ]
        for kind in range(3)
    ]
    skip_one = column(skip_one_ref[...])
    skip_two = column(skip_two_ref[...])

    def short(kind):
        field = pick(fields_ref, kind, received)
        total = scaled(field, tap[kind][0])
        for j in (1, 2):
            total = total + scaled(earlier(field, j, group), tap[kind][j])
        return total

    def keep(slot, field):
        low = field.astype(BF16)
        kept_ref[slot] = low
        return low

    def send(kind, field):
        part_rows = received // 4
        out_ref[:, kind * part_rows : (kind + 1) * part_rows, :] = field.astype(BF16).reshape(
            sources, part_rows, W
        )

    def send_back(kind, field):
        total = scaled(field, tap[kind][0])
        for j in (1, 2):
            total = total + scaled(later(field, j, group), tap[kind][j])
        send(kind, total)

    value = short(0)
    y_one = causal(0, keep(0, value)) + scaled(value, skip_one)
    gate_one = short(1)
    mid = gate_one * y_one
    y_two = causal(1, keep(1, mid)) + scaled(mid, skip_two)
    gate_two = short(2)
    send(3, gate_two * y_two)
    d_product = pick(fields_ref, 3, received)
    grad_two = d_product * gate_two
    d_gate_two = d_product * y_two
    keep(6, d_gate_two)
    send_back(2, d_gate_two)
    d_mid = anticausal(1, keep(3, grad_two)) + scaled(grad_two, skip_two)
    grad_one = d_mid * gate_one
    d_gate_one = d_mid * y_one
    keep(5, d_gate_one)
    send_back(1, d_gate_one)
    d_value = anticausal(0, keep(2, grad_one)) + scaled(grad_one, skip_one)
    keep(4, d_value)
    send_back(0, d_value)


def gradient_kernel(
    units,
    fields_ref,
    sent_ref,
    kept_ref,
    series_ref,
    cot_ref,
    out_ref,
    pad_ref,
    corr_ref,
    total_ref,
):
    sources, received, _ = fields_ref.shape
    width = series_ref.shape[3]
    group = width // units
    rows = sources * received // 4
    blocks = rows // group
    parts = blocks // sources
    length = blocks * W
    me = lax.axis_index("seq")
    f = lax.rem(me, units)
    e = me // units
    mine = own_lanes(f, group, width)

    def wide(ref):
        return jnp.concatenate([ref[s, e] for s in range(sources)], axis=0)

    def long_rows(kind):
        return jnp.concatenate(
            [
                sent_ref[s, (kind * parts + p) * group : (kind * parts + p + 1) * group, :]
                for s in range(sources)
                for p in range(parts)
            ],
            axis=1,
        )

    left = jnp.concatenate([long_rows(k) for k in range(3)], axis=0)
    total_ref[0 : 3 * group, :] = dot(left, wide(series_ref))
    total_ref[3 * group : 4 * group, :] = dot(long_rows(3), wide(cot_ref))

    zeros = jnp.zeros((rows, W), BF16)
    pad_ref[rows : 2 * rows, :] = zeros
    row8 = lax.broadcasted_iota(jnp.int32, (8, length), 0)
    for m in range(2):
        pad_ref[0:rows, :] = kept_ref[2 + m]
        right = jnp.concatenate(
            [pad_ref[group * d : rows + group * d, :] for d in range(blocks)], axis=1
        )
        held = kept_ref[m].astype(F32).T.astype(BF16)
        corr_ref[...] = dot(held, right)
        b = lax.broadcasted_iota(jnp.int32, (W, W), 0)
        r = lax.broadcasted_iota(jnp.int32, (W, W), 1)
        corr_ref[:, 0:W] = jnp.where(r >= b, corr_ref[:, 0:W], 0.0)

        def step(i, acc):
            start = pl.multiple_of((W // 8 - 1 - i) * 8, 8)
            return pltpu.roll(acc, length - 8, 1) + corr_ref[pl.ds(start, 8), :]

        acc = lax.fori_loop(0, W // 8, step, jnp.zeros((8, length), F32))
        for bit in (1, 2, 4):
            acc = jnp.where((row8 & bit) != 0, pltpu.roll(acc, length - bit, 1), acc)
        line = jnp.sum(acc, axis=0, keepdims=True)
        for q in range(length // width):
            at = 4 * group + m * (length // width) + q
            total_ref[at : at + 1, :] = line[:, q * width : (q + 1) * width]

    def spread(products):
        by_channel = jnp.sum(products.reshape(blocks, group, W), axis=0)
        col = jnp.sum(by_channel, axis=1, keepdims=True)
        return jnp.sum(jnp.where(mine, col, 0.0), axis=0, keepdims=True)

    small = []
    for j in range(3):
        for kind in range(3):
            field = pick(fields_ref, kind, received)
            small.append(spread(kept_ref[4 + kind].astype(F32) * earlier(field, j, group)))
    for m in range(2):
        small.append(spread(kept_ref[2 + m].astype(F32) * kept_ref[m].astype(F32)))
    base = 4 * group + 2 * (length // width)
    total_ref[base : base + 16, :] = jnp.zeros((16, width), F32)
    for n, line in enumerate(small):
        total_ref[base + n : base + n + 1, :] = line

    total = total_ref[...].astype(BF16)
    for i in range(out_ref.shape[0]):
        out_ref[i] = total


def spread_kernel(units, in_ref, out_ref, sum_ref):
    width = in_ref.shape[2]
    group = width // units
    targets = out_ref.shape[0]
    total = in_ref[0].astype(F32)
    for i in range(1, in_ref.shape[0]):
        total = total + in_ref[i].astype(F32)
    sum_ref[...] = total
    base = 4 * group
    lines = (total.shape[0] - base - 16) // 2
    each = lines // targets
    for s in range(targets):
        out_ref[s] = jnp.concatenate(
            [
                sum_ref[0:base, :],
                sum_ref[base + s * each : base + (s + 1) * each, :],
                sum_ref[base + lines + s * each : base + lines + (s + 1) * each, :],
                sum_ref[base + 2 * lines : base + 2 * lines + 16, :],
                jnp.zeros((16 - 2 * each, width), F32),
            ],
            axis=0,
        ).astype(BF16)


def parameter_kernel(
    units, scale, in_ref, w_in_ref, w_out_ref, taps_ref, skip_one_ref, skip_two_ref, one_ref, two_ref
):
    sources, _, width = in_ref.shape
    group = width // units
    count = sources // units
    each = one_ref.shape[1] // width

    def total(first, last):
        parts = [in_ref[e * units : (e + 1) * units, first:last, :] for e in range(count)]
        result = parts[0].astype(F32)
        for part in parts[1:]:
            result = result + part.astype(F32)
        return result

    blocks = total(0, 4 * group) * scale
    for kind in range(3):
        rows = blocks[:, kind * group : (kind + 1) * group, :].reshape(width, width)
        w_in_ref[:, kind * width : (kind + 1) * width] = rows.T
    w_out_ref[...] = blocks[:, 3 * group : 4 * group, :].reshape(width, width)
    rest = total(4 * group, in_ref.shape[1]) * scale
    filters = one_ref.shape[0]
    for q in range(each):
        for ref, at in ((one_ref, q), (two_ref, each + q)):
            by_unit = rest[:, at, :].reshape(filters, units // filters, width)
            ref[:, q * width : (q + 1) * width] = jnp.sum(by_unit, axis=1)
    small = jnp.sum(rest[:, 2 * each : 2 * each + 16, :], axis=0)
    for j in range(3):
        for kind in range(3):
            n = 3 * j + kind
            taps_ref[j : j + 1, kind * width : (kind + 1) * width] = small[n : n + 1]
    skip_one_ref[...] = small[9:10]
    skip_two_ref[...] = small[10:11]


def output_kernel(units, in_ref, w_in_ref, w_out_ref, out_ref, d_series_ref):
    count, block, width = out_ref.shape
    group = width // units
    parts = block // W
    w_in = w_in_ref[...]
    w_out_t = w_out_ref[...].T

    def field(e, kind, part):
        at = (kind * parts + part) * group
        return in_ref[e * units : (e + 1) * units, at : at + group, :].reshape(width, W)

    for e in range(count):
        for part in range(parts):
            rows = pl.ds(part * W, W)
            out_ref[e, rows, :] = dot(w_out_t, field(e, 3, part)).T.astype(BF16)
            grads = jnp.concatenate([field(e, kind, part) for kind in range(3)], axis=0)
            d_series_ref[e, rows, :] = dot(w_in, grads).T.astype(BF16)


def all_to_all(blocks, axis):
    return lax.all_to_all(blocks, axis, split_axis=0, concat_axis=0, tiled=True)


def shards(series, cotangent, w_in, w_out, taps, skip_one, skip_two, filter_one, filter_two):
    count, block, width = series.shape
    filters = filter_one.shape[0]
    sources = lax.axis_size("seq")
    copies = lax.axis_size("dp")
    length = block * sources
    units = sources // count
    group = width // units
    assert sources == count * units and units % filters == 0 and block % W == 0
    blocks = length // W
    rows = blocks * group
    scale = 1.0 / math.sqrt(count * copies * length)
    shape = jax.ShapeDtypeStruct

    slices = jnp.concatenate(
        [
            filter_one.reshape(filters, block // width, width),
            filter_two.reshape(filters, block // width, width),
        ],
        axis=1,
    )
    slices = jnp.concatenate([jnp.repeat(slices, units // filters, axis=0)] * count, axis=0)
    lines = all_to_all(slices, "seq")

    all_series = lax.all_gather(series, "seq")
    all_cot = lax.all_gather(cotangent, "seq")

    packed = 4 * (block // W) * group
    fields = call(
        functools.partial(project_kernel, units),
        shape((sources, packed, W), BF16),
        flops=2 * count * block * width * 4 * width,
        moved=8 * count * block * width * 4,
    )(series, cotangent, w_in, w_out)
    fields = all_to_all(fields, "seq")

    toeplitz = call(
        toeplitz_kernel,
        shape((2, blocks, W, W), BF16),
        [pltpu.VMEM((8, length), F32)],
        flops=2 * W * length * 200,
        moved=2 * W * length * 2,
    )(lines)

    sent, kept = call(
        functools.partial(operator_kernel, units),
        (shape((sources, packed, W), BF16), shape((7, rows, W), BF16)),
        [pltpu.VMEM((3 * rows, W), BF16)],
        flops=4 * 2 * rows * length * W,
        moved=2 * W * length * 2 * 2,
    )(fields, toeplitz, taps, skip_one.reshape(1, width), skip_two.reshape(1, width))

    back = all_to_all(sent, "seq")

    total_rows = 4 * group + 2 * (length // width) + 16
    sums = call(
        functools.partial(gradient_kernel, units),
        shape((copies, total_rows, width), BF16),
        [
            pltpu.VMEM((2 * rows, W), BF16),
            pltpu.VMEM((W, length), F32),
            pltpu.VMEM((total_rows, width), F32),
        ],
        flops=2 * 2 * rows * length * W,
        moved=2 * length * width * 2,
    )(fields, sent, kept, all_series, all_cot)
    sums = all_to_all(sums, "dp")

    spread_rows = 4 * group + 32
    sums = call(
        functools.partial(spread_kernel, units),
        shape((sources, spread_rows, width), BF16),
        [pltpu.VMEM((total_rows, width), F32)],
        flops=copies * total_rows * width,
        moved=2 * sources * spread_rows * width,
    )(sums)
    sums = all_to_all(sums, "seq")

    output, d_series = call(
        functools.partial(output_kernel, units),
        (shape(series.shape, BF16), shape(series.shape, BF16)),
        flops=2 * count * block * width * 4 * width,
        moved=2 * count * block * width * 6,
    )(back, w_in, w_out)

    grads = call(
        functools.partial(parameter_kernel, units, scale),
        (
            shape(w_in.shape, F32),
            shape(w_out.shape, F32),
            shape(taps.shape, F32),
            shape((1, width), F32),
            shape((1, width), F32),
            shape(filter_one.shape, F32),
            shape(filter_two.shape, F32),
        ),
        flops=sources * spread_rows * width,
        moved=2 * sources * spread_rows * width,
    )(sums)
    grad_w_in, grad_w_out, grad_taps, grad_skip_one, grad_skip_two, grad_one, grad_two = grads
    return (
        output,
        d_series,
        grad_w_in,
        grad_w_out,
        grad_taps,
        grad_skip_one.reshape(width),
        grad_skip_two.reshape(width),
        grad_one,
        grad_two,
    )


def solution(mesh):
    specs = (
        P("dp", "seq", None),
        P("dp", "seq", None),
        P(),
        P(),
        P(),
        P(),
        P(),
        P(None, "seq"),
        P(None, "seq"),
    )
    return jax.shard_map(shards, mesh=mesh, in_specs=specs, out_specs=specs, check_vma=False)
```

```python
import functools
import math

import jax
import jax.numpy as jnp
from jax import lax
from jax.experimental import pallas as pl
from jax.experimental.pallas import tpu as pltpu
from jax.sharding import PartitionSpec as P

W = 256
F32 = jnp.float32
BF16 = jnp.bfloat16
NT = (((1,), (1,)), ((), ()))
VMEM_LIMIT = 56 * 1024 * 1024


def call(body, out_shape, scratch=(), flops=0, moved=0):
    return pl.pallas_call(
        body,
        out_shape=out_shape,
        scratch_shapes=list(scratch),
        compiler_params=pltpu.CompilerParams(vmem_limit_bytes=VMEM_LIMIT),
        cost_estimate=pl.CostEstimate(flops=flops, bytes_accessed=moved, transcendentals=0),
    )


def dot(a, b):
    return jnp.dot(a, b, preferred_element_type=F32)


def dot_nt(a, b):
    return lax.dot_general(a, b, NT, preferred_element_type=F32)


def project_kernel(units, series_ref, cot_ref, w_in_ref, w_out_ref, one_ref, two_ref, out_ref):
    count, block, width = series_ref.shape
    group = width // units
    parts = block // W
    w_in_t = w_in_ref[...].T
    w_out = w_out_ref[...]
    for e in range(count):
        for part in range(parts):
            rows = pl.ds(part * W, W)
            proj = dot_nt(w_in_t, series_ref[e, rows, :]).astype(BF16)
            d_prod = dot_nt(w_out, cot_ref[e, rows, :]).astype(BF16)
            for kind in range(4):
                field = proj[kind * width : (kind + 1) * width] if kind < 3 else d_prod
                out_ref[
                    e * units : (e + 1) * units,
                    (kind * parts + part) * group : (kind * parts + part + 1) * group,
                    :,
                ] = field.reshape(units, group, W)
    lines = [
        ref[:, part * W : (part + 1) * W] for ref in (one_ref, two_ref) for part in range(parts)
    ]
    repeat = units // one_ref.shape[0]
    start = 4 * parts * group
    spare = jnp.zeros((out_ref.shape[1] - start - len(lines), W), F32)
    for u in range(units):
        row = u // repeat
        field = jnp.concatenate([line[row : row + 1] for line in lines] + [spare], axis=0)
        for e in range(count):
            out_ref[e * units + u, start:, :] = field.astype(BF16)


def build_toeplitz(fields_ref, start, toep_ref, base_ref):
    sources = fields_ref.shape[0]
    _, blocks, _, _ = toep_ref.shape
    parts = blocks // sources
    length = blocks * W
    half = W // 2
    row = lax.broadcasted_iota(jnp.int32, (8, length), 0)
    lane = lax.broadcasted_iota(jnp.int32, (16, W), 1)
    channel = lax.broadcasted_iota(jnp.int32, (16, W), 0)
    for m in range(2):
        for s in range(sources):
            lines = fields_ref[s, start : start + 16, :].astype(F32)
            for p in range(parts):
                at = (s * parts + p) * W
                base_ref[:, at : at + W] = jnp.broadcast_to(
                    lines[m * parts + p : m * parts + p + 1, :], (8, W)
                )
        base = base_ref[...]
        for bit in (1, 2, 4):
            base = jnp.where((row & bit) != 0, pltpu.roll(base, bit, 1), base)
        for q in range(half // 16):
            low = pltpu.roll(base, 16 * q, 1) if q else base
            both = jnp.concatenate([low, pltpu.roll(base, 16 * q + 8, 1)], axis=0)
            first = jnp.where(lane >= channel + 16 * q, both[:, :W], 0.0)
            both = jnp.concatenate([first, both[:, W:]], axis=1).astype(BF16)
            at = 16 * q
            moved = jnp.concatenate([jnp.zeros((16, half), BF16), both[:, :-half]], axis=1)
            for d in range(blocks):
                toep_ref[m, d, at : at + 16, :] = both[:, d * W : (d + 1) * W]
                toep_ref[m, d, half + at : half + at + 16, :] = moved[:, d * W : (d + 1) * W]


def earlier(field, j, group):
    if j == 0:
        return field
    turned = pltpu.roll(field, j, 1)
    above = jnp.concatenate([jnp.zeros((group, W), F32), turned[:-group]], axis=0)
    lane = lax.broadcasted_iota(jnp.int32, field.shape, 1)
    return jnp.where(lane < j, above, turned)


def later(field, j, group):
    if j == 0:
        return field
    turned = pltpu.roll(field, W - j, 1)
    below = jnp.concatenate([turned[group:], jnp.zeros((group, W), F32)], axis=0)
    lane = lax.broadcasted_iota(jnp.int32, field.shape, 1)
    return jnp.where(lane >= W - j, below, turned)


def own_lanes(f, group, width):
    lane = lax.broadcasted_iota(jnp.int32, (group, width), 1)
    channel = lax.broadcasted_iota(jnp.int32, (group, width), 0)
    return lane == f * group + channel


def pick(ref, kind, received):
    rows = received // 4
    field = ref[:, kind * rows : (kind + 1) * rows, :]
    return field.reshape(field.shape[0] * rows, W).astype(F32)


def operator_kernel(
    units,
    fields_ref,
    taps_ref,
    skip_one_ref,
    skip_two_ref,
    out_ref,
    kept_ref,
    pad_ref,
    toep_ref,
    base_ref,
):
    sources, received, _ = out_ref.shape
    build_toeplitz(fields_ref, received, toep_ref, base_ref)
    width = taps_ref.shape[1] // 3
    group = width // units
    rows = sources * received // 4
    blocks = rows // group
    f = lax.rem(lax.axis_index("seq"), units)
    mine = own_lanes(f, group, width)

    def column(values):
        col = jnp.sum(jnp.where(mine, values, 0.0), axis=1, keepdims=True)
        return jnp.broadcast_to(col, (group, W))

    def scaled(field, col):
        return (field.reshape(blocks, group, W) * col[None]).reshape(rows, W)

    zeros = jnp.zeros((rows, W), BF16)
    pad_ref[0:rows, :] = zeros
    pad_ref[2 * rows : 3 * rows, :] = zeros

    def causal(m, field):
        pad_ref[rows : 2 * rows, :] = field
        left = jnp.concatenate(
            [pad_ref[rows - group * d : 2 * rows - group * d, :] for d in range(blocks)], axis=1
        )
        return dot(left, toep_ref[m].reshape(blocks * W, W))

    def anticausal(m, field):
        pad_ref[rows : 2 * rows, :] = field
        left = jnp.concatenate(
            [pad_ref[rows + group * d : 2 * rows + group * d, :] for d in range(blocks)], axis=1
        )
        right = jnp.concatenate([toep_ref[m, d] for d in range(blocks)], axis=1)
        return dot_nt(left, right)

    tap = [
        [
            column(taps_ref[j : j + 1, kind * width : (kind + 1) * width])
            for j in range(3)
        ]
        for kind in range(3)
    ]
    skip_one = column(skip_one_ref[...])
    skip_two = column(skip_two_ref[...])

    def short(kind):
        field = pick(fields_ref, kind, received)
        total = scaled(field, tap[kind][0])
        for j in (1, 2):
            total = total + scaled(earlier(field, j, group), tap[kind][j])
        return total

    def keep(slot, field):
        low = field.astype(BF16)
        kept_ref[slot] = low
        return low

    def send(kind, field):
        part_rows = received // 4
        out_ref[:, kind * part_rows : (kind + 1) * part_rows, :] = field.astype(BF16).reshape(
            sources, part_rows, W
        )

    def send_back(kind, field):
        total = scaled(field, tap[kind][0])
        for j in (1, 2):
            total = total + scaled(later(field, j, group), tap[kind][j])
        send(kind, total)

    value = short(0)
    y_one = causal(0, keep(0, value)) + scaled(value, skip_one)
    gate_one = short(1)
    mid = gate_one * y_one
    y_two = causal(1, keep(1, mid)) + scaled(mid, skip_two)
    gate_two = short(2)
    send(3, gate_two * y_two)
    d_product = pick(fields_ref, 3, received)
    grad_two = d_product * gate_two
    d_gate_two = d_product * y_two
    keep(6, d_gate_two)
    send_back(2, d_gate_two)
    d_mid = anticausal(1, keep(3, grad_two)) + scaled(grad_two, skip_two)
    grad_one = d_mid * gate_one
    d_gate_one = d_mid * y_one
    keep(5, d_gate_one)
    send_back(1, d_gate_one)
    d_value = anticausal(0, keep(2, grad_one)) + scaled(grad_one, skip_one)
    keep(4, d_value)
    send_back(0, d_value)


def gradient_kernel(units, fields_ref, kept_ref, out_ref, pad_ref, corr_ref):
    sources, _, _ = fields_ref.shape
    _, rows, _ = kept_ref.shape
    _, length = corr_ref.shape
    width = out_ref.shape[1]
    blocks = length // W
    group = rows // blocks
    received = 4 * rows // sources
    half = W // 2
    u = lax.rem(lax.axis_index("seq"), units)
    mine = own_lanes(u, group, width)
    lines = length // width

    pad_ref[rows : 2 * rows, :] = jnp.zeros((rows, W), BF16)
    row8 = lax.broadcasted_iota(jnp.int32, (8, length), 0)
    b = lax.broadcasted_iota(jnp.int32, (W, W), 0)
    r = lax.broadcasted_iota(jnp.int32, (W, W), 1)
    for m in range(2):
        pad_ref[0:rows, :] = kept_ref[2 + m]
        right = jnp.concatenate(
            [pad_ref[group * d : rows + group * d, :] for d in range(blocks)], axis=1
        )
        held = kept_ref[m].astype(F32).T.astype(BF16)
        corr_ref[...] = dot(held, right)
        corr_ref[:, 0:W] = jnp.where(r >= b, corr_ref[:, 0:W], 0.0)
        total = None
        for q in range(half // 8):
            upper = corr_ref[half + 8 * q : half + 8 * q + 8, :]
            upper = jnp.concatenate([upper[:, half:], jnp.zeros((8, half), F32)], axis=1)
            both = corr_ref[8 * q : 8 * q + 8, :] + upper
            if q:
                both = pltpu.roll(both, length - 8 * q, 1)
            total = both if total is None else total + both
        for bit in (1, 2, 4):
            total = jnp.where((row8 & bit) != 0, pltpu.roll(total, length - bit, 1), total)
        line = jnp.sum(total, axis=0, keepdims=True)
        for q in range(lines):
            at = m * lines + q
            out_ref[at : at + 1, :] = line[:, q * width : (q + 1) * width]

    def spread(products):
        by_channel = jnp.sum(products.reshape(blocks, group, W), axis=0)
        col = jnp.sum(by_channel, axis=1, keepdims=True)
        return jnp.sum(jnp.where(mine, col, 0.0), axis=0, keepdims=True)

    small = []
    for j in range(3):
        for kind in range(3):
            field = pick(fields_ref, kind, received)
            small.append(spread(kept_ref[4 + kind].astype(F32) * earlier(field, j, group)))
    for m in range(2):
        small.append(spread(kept_ref[2 + m].astype(F32) * kept_ref[m].astype(F32)))
    out_ref[2 * lines : 2 * lines + 16, :] = jnp.concatenate(
        small + [jnp.zeros((16 - len(small), width), F32)], axis=0
    )


def output_kernel(
    units, in_ref, w_in_ref, w_out_ref, series_ref, cot_ref, own_ref, out_ref, d_series_ref, part_ref
):
    count, block, width = out_ref.shape
    group = width // units
    parts = block // W
    w_in = w_in_ref[...]
    w_out_t = w_out_ref[...].T

    def field(e, kind, part):
        at = (kind * parts + part) * group
        return in_ref[e * units : (e + 1) * units, at : at + group, :].reshape(width, W)

    w_in_part = 0.0
    w_out_part = 0.0
    for e in range(count):
        for part in range(parts):
            rows = pl.ds(part * W, W)
            product = field(e, 3, part)
            out_ref[e, rows, :] = dot(w_out_t, product).T.astype(BF16)
            grads = jnp.concatenate([field(e, kind, part) for kind in range(3)], axis=0)
            d_series_ref[e, rows, :] = dot(w_in, grads).T.astype(BF16)
            w_in_part += dot(grads, series_ref[e, rows, :])
            w_out_part += dot(product, cot_ref[e, rows, :])

    weights = jnp.concatenate([w_in_part, w_out_part], axis=0)
    targets, sent, _ = part_ref.shape
    each = weights.shape[0] // targets
    sources = in_ref.shape[0]
    lines = (own_ref.shape[0] - 16) // 2
    slots = lines // sources
    spare = jnp.zeros((sent - each - 2 * slots - 1, width), F32)
    for g in range(targets):
        s = g % sources
        small = 2 * lines + g * 16 // targets
        part_ref[g] = jnp.concatenate(
            [
                weights[g * each : (g + 1) * each],
                own_ref[s * slots : (s + 1) * slots, :],
                own_ref[lines + s * slots : lines + (s + 1) * slots, :],
                own_ref[small : small + 1, :],
                spare,
            ],
            axis=0,
        ).astype(BF16)


def sum_kernel(units, each, scale, in_ref, out_ref, one_ref, two_ref):
    targets, _, width = in_ref.shape
    filters, block = one_ref.shape
    slots = block // width
    total = in_ref[0].astype(F32)
    for g in range(1, targets):
        total = total + in_ref[g].astype(F32)
    weights = total[:each]
    small = total[each + 2 * slots : each + 2 * slots + 1]
    spare = jnp.zeros((out_ref.shape[1] - each - 1, width), F32)
    total = jnp.concatenate([weights, small, spare], axis=0).astype(BF16)
    for g in range(targets):
        out_ref[g] = total
    repeat = units // filters
    for row in range(filters):
        sums = 0.0
        for g in range(targets):
            if g % units // repeat == row:
                sums += in_ref[g, each : each + 2 * slots, :].astype(F32)
        for q in range(slots):
            one_ref[row : row + 1, q * width : (q + 1) * width] = sums[q : q + 1] * scale
            two_ref[row : row + 1, q * width : (q + 1) * width] = sums[slots + q : slots + q + 1] * scale


def weight_kernel(each, scale, in_ref, w_in_ref, w_out_ref, taps_ref, skip_one_ref, skip_two_ref):
    targets, _, width = in_ref.shape
    weights = jnp.concatenate([in_ref[g, 0:each, :].astype(F32) for g in range(targets)], axis=0) * scale
    for kind in range(3):
        w_in_ref[:, kind * width : (kind + 1) * width] = weights[kind * width : (kind + 1) * width].T
    w_out_ref[...] = weights[3 * width :]

    def small(n):
        return in_ref[n * targets // 16, each : each + 1, :].astype(F32) * scale

    for j in range(3):
        for kind in range(3):
            taps_ref[j : j + 1, kind * width : (kind + 1) * width] = small(3 * j + kind)
    skip_one_ref[...] = small(9)
    skip_two_ref[...] = small(10)


def all_to_all(blocks, axis):
    return lax.all_to_all(blocks, axis, split_axis=0, concat_axis=0, tiled=True)


def shards(series, cotangent, w_in, w_out, taps, skip_one, skip_two, filter_one, filter_two):
    count, block, width = series.shape
    filters = filter_one.shape[0]
    sources = lax.axis_size("seq")
    copies = lax.axis_size("dp")
    length = block * sources
    units = sources // count
    group = width // units
    assert sources == count * units and units % filters == 0 and block % W == 0
    blocks = length // W
    rows = blocks * group
    scale = 1.0 / math.sqrt(count * copies * length)
    shape = jax.ShapeDtypeStruct

    devices = sources * copies
    packed = 4 * (block // W) * group
    fields = call(
        functools.partial(project_kernel, units),
        shape((sources, packed + 16, W), BF16),
        flops=2 * count * block * width * 4 * width,
        moved=8 * count * block * width * 4,
    )(series, cotangent, w_in, w_out, filter_one, filter_two)
    fields = all_to_all(fields, "seq")

    sent, kept = call(
        functools.partial(operator_kernel, units),
        (shape((sources, packed, W), BF16), shape((7, rows, W), BF16)),
        [
            pltpu.VMEM((3 * rows, W), BF16),
            pltpu.VMEM((2, blocks, W, W), BF16),
            pltpu.VMEM((8, length), F32),
        ],
        flops=4 * 2 * rows * length * W,
        moved=2 * W * length * 2 * 2,
    )(fields, taps, skip_one.reshape(1, width), skip_two.reshape(1, width))

    back = all_to_all(sent, "seq")

    own = call(
        functools.partial(gradient_kernel, units),
        shape((2 * (length // width) + 16, width), F32),
        [pltpu.VMEM((2 * rows, W), BF16), pltpu.VMEM((W, length), F32)],
        flops=2 * 2 * rows * length * W,
        moved=2 * length * width * 2,
    )(fields, kept)

    each = 4 * width // devices
    sent_rows = -(-(each + 2 * (block // width) + 1) // 16) * 16
    output, d_series, partial = call(
        functools.partial(output_kernel, units),
        (
            shape(series.shape, BF16),
            shape(series.shape, BF16),
            shape((devices, sent_rows, width), BF16),
        ),
        flops=2 * count * block * width * 8 * width,
        moved=2 * count * block * width * 6,
    )(back, w_in, w_out, series, cotangent, own)
    partial = all_to_all(partial, ("dp", "seq"))

    sums, grad_one, grad_two = call(
        functools.partial(sum_kernel, units, each, scale),
        (
            shape((devices, -(-(each + 1) // 16) * 16, width), BF16),
            shape(filter_one.shape, F32),
            shape(filter_two.shape, F32),
        ),
        flops=devices * sent_rows * width,
        moved=4 * devices * sent_rows * width,
    )(partial)
    sums = all_to_all(sums, ("dp", "seq"))

    grad_w_in, grad_w_out, grad_taps, grad_skip_one, grad_skip_two = call(
        functools.partial(weight_kernel, each, scale),
        (
            shape(w_in.shape, F32),
            shape(w_out.shape, F32),
            shape(taps.shape, F32),
            shape((1, width), F32),
            shape((1, width), F32),
        ),
        flops=devices * sent_rows * width,
        moved=2 * devices * sent_rows * width,
    )(sums)
    return (
        output,
        d_series,
        grad_w_in,
        grad_w_out,
        grad_taps,
        grad_skip_one.reshape(width),
        grad_skip_two.reshape(width),
        grad_one,
        grad_two,
    )


def solution(mesh):
    specs = (
        P("dp", "seq", None),
        P("dp", "seq", None),
        P(),
        P(),
        P(),
        P(),
        P(),
        P(None, "seq"),
        P(None, "seq"),
    )
    return jax.shard_map(shards, mesh=mesh, in_specs=specs, out_specs=specs, check_vma=False)
```

```python
import functools
import math

import jax
import jax.numpy as jnp
from jax import lax
from jax.experimental import pallas as pl
from jax.experimental.pallas import tpu as pltpu
from jax.sharding import PartitionSpec as P

W = 256
F32 = jnp.float32
BF16 = jnp.bfloat16
NT = (((1,), (1,)), ((), ()))
VMEM_LIMIT = 56 * 1024 * 1024


def call(body, out_shape, scratch=(), flops=0, moved=0):
    return pl.pallas_call(
        body,
        out_shape=out_shape,
        scratch_shapes=list(scratch),
        compiler_params=pltpu.CompilerParams(vmem_limit_bytes=VMEM_LIMIT),
        cost_estimate=pl.CostEstimate(flops=flops, bytes_accessed=moved, transcendentals=0),
    )


def dot(a, b):
    return jnp.dot(a, b, preferred_element_type=F32)


def dot_nt(a, b):
    return lax.dot_general(a, b, NT, preferred_element_type=F32)


def slice_kernel(units, one_ref, two_ref, out_ref):
    targets, _, width = out_ref.shape
    filters, block = one_ref.shape
    repeat = units // filters
    for f in range(filters):
        rows = [
            ref[f : f + 1, q * width : (q + 1) * width]
            for ref in (one_ref, two_ref)
            for q in range(block // width)
        ]
        rows = jnp.concatenate(rows, axis=0)
        for g in range(targets):
            if g % units // repeat == f:
                out_ref[g] = rows


def toeplitz_kernel(lines_ref, toep_ref, base_ref):
    sources, rows, width = lines_ref.shape
    _, blocks, _, _ = toep_ref.shape
    slots = rows // 2
    length = blocks * W
    half = W // 2
    row = lax.broadcasted_iota(jnp.int32, (8, length), 0)
    lane = lax.broadcasted_iota(jnp.int32, (16, W), 1)
    channel = lax.broadcasted_iota(jnp.int32, (16, W), 0)
    for m in range(2):
        for s in range(sources):
            for q in range(slots):
                at = (s * slots + q) * width
                base_ref[:, at : at + width] = jnp.broadcast_to(
                    lines_ref[s, m * slots + q : m * slots + q + 1, :], (8, width)
                )
        base = base_ref[...]
        for bit in (1, 2, 4):
            base = jnp.where((row & bit) != 0, pltpu.roll(base, bit, 1), base)
        for q in range(half // 16):
            low = pltpu.roll(base, 16 * q, 1) if q else base
            both = jnp.concatenate([low, pltpu.roll(base, 16 * q + 8, 1)], axis=0)
            first = jnp.where(lane >= channel + 16 * q, both[:, :W], 0.0)
            both = jnp.concatenate([first, both[:, W:]], axis=1).astype(BF16)
            at = 16 * q
            moved = jnp.concatenate([jnp.zeros((16, half), BF16), both[:, :-half]], axis=1)
            for d in range(blocks):
                toep_ref[m, d, at : at + 16, :] = both[:, d * W : (d + 1) * W]
                toep_ref[m, d, half + at : half + at + 16, :] = moved[:, d * W : (d + 1) * W]


def earlier(field, j, group):
    if j == 0:
        return field
    turned = pltpu.roll(field, j, 1)
    above = jnp.concatenate([jnp.zeros((group, W), F32), turned[:-group]], axis=0)
    lane = lax.broadcasted_iota(jnp.int32, field.shape, 1)
    return jnp.where(lane < j, above, turned)


def later(field, j, group):
    if j == 0:
        return field
    turned = pltpu.roll(field, W - j, 1)
    below = jnp.concatenate([turned[group:], jnp.zeros((group, W), F32)], axis=0)
    lane = lax.broadcasted_iota(jnp.int32, field.shape, 1)
    return jnp.where(lane >= W - j, below, turned)


def own_lanes(f, group, width):
    lane = lax.broadcasted_iota(jnp.int32, (group, width), 1)
    channel = lax.broadcasted_iota(jnp.int32, (group, width), 0)
    return lane == f * group + channel


def places(own, other, other_last):
    m = len(own)
    me = lax.axis_index("seq")
    row, core = me // 2, lax.rem(me, 2)
    for k in range(m):
        place = 2 * lax.rem(row - k + m, m)
        yield place + core, own[k][...]
        yield place + 1 - core, (other[k] if k < m - 1 else other_last[...])


def operator_kernel(units, m, *refs):
    series = refs[0 : m + 2]
    cot = refs[m + 2 : 2 * m + 4]
    toep_ref, w_in_ref, w_out_ref, taps_ref, skip_one_ref, skip_two_ref = refs[2 * m + 4 : 2 * m + 10]
    out_ref, kept_ref, pad_ref, raw_ref, wide_ref = refs[2 * m + 10 :]
    sources, received, _ = out_ref.shape
    width = taps_ref.shape[1] // 3
    group = width // units
    rows = sources * received // 4
    blocks = rows // group
    parts = blocks // sources
    u = lax.rem(lax.axis_index("seq"), units)
    mine = own_lanes(u, group, width)

    wide_ref[0 : 3 * width, :] = w_in_ref[...].astype(F32).T
    wide_ref[3 * width :, :] = w_out_ref[...].astype(F32)

    def weights(kind):
        return wide_ref[pl.ds(pl.multiple_of(kind * width + u * group, group), group), :]

    w_in = jnp.concatenate([weights(kind) for kind in range(3)], axis=0).astype(BF16)
    w_out = weights(3).astype(BF16)

    def project(first, matrix, gathered):
        for place, block in places(gathered[:m], gathered[m], gathered[m + 1]):
            for p in range(parts):
                field = dot_nt(matrix, block[p * W : (p + 1) * W])
                at = pl.multiple_of((place * parts + p) * group, group)
                for i in range(field.shape[0] // group):
                    raw_ref[first + i, pl.ds(at, group), :] = field[i * group : (i + 1) * group]

    project(0, w_in, series)
    project(3, w_out, cot)

    def column(values):
        col = jnp.sum(jnp.where(mine, values, 0.0), axis=1, keepdims=True)
        return jnp.broadcast_to(col, (group, W))

    def scaled(field, col):
        return (field.reshape(blocks, group, W) * col[None]).reshape(rows, W)

    zeros = jnp.zeros((rows, W), BF16)
    pad_ref[0:rows, :] = zeros
    pad_ref[2 * rows : 3 * rows, :] = zeros

    def causal(m, field):
        pad_ref[rows : 2 * rows, :] = field
        left = jnp.concatenate(
            [pad_ref[rows - group * d : 2 * rows - group * d, :] for d in range(blocks)], axis=1
        )
        return dot(left, toep_ref[m].reshape(blocks * W, W))

    def anticausal(m, field):
        pad_ref[rows : 2 * rows, :] = field
        left = jnp.concatenate(
            [pad_ref[rows + group * d : 2 * rows + group * d, :] for d in range(blocks)], axis=1
        )
        right = jnp.concatenate([toep_ref[m, d] for d in range(blocks)], axis=1)
        return dot_nt(left, right)

    tap = [
        [
            column(taps_ref[j : j + 1, kind * width : (kind + 1) * width])
            for j in range(3)
        ]
        for kind in range(3)
    ]
    skip_one = column(skip_one_ref[...])
    skip_two = column(skip_two_ref[...])

    def short(kind):
        field = raw_ref[kind]
        kept_ref[7 + kind] = field.astype(BF16)
        total = scaled(field, tap[kind][0])
        for j in (1, 2):
            total = total + scaled(earlier(field, j, group), tap[kind][j])
        return total

    def keep(slot, field):
        low = field.astype(BF16)
        kept_ref[slot] = low
        return low

    def send(kind, field):
        part_rows = received // 4
        out_ref[:, kind * part_rows : (kind + 1) * part_rows, :] = field.astype(BF16).reshape(
            sources, part_rows, W
        )

    def send_back(kind, field):
        total = scaled(field, tap[kind][0])
        for j in (1, 2):
            total = total + scaled(later(field, j, group), tap[kind][j])
        send(kind, total)

    value = short(0)
    y_one = causal(0, keep(0, value)) + scaled(value, skip_one)
    gate_one = short(1)
    mid = gate_one * y_one
    y_two = causal(1, keep(1, mid)) + scaled(mid, skip_two)
    gate_two = short(2)
    send(3, gate_two * y_two)
    d_product = raw_ref[3]
    grad_two = d_product * gate_two
    d_gate_two = d_product * y_two
    keep(6, d_gate_two)
    send_back(2, d_gate_two)
    d_mid = anticausal(1, keep(3, grad_two)) + scaled(grad_two, skip_two)
    grad_one = d_mid * gate_one
    d_gate_one = d_mid * y_one
    keep(5, d_gate_one)
    send_back(1, d_gate_one)
    d_value = anticausal(0, keep(2, grad_one)) + scaled(grad_one, skip_one)
    keep(4, d_value)
    send_back(0, d_value)


def gradient_kernel(units, m, *refs):
    series = refs[0 : m + 2]
    cot = refs[m + 2 : 2 * m + 4]
    sent_ref, kept_ref, out_ref, pad_ref, corr_ref, total_ref = refs[2 * m + 4 :]
    sources, _, _ = sent_ref.shape
    _, rows, _ = kept_ref.shape
    _, length = corr_ref.shape
    width = out_ref.shape[1]
    blocks = length // W
    group = rows // blocks
    parts = blocks // sources
    half = W // 2
    u = lax.rem(lax.axis_index("seq"), units)
    mine = own_lanes(u, group, width)
    lines = length // width

    def weights(kinds, gathered):
        left, right = [], []
        for place, block in places(gathered[:m], gathered[m], gathered[m + 1]):
            right.append(block)
            for p in range(parts):
                at = [(kind * parts + p) * group for kind in kinds]
                left.append(jnp.concatenate([sent_ref[place, i : i + group, :] for i in at], axis=0))
        return dot(jnp.concatenate(left, axis=1), jnp.concatenate(right, axis=0))

    total_ref[0 : 3 * group, :] = weights((0, 1, 2), series)
    total_ref[3 * group : 4 * group, :] = weights((3,), cot)

    pad_ref[rows : 2 * rows, :] = jnp.zeros((rows, W), BF16)
    row8 = lax.broadcasted_iota(jnp.int32, (8, length), 0)
    b = lax.broadcasted_iota(jnp.int32, (W, W), 0)
    r = lax.broadcasted_iota(jnp.int32, (W, W), 1)
    for order in range(2):
        pad_ref[0:rows, :] = kept_ref[2 + order]
        right = jnp.concatenate(
            [pad_ref[group * d : rows + group * d, :] for d in range(blocks)], axis=1
        )
        held = kept_ref[order].astype(F32).T.astype(BF16)
        corr_ref[...] = dot(held, right)
        corr_ref[:, 0:W] = jnp.where(r >= b, corr_ref[:, 0:W], 0.0)
        total = None
        for q in range(half // 8):
            upper = corr_ref[half + 8 * q : half + 8 * q + 8, :]
            upper = jnp.concatenate([upper[:, half:], jnp.zeros((8, half), F32)], axis=1)
            both = corr_ref[8 * q : 8 * q + 8, :] + upper
            if q:
                both = pltpu.roll(both, length - 8 * q, 1)
            total = both if total is None else total + both
        for bit in (1, 2, 4):
            total = jnp.where((row8 & bit) != 0, pltpu.roll(total, length - bit, 1), total)
        line = jnp.sum(total, axis=0, keepdims=True)
        for q in range(lines):
            at = 4 * group + order * lines + q
            total_ref[at : at + 1, :] = line[:, q * width : (q + 1) * width]

    def spread(products):
        by_channel = jnp.sum(products.reshape(blocks, group, W), axis=0)
        col = jnp.sum(by_channel, axis=1, keepdims=True)
        return jnp.sum(jnp.where(mine, col, 0.0), axis=0, keepdims=True)

    small = []
    for j in range(3):
        for kind in range(3):
            field = kept_ref[7 + kind].astype(F32)
            small.append(spread(kept_ref[4 + kind].astype(F32) * earlier(field, j, group)))
    for order in range(2):
        small.append(spread(kept_ref[2 + order].astype(F32) * kept_ref[order].astype(F32)))
    total_ref[4 * group + 2 * lines :, :] = jnp.concatenate(
        small + [jnp.zeros((16 - len(small), width), F32)], axis=0
    )
    out_ref[...] = total_ref[...].astype(BF16)


def spread_kernel(units, *refs):
    in_refs, out_ref, sum_ref = refs[:-2], refs[-2], refs[-1]
    width = out_ref.shape[2]
    group = width // units
    targets = out_ref.shape[0]
    total = in_refs[0][...].astype(F32)
    for ref in in_refs[1:]:
        total = total + ref[...].astype(F32)
    sum_ref[...] = total
    base = 4 * group
    lines = (total.shape[0] - base - 16) // 2
    each = lines // targets
    for s in range(targets):
        out_ref[s] = jnp.concatenate(
            [
                sum_ref[0:base, :],
                sum_ref[base + s * each : base + (s + 1) * each, :],
                sum_ref[base + lines + s * each : base + lines + (s + 1) * each, :],
                sum_ref[base + 2 * lines : base + 2 * lines + 16, :],
                jnp.zeros((16 - 2 * each, width), F32),
            ],
            axis=0,
        ).astype(BF16)


def parameter_kernel(
    units, scale, in_ref, w_in_ref, w_out_ref, taps_ref, skip_one_ref, skip_two_ref, one_ref, two_ref
):
    sources, _, width = in_ref.shape
    group = width // units
    count = sources // units
    each = one_ref.shape[1] // width

    def total(first, last):
        parts = [in_ref[e * units : (e + 1) * units, first:last, :] for e in range(count)]
        result = parts[0].astype(F32)
        for part in parts[1:]:
            result = result + part.astype(F32)
        return result

    blocks = total(0, 4 * group) * scale
    for kind in range(3):
        rows = blocks[:, kind * group : (kind + 1) * group, :].reshape(width, width)
        w_in_ref[:, kind * width : (kind + 1) * width] = rows.T
    w_out_ref[...] = blocks[:, 3 * group : 4 * group, :].reshape(width, width)
    rest = total(4 * group, in_ref.shape[1]) * scale
    filters = one_ref.shape[0]
    for q in range(each):
        for ref, at in ((one_ref, q), (two_ref, each + q)):
            by_unit = rest[:, at, :].reshape(filters, units // filters, width)
            ref[:, q * width : (q + 1) * width] = jnp.sum(by_unit, axis=1)
    small = jnp.sum(rest[:, 2 * each : 2 * each + 16, :], axis=0)
    for j in range(3):
        for kind in range(3):
            n = 3 * j + kind
            taps_ref[j : j + 1, kind * width : (kind + 1) * width] = small[n : n + 1]
    skip_one_ref[...] = small[9:10]
    skip_two_ref[...] = small[10:11]


def output_kernel(units, in_ref, w_in_ref, w_out_ref, out_ref, d_series_ref):
    count, block, width = out_ref.shape
    group = width // units
    parts = block // W
    w_in = w_in_ref[...]
    w_out_t = w_out_ref[...].T

    def field(e, kind, part):
        at = (kind * parts + part) * group
        return in_ref[e * units : (e + 1) * units, at : at + group, :].reshape(width, W)

    for e in range(count):
        for part in range(parts):
            rows = pl.ds(part * W, W)
            out_ref[e, rows, :] = dot(w_out_t, field(e, 3, part)).T.astype(BF16)
            grads = jnp.concatenate([field(e, kind, part) for kind in range(3)], axis=0)
            d_series_ref[e, rows, :] = dot(w_in, grads).T.astype(BF16)


def all_to_all(blocks, axis):
    return lax.all_to_all(blocks, axis, split_axis=0, concat_axis=0, tiled=True)


def passed(block, axis, route):
    return lax.ppermute(block, axis, route)


def ring(block):
    devices = lax.axis_size("seq")
    onward = [(i, (i + 2) % devices) for i in range(devices)]
    swap = [(i, i ^ 1) for i in range(devices)]
    own = [block]
    for _ in range(devices // 2 - 1):
        own.append(passed(own[-1], "seq", onward))
    other = passed(jnp.stack(own[:-1]), "seq", swap)
    return own + [other, passed(own[-1], "seq", swap)]


def shards(series, cotangent, w_in, w_out, taps, skip_one, skip_two, filter_one, filter_two):
    count, block, width = series.shape
    filters = filter_one.shape[0]
    sources = lax.axis_size("seq")
    copies = lax.axis_size("dp")
    length = block * sources
    units = sources // count
    group = width // units
    assert count == 1 and units % filters == 0 and block % W == 0
    assert sources % 2 == 0
    blocks = length // W
    rows = blocks * group
    scale = 1.0 / math.sqrt(count * copies * length)
    shape = jax.ShapeDtypeStruct
    m = sources // 2

    slices = call(
        functools.partial(slice_kernel, units),
        shape((sources, 2 * block // width, width), F32),
        flops=1000,
        moved=4 * 4 * filters * block,
    )(filter_one, filter_two)
    lines = all_to_all(slices, "seq")
    toeplitz = call(
        toeplitz_kernel,
        shape((2, blocks, W, W), BF16),
        [pltpu.VMEM((8, length), F32)],
        flops=2 * W * length * 200,
        moved=2 * W * length * 2,
    )(lines)

    all_series = ring(series.reshape(block, width))
    all_cot = ring(cotangent.reshape(block, width))

    packed = 4 * (block // W) * group
    sent, kept = call(
        functools.partial(operator_kernel, units, m),
        (shape((sources, packed, W), BF16), shape((10, rows, W), BF16)),
        [
            pltpu.VMEM((3 * rows, W), BF16),
            pltpu.VMEM((4, rows, W), F32),
            pltpu.VMEM((4 * width, width), F32),
        ],
        flops=4 * 2 * rows * length * W,
        moved=2 * W * length * 2 * 2,
    )(
        *all_series,
        *all_cot,
        toeplitz,
        w_in,
        w_out,
        taps,
        skip_one.reshape(1, width),
        skip_two.reshape(1, width),
    )

    back = all_to_all(sent, "seq")

    total_rows = 4 * group + 2 * (length // width) + 16
    total = call(
        functools.partial(gradient_kernel, units, m),
        shape((total_rows, width), BF16),
        [
            pltpu.VMEM((2 * rows, W), BF16),
            pltpu.VMEM((W, length), F32),
            pltpu.VMEM((total_rows, width), F32),
        ],
        flops=2 * 2 * rows * length * W,
        moved=2 * length * width * 2,
    )(*all_series, *all_cot, sent, kept)
    totals = [total] + [
        passed(total, "dp", [(i, (i + d) % copies) for i in range(copies)]) for d in range(1, copies)
    ]

    spread_rows = 4 * group + 32
    sums = call(
        functools.partial(spread_kernel, units),
        shape((sources, spread_rows, width), BF16),
        [pltpu.VMEM((total_rows, width), F32)],
        flops=copies * total_rows * width,
        moved=2 * sources * spread_rows * width,
    )(*totals)
    sums = all_to_all(sums, "seq")

    output, d_series = call(
        functools.partial(output_kernel, units),
        (shape(series.shape, BF16), shape(series.shape, BF16)),
        flops=2 * count * block * width * 4 * width,
        moved=2 * count * block * width * 6,
    )(back, w_in, w_out)

    grads = call(
        functools.partial(parameter_kernel, units, scale),
        (
            shape(w_in.shape, F32),
            shape(w_out.shape, F32),
            shape(taps.shape, F32),
            shape((1, width), F32),
            shape((1, width), F32),
            shape(filter_one.shape, F32),
            shape(filter_two.shape, F32),
        ),
        flops=sources * spread_rows * width,
        moved=2 * sources * spread_rows * width,
    )(sums)
    grad_w_in, grad_w_out, grad_taps, grad_skip_one, grad_skip_two, grad_one, grad_two = grads
    return (
        output,
        d_series,
        grad_w_in,
        grad_w_out,
        grad_taps,
        grad_skip_one.reshape(width),
        grad_skip_two.reshape(width),
        grad_one,
        grad_two,
    )


def solution(mesh):
    specs = (
        P("dp", "seq", None),
        P("dp", "seq", None),
        P(),
        P(),
        P(),
        P(),
        P(),
        P(None, "seq"),
        P(None, "seq"),
    )
    return jax.shard_map(shards, mesh=mesh, in_specs=specs, out_specs=specs, check_vma=False)
```

```python
import functools
import math

import jax
import jax.numpy as jnp
from jax import lax
from jax.experimental import pallas as pl
from jax.experimental.pallas import tpu as pltpu
from jax.sharding import PartitionSpec as P

W = 256
F32 = jnp.float32
BF16 = jnp.bfloat16
NT = (((1,), (1,)), ((), ()))
VMEM_LIMIT = 56 * 1024 * 1024


def call(body, out_shape, scratch=(), flops=0, moved=0):
    return pl.pallas_call(
        body,
        out_shape=out_shape,
        scratch_shapes=list(scratch),
        compiler_params=pltpu.CompilerParams(vmem_limit_bytes=VMEM_LIMIT),
        cost_estimate=pl.CostEstimate(flops=flops, bytes_accessed=moved, transcendentals=0),
    )


def dot(a, b):
    return jnp.dot(a, b, preferred_element_type=F32)


def dot_nt(a, b):
    return lax.dot_general(a, b, NT, preferred_element_type=F32)


def slice_kernel(units, one_ref, two_ref, *out_refs):
    filters, block = one_ref.shape
    rows, width = out_refs[0].shape
    row = lax.broadcasted_iota(jnp.int32, (filters, block), 0)
    me = lax.axis_index("seq")
    for d, out_ref in enumerate(out_refs):
        f = lax.rem(jnp.bitwise_xor(me, d), units) // (units // filters)
        for order, ref in enumerate((one_ref, two_ref)):
            line = jnp.sum(jnp.where(row == f, ref[...], 0.0), axis=0, keepdims=True)
            for q in range(rows // 2):
                at = order * rows // 2 + q
                out_ref[at : at + 1, :] = line[:, q * width : (q + 1) * width]


def toeplitz_kernel(*refs):
    lines_refs, (toep_ref, base_ref) = refs[:-2], refs[-2:]
    rows, width = lines_refs[0].shape
    me = lax.axis_index("seq")
    _, blocks, _, _ = toep_ref.shape
    slots = rows // 2
    length = blocks * W
    half = W // 2
    row = lax.broadcasted_iota(jnp.int32, (8, length), 0)
    lane = lax.broadcasted_iota(jnp.int32, (16, W), 1)
    channel = lax.broadcasted_iota(jnp.int32, (16, W), 0)
    for m in range(2):
        for d, ref in enumerate(lines_refs):
            for q in range(slots):
                at = pl.multiple_of((jnp.bitwise_xor(me, d) * slots + q) * width, width)
                base_ref[:, pl.ds(at, width)] = jnp.broadcast_to(
                    ref[m * slots + q : m * slots + q + 1, :], (8, width)
                )
        base = base_ref[...]
        for bit in (1, 2, 4):
            base = jnp.where((row & bit) != 0, pltpu.roll(base, bit, 1), base)
        for q in range(half // 16):
            low = pltpu.roll(base, 16 * q, 1) if q else base
            both = jnp.concatenate([low, pltpu.roll(base, 16 * q + 8, 1)], axis=0)
            first = jnp.where(lane >= channel + 16 * q, both[:, :W], 0.0)
            both = jnp.concatenate([first, both[:, W:]], axis=1).astype(BF16)
            at = 16 * q
            moved = jnp.concatenate([jnp.zeros((16, half), BF16), both[:, :-half]], axis=1)
            for d in range(blocks):
                toep_ref[m, d, at : at + 16, :] = both[:, d * W : (d + 1) * W]
                toep_ref[m, d, half + at : half + at + 16, :] = moved[:, d * W : (d + 1) * W]


def earlier(field, j, group):
    if j == 0:
        return field
    turned = pltpu.roll(field, j, 1)
    above = jnp.concatenate([jnp.zeros((group, W), F32), turned[:-group]], axis=0)
    lane = lax.broadcasted_iota(jnp.int32, field.shape, 1)
    return jnp.where(lane < j, above, turned)


def later(field, j, group):
    if j == 0:
        return field
    turned = pltpu.roll(field, W - j, 1)
    below = jnp.concatenate([turned[group:], jnp.zeros((group, W), F32)], axis=0)
    lane = lax.broadcasted_iota(jnp.int32, field.shape, 1)
    return jnp.where(lane >= W - j, below, turned)


def own_lanes(f, group, width):
    lane = lax.broadcasted_iota(jnp.int32, (group, width), 1)
    channel = lax.broadcasted_iota(jnp.int32, (group, width), 0)
    return lane == f * group + channel


def places(gathered):
    m = len(gathered) // 2
    me = lax.axis_index("seq")
    row, core = me // 2, lax.rem(me, 2)
    for k in range(m):
        place = 2 * lax.rem(row - k + m, m)
        yield place + core, gathered[k]
        yield place + 1 - core, gathered[m + k]


def project(raw_ref, kinds, matrix, gathered):
    group = matrix.shape[0] // len(kinds)
    for place, block in places(gathered):
        parts = block.shape[0] // W
        for p in range(parts):
            field = dot_nt(matrix, block[p * W : (p + 1) * W, :])
            at = pl.multiple_of((place * parts + p) * group, group)
            for i, kind in enumerate(kinds):
                raw_ref[kind, pl.ds(at, group), :] = field[i * group : (i + 1) * group]


def columns(mine):
    def column(values):
        col = jnp.sum(jnp.where(mine, values, 0.0), axis=1, keepdims=True)
        return jnp.broadcast_to(col, (mine.shape[0], W))

    return column


def scaled(field, col):
    group = col.shape[0]
    return (field.reshape(-1, group, W) * col[None]).reshape(field.shape)


def tap_columns(column, taps_ref):
    width = taps_ref.shape[1] // 3
    return [
        [column(taps_ref[j : j + 1, kind * width : (kind + 1) * width]) for j in range(3)]
        for kind in range(3)
    ]


def forward_kernel(units, *refs):
    sources = len(refs) - 11
    series = refs[:sources]
    toep_ref, w_in_ref, taps_ref, skip_one_ref, skip_two_ref = refs[sources : sources + 5]
    kept_ref, wide_ref, product_ref, pad_ref, raw_ref, turned_ref = refs[sources + 5 :]
    _, rows, _ = kept_ref.shape
    width = series[0].shape[1]
    group = width // units
    blocks = rows // group
    u = lax.rem(lax.axis_index("seq"), units)
    column = columns(own_lanes(u, group, width))

    turned_ref[...] = w_in_ref[...].astype(F32).T
    w_in = [
        turned_ref[pl.ds(pl.multiple_of(kind * width + u * group, group), group), :]
        for kind in range(3)
    ]
    project(raw_ref, (0, 1, 2), jnp.concatenate(w_in, axis=0).astype(BF16), series)

    pad_ref[0:rows, :] = jnp.zeros((rows, W), BF16)

    def causal(order, field):
        low = field.astype(BF16)
        kept_ref[order] = low
        pad_ref[rows : 2 * rows, :] = low
        left = jnp.concatenate(
            [pad_ref[rows - group * d : 2 * rows - group * d, :] for d in range(blocks)], axis=1
        )
        return dot(left, toep_ref[order].reshape(blocks * W, W))

    tap = tap_columns(column, taps_ref)

    def short(kind):
        field = raw_ref[kind]
        kept_ref[2 + kind] = field.astype(BF16)
        total = scaled(field, tap[kind][0])
        for j in (1, 2):
            total = total + scaled(earlier(field, j, group), tap[kind][j])
        return total

    value = short(0)
    y_one = causal(0, value) + scaled(value, column(skip_one_ref[...]))
    wide_ref[0] = y_one
    gate_one = short(1)
    wide_ref[1] = gate_one
    mid = gate_one * y_one
    y_two = causal(1, mid) + scaled(mid, column(skip_two_ref[...]))
    wide_ref[2] = y_two
    gate_two = short(2)
    wide_ref[3] = gate_two
    product_ref[...] = (gate_two * y_two).astype(BF16)


def backward_kernel(units, *refs):
    sources = (len(refs) - 12) // 2
    cot = refs[:sources]
    toep_ref, w_out_ref, taps_ref, skip_one_ref, skip_two_ref, wide_ref, product_ref = refs[
        sources : sources + 7
    ]
    kept_ref, sent_ref = refs[sources + 7 : sources + 9]
    block_refs = refs[sources + 9 : 2 * sources + 9]
    pad_ref, raw_ref, turned_ref = refs[2 * sources + 9 :]
    _, rows, _ = kept_ref.shape
    width = cot[0].shape[1]
    group = width // units
    blocks = rows // group
    me = lax.axis_index("seq")
    u = lax.rem(me, units)
    column = columns(own_lanes(u, group, width))

    turned_ref[...] = w_out_ref[...].astype(F32)
    w_out = turned_ref[pl.ds(pl.multiple_of(u * group, group), group), :].astype(BF16)
    project(raw_ref, (0,), w_out, cot)

    pad_ref[rows : 2 * rows, :] = jnp.zeros((rows, W), BF16)

    def anticausal(order, field):
        low = field.astype(BF16)
        kept_ref[order] = low
        pad_ref[0:rows, :] = low
        left = jnp.concatenate(
            [pad_ref[group * d : rows + group * d, :] for d in range(blocks)], axis=1
        )
        right = jnp.concatenate([toep_ref[order, d] for d in range(blocks)], axis=1)
        return dot_nt(left, right)

    tap = tap_columns(column, taps_ref)

    def send_back(kind, field):
        kept_ref[2 + kind] = field.astype(BF16)
        total = scaled(field, tap[kind][0])
        for j in (1, 2):
            total = total + scaled(later(field, j, group), tap[kind][j])
        send(kind, total.astype(BF16))

    each = rows // sources

    def send(kind, field):
        sent_ref[:, kind * each : (kind + 1) * each, :] = field.reshape(sources, each, W)

    send(3, product_ref[...])
    d_product = raw_ref[0]
    grad_two = d_product * wide_ref[3]
    d_mid = anticausal(1, grad_two) + scaled(grad_two, column(skip_two_ref[...]))
    send_back(2, d_product * wide_ref[2])
    grad_one = d_mid * wide_ref[1]
    d_value = anticausal(0, grad_one) + scaled(grad_one, column(skip_one_ref[...]))
    send_back(1, d_mid * wide_ref[0])
    send_back(0, d_value)
    for d, ref in enumerate(block_refs):
        ref[...] = sent_ref[jnp.bitwise_xor(me, d)]


def gradient_kernel(units, *refs):
    sources = (len(refs) - 7) // 2
    series = refs[:sources]
    cot = refs[sources : 2 * sources]
    fore_ref, back_ref, sent_ref, out_ref = refs[2 * sources : 2 * sources + 4]
    pad_ref, corr_ref, total_ref = refs[2 * sources + 4 :]
    _, rows, _ = back_ref.shape
    _, length = corr_ref.shape
    width = out_ref.shape[1]
    blocks = length // W
    group = rows // blocks
    parts = blocks // sources
    half = W // 2
    u = lax.rem(lax.axis_index("seq"), units)
    mine = own_lanes(u, group, width)
    slots = length // width // sources

    def weights(kinds, gathered):
        left, right = [], []
        for place, block in places(gathered):
            right.append(block[...])
            for p in range(parts):
                at = [(kind * parts + p) * group for kind in kinds]
                left.append(jnp.concatenate([sent_ref[place, i : i + group, :] for i in at], axis=0))
        return dot(jnp.concatenate(left, axis=1), jnp.concatenate(right, axis=0))

    total_ref[0 : 3 * group, :] = weights((0, 1, 2), series)
    total_ref[3 * group : 4 * group, :] = weights((3,), cot)

    pad_ref[rows : 2 * rows, :] = jnp.zeros((rows, W), BF16)
    row8 = lax.broadcasted_iota(jnp.int32, (8, length), 0)
    b = lax.broadcasted_iota(jnp.int32, (W, W), 0)
    r = lax.broadcasted_iota(jnp.int32, (W, W), 1)
    for order in range(2):
        pad_ref[0:rows, :] = back_ref[order]
        right = jnp.concatenate(
            [pad_ref[group * d : rows + group * d, :] for d in range(blocks)], axis=1
        )
        held = fore_ref[order].astype(F32).T.astype(BF16)
        corr_ref[...] = dot(held, right)
        corr_ref[:, 0:W] = jnp.where(r >= b, corr_ref[:, 0:W], 0.0)
        total = None
        for q in range(half // 8):
            upper = corr_ref[half + 8 * q : half + 8 * q + 8, :]
            upper = jnp.concatenate([upper[:, half:], jnp.zeros((8, half), F32)], axis=1)
            both = corr_ref[8 * q : 8 * q + 8, :] + upper
            if q:
                both = pltpu.roll(both, length - 8 * q, 1)
            total = both if total is None else total + both
        for bit in (1, 2, 4):
            total = jnp.where((row8 & bit) != 0, pltpu.roll(total, length - bit, 1), total)
        line = jnp.sum(total, axis=0, keepdims=True)
        for q in range(sources * slots):
            at = 4 * group + (q // slots * 2 + order) * slots + q % slots
            total_ref[at : at + 1, :] = line[:, q * width : (q + 1) * width]

    def spread(products):
        by_channel = jnp.sum(products.reshape(blocks, group, W), axis=0)
        col = jnp.sum(by_channel, axis=1, keepdims=True)
        return jnp.sum(jnp.where(mine, col, 0.0), axis=0, keepdims=True)

    small = []
    for j in range(3):
        for kind in range(3):
            field = fore_ref[2 + kind].astype(F32)
            small.append(spread(back_ref[2 + kind].astype(F32) * earlier(field, j, group)))
    for order in range(2):
        small.append(spread(back_ref[order].astype(F32) * fore_ref[order].astype(F32)))
    total_ref[4 * group + 2 * sources * slots :, :] = jnp.concatenate(
        small + [jnp.zeros((16 - len(small), width), F32)], axis=0
    )
    out_ref[...] = total_ref[...].astype(BF16)


def spread_kernel(copies, *refs):
    in_refs, out_refs, sum_ref = refs[:copies], refs[copies:-1], refs[-1]
    targets = len(out_refs)
    sent, width = out_refs[0].shape
    total = in_refs[0][...].astype(F32)
    for ref in in_refs[1:]:
        total = total + ref[...].astype(F32)
    sum_ref[...] = total
    base = sent - 32
    each = (total.shape[0] - base - 16) // targets
    weights = sum_ref[0:base, :].astype(BF16)
    small = sum_ref[base + targets * each :, :]
    spare = jnp.zeros((16 - each, width), F32)
    me = lax.axis_index("seq")
    for d in range(targets):
        at = pl.multiple_of(base + jnp.bitwise_xor(me, d) * each, each)
        out_refs[d][0:base, :] = weights
        rest = jnp.concatenate([small, sum_ref[pl.ds(at, each), :], spare], axis=0)
        out_refs[d][base:, :] = rest.astype(BF16)


def parameter_kernel(units, scale, *refs):
    in_refs = refs[:-8]
    w_in_ref, w_out_ref, taps_ref, skip_one_ref, skip_two_ref, one_ref, two_ref, rows_ref = refs[-8:]
    sources = len(in_refs)
    width = w_in_ref.shape[0]
    group = width // units
    filters, block = one_ref.shape
    slots = block // width
    me = lax.axis_index("seq")
    small = 0.0
    sums = [0.0] * (2 * slots)
    row = lax.broadcasted_iota(jnp.int32, (filters, width), 0)
    for d in range(sources):
        u = jnp.bitwise_xor(me, d)
        for kind in range(4):
            at = pl.multiple_of(kind * width + u * group, group)
            rows_ref[pl.ds(at, group), :] = (
                in_refs[d][kind * group : (kind + 1) * group, :].astype(F32) * scale
            )
        rest = in_refs[d][4 * group :, :].astype(F32) * scale
        small = small + rest[0:16]
        for q in range(2 * slots):
            sums[q] += jnp.where(row == u // (units // filters), rest[16 + q : 17 + q], 0.0)
    for q in range(slots):
        one_ref[:, q * width : (q + 1) * width] = sums[q]
        two_ref[:, q * width : (q + 1) * width] = sums[slots + q]
    for kind in range(3):
        lanes = slice(kind * width, (kind + 1) * width)
        w_in_ref[:, lanes] = rows_ref[lanes, :].T
        for j in range(3):
            n = 3 * j + kind
            taps_ref[j : j + 1, lanes] = small[n : n + 1]
    w_out_ref[...] = rows_ref[3 * width :, :]
    skip_one_ref[...] = small[9:10]
    skip_two_ref[...] = small[10:11]


def output_kernel(*refs):
    in_refs = refs[:-5]
    w_in_ref, w_out_ref, out_ref, d_series_ref, field_ref = refs[-5:]
    _, block, width = out_ref.shape
    group = width // len(in_refs)
    parts = block // W
    w_in = w_in_ref[...]
    w_out_t = w_out_ref[...].T
    me = lax.axis_index("seq")
    for d, ref in enumerate(in_refs):
        u = jnp.bitwise_xor(me, d)
        for kind in range(4):
            at = pl.multiple_of(kind * width + u * group, group)
            for part in range(parts):
                start = (kind * parts + part) * group
                field = ref[start : start + group, :].astype(field_ref.dtype)
                field_ref[part, pl.ds(at, group), :] = field
    for part in range(parts):
        rows = pl.ds(part * W, W)
        product = field_ref[part, 3 * width :, :].astype(BF16)
        out_ref[0, rows, :] = dot(w_out_t, product).T.astype(BF16)
        grads = field_ref[part, 0 : 3 * width, :].astype(BF16)
        d_series_ref[0, rows, :] = dot(w_in, grads).T.astype(BF16)


def exchange(blocks, axis):
    devices = range(len(blocks))
    return [blocks[0]] + [
        lax.ppermute(blocks[d], axis, [(i, i ^ d) for i in devices]) for d in devices if d
    ]


def swapped(block):
    return lax.ppermute(block, "seq", [(i, i ^ 1) for i in range(lax.axis_size("seq"))])


def onward(block):
    devices = lax.axis_size("seq")
    return lax.ppermute(block, "seq", [(i, (i + 2) % devices) for i in range(devices)])


after = lax.optimization_barrier


def shards(series, cotangent, w_in, w_out, taps, skip_one, skip_two, filter_one, filter_two):
    count, block, width = series.shape
    filters = filter_one.shape[0]
    sources = lax.axis_size("seq")
    copies = lax.axis_size("dp")
    length = block * sources
    units = sources // count
    group = width // units
    assert count == 1 and units % filters == 0 and block % W == 0
    assert sources % 2 == 0
    blocks = length // W
    rows = blocks * group
    scale = 1.0 / math.sqrt(count * copies * length)
    shape = jax.ShapeDtypeStruct
    m = sources // 2

    own_series, own_cot = [series.reshape(block, width)], [cotangent.reshape(block, width)]
    own_series.append(onward(own_series[0]))
    slices = call(
        functools.partial(slice_kernel, units),
        [shape((2 * block // width, width), F32)] * sources,
        flops=1000,
        moved=4 * 4 * filters * block,
    )(filter_one, filter_two)
    lines = exchange(slices, "seq")
    own_series[1], own_cot[0] = after((own_series[1], own_cot[0]))
    toeplitz = None
    for k in range(1, m):
        if k + 1 < m:
            own_series.append(onward(own_series[k]))
        own_cot.append(onward(own_cot[k - 1]))
        if k == 1:
            toeplitz = call(
                toeplitz_kernel,
                shape((2, blocks, W, W), BF16),
                [pltpu.VMEM((8, length), F32)],
                flops=2 * W * length * 200,
                moved=2 * W * length * 2,
            )(*lines)
        if k + 1 < m:
            tied = after((own_series[k + 1], own_cot[k], toeplitz))
            own_series[k + 1], own_cot[k], toeplitz = tied
    all_series = own_series + [swapped(part) for part in own_series]
    all_cot = own_cot + [swapped(part) for part in own_cot]

    skips = (skip_one.reshape(1, width), skip_two.reshape(1, width))
    fore, wide, product = call(
        functools.partial(forward_kernel, units),
        (shape((5, rows, W), BF16), shape((4, rows, W), F32), shape((rows, W), BF16)),
        [
            pltpu.VMEM((2 * rows, W), BF16),
            pltpu.VMEM((3, rows, W), F32),
            pltpu.VMEM((3 * width, width), F32),
        ],
        flops=2 * 2 * rows * length * W,
        moved=W * length * 2 * 2,
    )(*all_series, toeplitz, w_in, taps, *skips)

    each = rows // sources
    back, sent, *blocks_back = call(
        functools.partial(backward_kernel, units),
        [shape((5, rows, W), BF16), shape((sources, 4 * each, W), BF16)]
        + [shape((4 * each, W), BF16)] * sources,
        [
            pltpu.VMEM((2 * rows, W), BF16),
            pltpu.VMEM((1, rows, W), F32),
            pltpu.VMEM((width, width), F32),
        ],
        flops=2 * 2 * rows * length * W,
        moved=W * length * 2 * 2,
    )(*all_cot, toeplitz, w_out, taps, *skips, wide, product)
    blocks_back = exchange(blocks_back, "seq")

    total_rows = 4 * group + 2 * (length // width) + 16
    total = call(
        functools.partial(gradient_kernel, units),
        shape((total_rows, width), BF16),
        [
            pltpu.VMEM((2 * rows, W), BF16),
            pltpu.VMEM((W, length), F32),
            pltpu.VMEM((total_rows, width), F32),
        ],
        flops=2 * 2 * rows * length * W,
        moved=2 * length * width * 2,
    )(*all_series, *all_cot, fore, back, sent)
    totals = exchange([total] * copies, "dp")
    blocks_back, totals = after((blocks_back, totals))

    spread_rows = 4 * group + 32
    sums = call(
        functools.partial(spread_kernel, copies),
        [shape((spread_rows, width), BF16)] * sources,
        [pltpu.VMEM((total_rows, width), F32)],
        flops=copies * total_rows * width,
        moved=2 * sources * spread_rows * width,
    )(*totals)
    sums = exchange(sums, "seq")

    output, d_series = call(
        output_kernel,
        (shape(series.shape, BF16), shape(series.shape, BF16)),
        [pltpu.VMEM((block // W, 4 * width, W), F32 if group % 16 else BF16)],
        flops=2 * count * block * width * 4 * width,
        moved=2 * count * block * width * 6,
    )(*blocks_back, w_in, w_out)

    grads = call(
        functools.partial(parameter_kernel, units, scale),
        (
            shape(w_in.shape, F32),
            shape(w_out.shape, F32),
            shape(taps.shape, F32),
            shape((1, width), F32),
            shape((1, width), F32),
            shape(filter_one.shape, F32),
            shape(filter_two.shape, F32),
        ),
        [pltpu.VMEM((4 * width, width), F32)],
        flops=sources * spread_rows * width,
        moved=2 * sources * spread_rows * width,
    )(*sums)
    grad_w_in, grad_w_out, grad_taps, grad_skip_one, grad_skip_two, grad_one, grad_two = grads
    return (
        output,
        d_series,
        grad_w_in,
        grad_w_out,
        grad_taps,
        grad_skip_one.reshape(width),
        grad_skip_two.reshape(width),
        grad_one,
        grad_two,
    )


def solution(mesh):
    specs = (
        P("dp", "seq", None),
        P("dp", "seq", None),
        P(),
        P(),
        P(),
        P(),
        P(),
        P(None, "seq"),
        P(None, "seq"),
    )
    return jax.shard_map(shards, mesh=mesh, in_specs=specs, out_specs=specs, check_vma=False)
```

```python
import functools
import math

import jax
import jax.numpy as jnp
from jax import lax
from jax.experimental import pallas as pl
from jax.experimental.pallas import tpu as pltpu
from jax.sharding import PartitionSpec as P

W = 256
F32 = jnp.float32
BF16 = jnp.bfloat16
NT = (((1,), (1,)), ((), ()))
VMEM_LIMIT = 56 * 1024 * 1024


def call(body, out_shape, scratch=(), flops=0, moved=0):
    return pl.pallas_call(
        body,
        out_shape=out_shape,
        scratch_shapes=list(scratch),
        compiler_params=pltpu.CompilerParams(vmem_limit_bytes=VMEM_LIMIT),
        cost_estimate=pl.CostEstimate(flops=flops, bytes_accessed=moved, transcendentals=0),
    )


def dot(a, b):
    return jnp.dot(a, b, preferred_element_type=F32)


def dot_nt(a, b):
    return lax.dot_general(a, b, NT, preferred_element_type=F32)


def project_kernel(units, series_ref, cot_ref, w_in_ref, w_out_ref, one_ref, two_ref, out_ref):
    count, block, width = series_ref.shape
    group = width // units
    parts = block // W
    w_in_t = w_in_ref[...].T
    w_out = w_out_ref[...]
    for e in range(count):
        for part in range(parts):
            rows = pl.ds(part * W, W)
            proj = dot_nt(w_in_t, series_ref[e, rows, :]).astype(BF16)
            d_prod = dot_nt(w_out, cot_ref[e, rows, :]).astype(BF16)
            for kind in range(4):
                field = proj[kind * width : (kind + 1) * width] if kind < 3 else d_prod
                out_ref[
                    e * units : (e + 1) * units,
                    (kind * parts + part) * group : (kind * parts + part + 1) * group,
                    :,
                ] = field.reshape(units, group, W)
    lines = [
        ref[:, part * W : (part + 1) * W] for ref in (one_ref, two_ref) for part in range(parts)
    ]
    repeat = units // one_ref.shape[0]
    start = 4 * parts * group
    spare = jnp.zeros((out_ref.shape[1] - start - len(lines), W), F32)
    for u in range(units):
        row = u // repeat
        field = jnp.concatenate([line[row : row + 1] for line in lines] + [spare], axis=0)
        for e in range(count):
            out_ref[e * units + u, start:, :] = field.astype(BF16)


def build_toeplitz(fields_ref, start, toep_ref, base_ref):
    sources = fields_ref.shape[0]
    _, blocks, _, _ = toep_ref.shape
    parts = blocks // sources
    length = blocks * W
    half = W // 2
    row = lax.broadcasted_iota(jnp.int32, (8, length), 0)
    lane = lax.broadcasted_iota(jnp.int32, (16, W), 1)
    channel = lax.broadcasted_iota(jnp.int32, (16, W), 0)
    for m in range(2):
        for s in range(sources):
            lines = fields_ref[s, start : start + 16, :].astype(F32)
            for p in range(parts):
                at = (s * parts + p) * W
                base_ref[:, at : at + W] = jnp.broadcast_to(
                    lines[m * parts + p : m * parts + p + 1, :], (8, W)
                )
        base = base_ref[...]
        for bit in (1, 2, 4):
            base = jnp.where((row & bit) != 0, pltpu.roll(base, bit, 1), base)
        for q in range(half // 16):
            low = pltpu.roll(base, 16 * q, 1) if q else base
            both = jnp.concatenate([low, pltpu.roll(base, 16 * q + 8, 1)], axis=0)
            first = jnp.where(lane >= channel + 16 * q, both[:, :W], 0.0)
            both = jnp.concatenate([first, both[:, W:]], axis=1).astype(BF16)
            at = 16 * q
            moved = jnp.concatenate([jnp.zeros((16, half), BF16), both[:, :-half]], axis=1)
            for d in range(blocks):
                toep_ref[m, d, at : at + 16, :] = both[:, d * W : (d + 1) * W]
                toep_ref[m, d, half + at : half + at + 16, :] = moved[:, d * W : (d + 1) * W]


def earlier(field, j, group):
    if j == 0:
        return field
    turned = pltpu.roll(field, j, 1)
    above = jnp.concatenate([jnp.zeros((group, W), F32), turned[:-group]], axis=0)
    lane = lax.broadcasted_iota(jnp.int32, field.shape, 1)
    return jnp.where(lane < j, above, turned)


def later(field, j, group):
    if j == 0:
        return field
    turned = pltpu.roll(field, W - j, 1)
    below = jnp.concatenate([turned[group:], jnp.zeros((group, W), F32)], axis=0)
    lane = lax.broadcasted_iota(jnp.int32, field.shape, 1)
    return jnp.where(lane >= W - j, below, turned)


def own_lanes(f, group, width):
    lane = lax.broadcasted_iota(jnp.int32, (group, width), 1)
    channel = lax.broadcasted_iota(jnp.int32, (group, width), 0)
    return lane == f * group + channel


def pick(ref, kind, received):
    rows = received // 4
    field = ref[:, kind * rows : (kind + 1) * rows, :]
    return field.reshape(field.shape[0] * rows, W).astype(F32)


def operator_kernel(
    units,
    fields_ref,
    taps_ref,
    skip_one_ref,
    skip_two_ref,
    out_ref,
    kept_ref,
    pad_ref,
    toep_ref,
    base_ref,
):
    sources, received, _ = out_ref.shape
    build_toeplitz(fields_ref, received, toep_ref, base_ref)
    width = taps_ref.shape[1] // 3
    group = width // units
    rows = sources * received // 4
    blocks = rows // group
    f = lax.rem(lax.axis_index("seq"), units)
    mine = own_lanes(f, group, width)

    def column(values):
        col = jnp.sum(jnp.where(mine, values, 0.0), axis=1, keepdims=True)
        return jnp.broadcast_to(col, (group, W))

    def scaled(field, col):
        return (field.reshape(blocks, group, W) * col[None]).reshape(rows, W)

    zeros = jnp.zeros((rows, W), BF16)
    pad_ref[0:rows, :] = zeros
    pad_ref[2 * rows : 3 * rows, :] = zeros

    def causal(m, field):
        pad_ref[rows : 2 * rows, :] = field
        left = jnp.concatenate(
            [pad_ref[rows - group * d : 2 * rows - group * d, :] for d in range(blocks)], axis=1
        )
        return dot(left, toep_ref[m].reshape(blocks * W, W))

    def anticausal(m, field):
        pad_ref[rows : 2 * rows, :] = field
        left = jnp.concatenate(
            [pad_ref[rows + group * d : 2 * rows + group * d, :] for d in range(blocks)], axis=1
        )
        right = jnp.concatenate([toep_ref[m, d] for d in range(blocks)], axis=1)
        return dot_nt(left, right)

    tap = [
        [
            column(taps_ref[j : j + 1, kind * width : (kind + 1) * width])
            for j in range(3)
        ]
        for kind in range(3)
    ]
    skip_one = column(skip_one_ref[...])
    skip_two = column(skip_two_ref[...])

    def short(kind):
        field = pick(fields_ref, kind, received)
        total = scaled(field, tap[kind][0])
        for j in (1, 2):
            total = total + scaled(earlier(field, j, group), tap[kind][j])
        return total

    def keep(slot, field):
        low = field.astype(BF16)
        kept_ref[slot] = low
        return low

    def send(kind, field):
        part_rows = received // 4
        out_ref[:, kind * part_rows : (kind + 1) * part_rows, :] = field.astype(BF16).reshape(
            sources, part_rows, W
        )

    def send_back(kind, field):
        total = scaled(field, tap[kind][0])
        for j in (1, 2):
            total = total + scaled(later(field, j, group), tap[kind][j])
        send(kind, total)

    value = short(0)
    y_one = causal(0, keep(0, value)) + scaled(value, skip_one)
    gate_one = short(1)
    mid = gate_one * y_one
    y_two = causal(1, keep(1, mid)) + scaled(mid, skip_two)
    gate_two = short(2)
    send(3, gate_two * y_two)
    d_product = pick(fields_ref, 3, received)
    grad_two = d_product * gate_two
    d_gate_two = d_product * y_two
    keep(6, d_gate_two)
    send_back(2, d_gate_two)
    d_mid = anticausal(1, keep(3, grad_two)) + scaled(grad_two, skip_two)
    grad_one = d_mid * gate_one
    d_gate_one = d_mid * y_one
    keep(5, d_gate_one)
    send_back(1, d_gate_one)
    d_value = anticausal(0, keep(2, grad_one)) + scaled(grad_one, skip_one)
    keep(4, d_value)
    send_back(0, d_value)


def gradient_kernel(units, fields_ref, kept_ref, out_ref, pad_ref, corr_ref):
    sources, _, _ = fields_ref.shape
    _, rows, _ = kept_ref.shape
    _, length = corr_ref.shape
    width = out_ref.shape[1]
    blocks = length // W
    group = rows // blocks
    received = 4 * rows // sources
    half = W // 2
    lines = length // width

    pad_ref[rows : 2 * rows, :] = jnp.zeros((rows, W), BF16)
    row8 = lax.broadcasted_iota(jnp.int32, (8, length), 0)
    b = lax.broadcasted_iota(jnp.int32, (W, W), 0)
    r = lax.broadcasted_iota(jnp.int32, (W, W), 1)
    for m in range(2):
        pad_ref[0:rows, :] = kept_ref[2 + m]
        right = jnp.concatenate(
            [pad_ref[group * d : rows + group * d, :] for d in range(blocks)], axis=1
        )
        held = kept_ref[m].astype(F32).T.astype(BF16)
        corr_ref[...] = dot(held, right)
        corr_ref[:, 0:W] = jnp.where(r >= b, corr_ref[:, 0:W], 0.0)
        total = None
        for q in range(half // 8):
            upper = corr_ref[half + 8 * q : half + 8 * q + 8, :]
            upper = jnp.concatenate([upper[:, half:], jnp.zeros((8, half), F32)], axis=1)
            both = corr_ref[8 * q : 8 * q + 8, :] + upper
            if q:
                both = pltpu.roll(both, length - 8 * q, 1)
            total = both if total is None else total + both
        for bit in (1, 2, 4):
            total = jnp.where((row8 & bit) != 0, pltpu.roll(total, length - bit, 1), total)
        line = jnp.sum(total, axis=0, keepdims=True)
        for q in range(lines):
            at = m * lines + q
            out_ref[at : at + 1, :] = line[:, q * width : (q + 1) * width]

    lane = lax.broadcasted_iota(jnp.int32, (group, width), 1)
    channel = lax.broadcasted_iota(jnp.int32, (group, width), 0)
    small = [jnp.zeros((1, width), F32)] * 16

    def put(n, products):
        by_channel = jnp.sum(products.reshape(blocks, group, W), axis=0)
        col = jnp.sum(by_channel, axis=1, keepdims=True)
        mine = lane == n % units * group + channel
        small[n // units] += jnp.sum(jnp.where(mine, col, 0.0), axis=0, keepdims=True)

    for j in range(3):
        for kind in range(3):
            field = pick(fields_ref, kind, received)
            put(3 * j + kind, kept_ref[4 + kind].astype(F32) * earlier(field, j, group))
    for m in range(2):
        put(9 + m, kept_ref[2 + m].astype(F32) * kept_ref[m].astype(F32))
    out_ref[2 * lines : 2 * lines + 16, :] = jnp.concatenate(small, axis=0)


def received_field(in_ref, units, group, parts, e, kind, part):
    at = (kind * parts + part) * group
    return in_ref[e * units : (e + 1) * units, at : at + group, :].reshape(units * group, W)


def partial_kernel(units, in_ref, series_ref, cot_ref, own_ref, part_ref):
    count, block, width = series_ref.shape
    group = width // units
    parts = block // W
    w_in_part = 0.0
    w_out_part = 0.0
    for e in range(count):
        for part in range(parts):
            rows = pl.ds(part * W, W)
            field = [received_field(in_ref, units, group, parts, e, k, part) for k in range(4)]
            w_in_part += dot(jnp.concatenate(field[:3], axis=0), series_ref[e, rows, :])
            w_out_part += dot(field[3], cot_ref[e, rows, :])

    weights = jnp.concatenate([w_in_part, w_out_part], axis=0)
    targets, sent, _ = part_ref.shape
    each = weights.shape[0] // targets
    sources = in_ref.shape[0]
    lines = (own_ref.shape[0] - 16) // 2
    slots = lines // sources
    small = -(-11 // units)
    spare = jnp.zeros((sent - each - 2 * slots - small, width), F32)
    for g in range(targets):
        s = g % sources
        part_ref[g] = jnp.concatenate(
            [
                weights[g * each : (g + 1) * each],
                own_ref[s * slots : (s + 1) * slots, :],
                own_ref[lines + s * slots : lines + (s + 1) * slots, :],
                own_ref[2 * lines : 2 * lines + small, :],
                spare,
            ],
            axis=0,
        ).astype(BF16)


def output_kernel(units, in_ref, w_in_ref, w_out_ref, out_ref, d_series_ref):
    count, block, width = out_ref.shape
    group = width // units
    parts = block // W
    w_in = w_in_ref[...]
    w_out_t = w_out_ref[...].T
    for e in range(count):
        for part in range(parts):
            rows = pl.ds(part * W, W)
            field = [received_field(in_ref, units, group, parts, e, k, part) for k in range(4)]
            out_ref[e, rows, :] = dot(w_out_t, field[3]).T.astype(BF16)
            grads = jnp.concatenate(field[:3], axis=0)
            d_series_ref[e, rows, :] = dot(w_in, grads).T.astype(BF16)


def sum_kernel(in_ref, out_ref):
    targets, each, _ = out_ref.shape
    total = in_ref[0, 0:each, :].astype(F32)
    for g in range(1, targets):
        total = total + in_ref[g, 0:each, :].astype(F32)
    total = total.astype(BF16)
    for g in range(targets):
        out_ref[g] = total


def small_kernel(units, each, scale, in_ref, one_ref, two_ref, taps_ref, skip_one_ref, skip_two_ref):
    targets, _, width = in_ref.shape
    filters, block = one_ref.shape
    slots = block // width
    group = width // units
    by_unit = []
    for u in range(units):
        sums = 0.0
        for g in range(u, targets, units):
            sums += in_ref[g, each:, :].astype(F32)
        by_unit.append(sums * scale)
    repeat = units // filters
    for f in range(filters):
        sums = by_unit[f * repeat]
        for u in range(f * repeat + 1, (f + 1) * repeat):
            sums = sums + by_unit[u]
        for q in range(slots):
            one_ref[f : f + 1, q * width : (q + 1) * width] = sums[q : q + 1]
            two_ref[f : f + 1, q * width : (q + 1) * width] = sums[slots + q : slots + q + 1]

    row = lax.broadcasted_iota(jnp.int32, (units, width), 0)
    lane = lax.broadcasted_iota(jnp.int32, (units, width), 1)
    small = []
    for r in range(-(-11 // units)):
        held = jnp.concatenate([sums[2 * slots + r : 2 * slots + r + 1] for sums in by_unit], axis=0)
        turned = 0.0
        for shift in range(units):
            moved = pltpu.roll(held, shift * group, 1) if shift else held
            moved = jnp.where(lane // group == row, moved, 0.0)
            turned += pltpu.roll(moved, units - shift, 0) if shift else moved
        small += [turned[n : n + 1] for n in range(units)]
    for j in range(3):
        for kind in range(3):
            taps_ref[j : j + 1, kind * width : (kind + 1) * width] = small[3 * j + kind]
    skip_one_ref[...] = small[9]
    skip_two_ref[...] = small[10]


def weight_kernel(scale, in_ref, w_in_ref, w_out_ref):
    targets, each, width = in_ref.shape
    weights = jnp.concatenate([in_ref[g].astype(F32) for g in range(targets)], axis=0) * scale
    for kind in range(3):
        w_in_ref[:, kind * width : (kind + 1) * width] = weights[kind * width : (kind + 1) * width].T
    w_out_ref[...] = weights[3 * width :]


def all_to_all(blocks, axis):
    return lax.all_to_all(blocks, axis, split_axis=0, concat_axis=0, tiled=True)


def shards(series, cotangent, w_in, w_out, taps, skip_one, skip_two, filter_one, filter_two):
    count, block, width = series.shape
    filters = filter_one.shape[0]
    sources = lax.axis_size("seq")
    copies = lax.axis_size("dp")
    length = block * sources
    units = sources // count
    group = width // units
    assert sources == count * units and units % filters == 0 and block % W == 0
    blocks = length // W
    rows = blocks * group
    scale = 1.0 / math.sqrt(count * copies * length)
    shape = jax.ShapeDtypeStruct

    devices = sources * copies
    packed = 4 * (block // W) * group
    fields = call(
        functools.partial(project_kernel, units),
        shape((sources, packed + 16, W), BF16),
        flops=2 * count * block * width * 4 * width,
        moved=8 * count * block * width * 4,
    )(series, cotangent, w_in, w_out, filter_one, filter_two)
    fields = all_to_all(fields, "seq")

    sent, kept = call(
        functools.partial(operator_kernel, units),
        (shape((sources, packed, W), BF16), shape((7, rows, W), BF16)),
        [
            pltpu.VMEM((3 * rows, W), BF16),
            pltpu.VMEM((2, blocks, W, W), BF16),
            pltpu.VMEM((8, length), F32),
        ],
        flops=4 * 2 * rows * length * W,
        moved=2 * W * length * 2 * 2,
    )(fields, taps, skip_one.reshape(1, width), skip_two.reshape(1, width))

    back = all_to_all(sent, "seq")

    own = call(
        functools.partial(gradient_kernel, units),
        shape((2 * (length // width) + 16, width), F32),
        [pltpu.VMEM((2 * rows, W), BF16), pltpu.VMEM((W, length), F32)],
        flops=2 * 2 * rows * length * W,
        moved=2 * length * width * 2,
    )(fields, kept)

    each = 4 * width // devices
    sent_rows = -(-(each + 2 * (block // width) + -(-11 // units)) // 16) * 16
    partial = call(
        functools.partial(partial_kernel, units),
        shape((devices, sent_rows, width), BF16),
        flops=2 * count * block * width * 4 * width,
        moved=2 * count * block * width * 6,
    )(back, series, cotangent, own)
    partial = all_to_all(partial, ("dp", "seq"))

    output, d_series = call(
        functools.partial(output_kernel, units),
        (shape(series.shape, BF16), shape(series.shape, BF16)),
        flops=2 * count * block * width * 4 * width,
        moved=2 * count * block * width * 6,
    )(back, w_in, w_out)

    sums = call(
        sum_kernel,
        shape((devices, each, width), BF16),
        flops=devices * each * width,
        moved=4 * devices * each * width,
    )(partial)
    sums = all_to_all(sums, ("dp", "seq"))

    grad_one, grad_two, grad_taps, grad_skip_one, grad_skip_two = call(
        functools.partial(small_kernel, units, each, scale),
        (
            shape(filter_one.shape, F32),
            shape(filter_two.shape, F32),
            shape(taps.shape, F32),
            shape((1, width), F32),
            shape((1, width), F32),
        ),
        flops=devices * sent_rows * width,
        moved=4 * devices * sent_rows * width,
    )(partial)
    grad_w_in, grad_w_out = call(
        functools.partial(weight_kernel, scale),
        (shape(w_in.shape, F32), shape(w_out.shape, F32)),
        flops=devices * each * width,
        moved=2 * devices * each * width,
    )(sums)
    return (
        output,
        d_series,
        grad_w_in,
        grad_w_out,
        grad_taps,
        grad_skip_one.reshape(width),
        grad_skip_two.reshape(width),
        grad_one,
        grad_two,
    )


def solution(mesh):
    specs = (
        P("dp", "seq", None),
        P("dp", "seq", None),
        P(),
        P(),
        P(),
        P(),
        P(),
        P(None, "seq"),
        P(None, "seq"),
    )
    return jax.shard_map(shards, mesh=mesh, in_specs=specs, out_specs=specs, check_vma=False)
```

```python
import functools
import math

import jax
import jax.numpy as jnp
from jax import lax
from jax.experimental import pallas as pl
from jax.experimental.pallas import tpu as pltpu
from jax.sharding import PartitionSpec as P

W = 256
F32 = jnp.float32
BF16 = jnp.bfloat16
NT = (((1,), (1,)), ((), ()))
VMEM_LIMIT = 56 * 1024 * 1024


def call(body, out_shape, scratch=(), flops=0, moved=0):
    return pl.pallas_call(
        body,
        out_shape=out_shape,
        scratch_shapes=list(scratch),
        compiler_params=pltpu.CompilerParams(vmem_limit_bytes=VMEM_LIMIT),
        cost_estimate=pl.CostEstimate(flops=flops, bytes_accessed=moved, transcendentals=0),
    )


def dot(a, b):
    return jnp.dot(a, b, preferred_element_type=F32)


def dot_nt(a, b):
    return lax.dot_general(a, b, NT, preferred_element_type=F32)


def project_kernel(units, series_ref, cot_ref, w_in_ref, w_out_ref, one_ref, two_ref, out_ref):
    count, block, width = series_ref.shape
    group = width // units
    parts = block // W
    w_in_t = w_in_ref[...].T
    w_out = w_out_ref[...]
    for e in range(count):
        for part in range(parts):
            rows = pl.ds(part * W, W)
            proj = dot_nt(w_in_t, series_ref[e, rows, :]).astype(BF16)
            d_prod = dot_nt(w_out, cot_ref[e, rows, :]).astype(BF16)
            for kind in range(4):
                field = proj[kind * width : (kind + 1) * width] if kind < 3 else d_prod
                out_ref[
                    e * units : (e + 1) * units,
                    (kind * parts + part) * group : (kind * parts + part + 1) * group,
                    :,
                ] = field.reshape(units, group, W)
    lines = [
        ref[:, part * W : (part + 1) * W] for ref in (one_ref, two_ref) for part in range(parts)
    ]
    repeat = units // one_ref.shape[0]
    start = 4 * parts * group
    spare = jnp.zeros((out_ref.shape[1] - start - len(lines), W), F32)
    for u in range(units):
        row = u // repeat
        field = jnp.concatenate([line[row : row + 1] for line in lines] + [spare], axis=0)
        for e in range(count):
            out_ref[e * units + u, start:, :] = field.astype(BF16)


def build_toeplitz(fields_ref, start, toep_ref, base_ref):
    sources = fields_ref.shape[0]
    _, blocks, _, _ = toep_ref.shape
    parts = blocks // sources
    length = blocks * W
    half = W // 2
    row = lax.broadcasted_iota(jnp.int32, (8, length), 0)
    lane = lax.broadcasted_iota(jnp.int32, (16, W), 1)
    channel = lax.broadcasted_iota(jnp.int32, (16, W), 0)
    for m in range(2):
        for s in range(sources):
            lines = fields_ref[s, start : start + 16, :].astype(F32)
            for p in range(parts):
                at = (s * parts + p) * W
                base_ref[:, at : at + W] = jnp.broadcast_to(
                    lines[m * parts + p : m * parts + p + 1, :], (8, W)
                )
        base = base_ref[...]
        for bit in (1, 2, 4):
            base = jnp.where((row & bit) != 0, pltpu.roll(base, bit, 1), base)
        for q in range(half // 16):
            low = pltpu.roll(base, 16 * q, 1) if q else base
            both = jnp.concatenate([low, pltpu.roll(base, 16 * q + 8, 1)], axis=0)
            first = jnp.where(lane >= channel + 16 * q, both[:, :W], 0.0)
            both = jnp.concatenate([first, both[:, W:]], axis=1).astype(BF16)
            at = 16 * q
            moved = jnp.concatenate([jnp.zeros((16, half), BF16), both[:, :-half]], axis=1)
            for d in range(blocks):
                toep_ref[m, d, at : at + 16, :] = both[:, d * W : (d + 1) * W]
                toep_ref[m, d, half + at : half + at + 16, :] = moved[:, d * W : (d + 1) * W]


def earlier(field, j, group):
    if j == 0:
        return field
    turned = pltpu.roll(field, j, 1)
    above = jnp.concatenate([jnp.zeros((group, W), F32), turned[:-group]], axis=0)
    lane = lax.broadcasted_iota(jnp.int32, field.shape, 1)
    return jnp.where(lane < j, above, turned)


def later(field, j, group):
    if j == 0:
        return field
    turned = pltpu.roll(field, W - j, 1)
    below = jnp.concatenate([turned[group:], jnp.zeros((group, W), F32)], axis=0)
    lane = lax.broadcasted_iota(jnp.int32, field.shape, 1)
    return jnp.where(lane >= W - j, below, turned)


def own_lanes(f, group, width):
    lane = lax.broadcasted_iota(jnp.int32, (group, width), 1)
    channel = lax.broadcasted_iota(jnp.int32, (group, width), 0)
    return lane == f * group + channel


def pick(ref, kind, received):
    rows = received // 4
    field = ref[:, kind * rows : (kind + 1) * rows, :]
    return field.reshape(field.shape[0] * rows, W).astype(F32)


def operator_kernel(
    units,
    fields_ref,
    taps_ref,
    skip_one_ref,
    skip_two_ref,
    out_ref,
    kept_ref,
    pad_ref,
    toep_ref,
    base_ref,
):
    sources, received, _ = out_ref.shape
    build_toeplitz(fields_ref, received, toep_ref, base_ref)
    width = taps_ref.shape[1] // 3
    group = width // units
    rows = sources * received // 4
    blocks = rows // group
    f = lax.rem(lax.axis_index("seq"), units)
    mine = own_lanes(f, group, width)

    def column(values):
        col = jnp.sum(jnp.where(mine, values, 0.0), axis=1, keepdims=True)
        return jnp.broadcast_to(col, (group, W))

    def scaled(field, col):
        return (field.reshape(blocks, group, W) * col[None]).reshape(rows, W)

    zeros = jnp.zeros((rows, W), BF16)
    pad_ref[0:rows, :] = zeros
    pad_ref[2 * rows : 3 * rows, :] = zeros

    def causal(m, field):
        pad_ref[rows : 2 * rows, :] = field
        left = jnp.concatenate(
            [pad_ref[rows - group * d : 2 * rows - group * d, :] for d in range(blocks)], axis=1
        )
        return dot(left, toep_ref[m].reshape(blocks * W, W))

    def anticausal(m, field):
        pad_ref[rows : 2 * rows, :] = field
        left = jnp.concatenate(
            [pad_ref[rows + group * d : 2 * rows + group * d, :] for d in range(blocks)], axis=1
        )
        right = jnp.concatenate([toep_ref[m, d] for d in range(blocks)], axis=1)
        return dot_nt(left, right)

    tap = [
        [
            column(taps_ref[j : j + 1, kind * width : (kind + 1) * width])
            for j in range(3)
        ]
        for kind in range(3)
    ]
    skip_one = column(skip_one_ref[...])
    skip_two = column(skip_two_ref[...])

    def short(kind):
        field = pick(fields_ref, kind, received)
        total = scaled(field, tap[kind][0])
        for j in (1, 2):
            total = total + scaled(earlier(field, j, group), tap[kind][j])
        return total

    def keep(slot, field):
        low = field.astype(BF16)
        kept_ref[slot] = low
        return low

    def send(kind, field):
        part_rows = received // 4
        out_ref[:, kind * part_rows : (kind + 1) * part_rows, :] = field.astype(BF16).reshape(
            sources, part_rows, W
        )

    def send_back(kind, field):
        total = scaled(field, tap[kind][0])
        for j in (1, 2):
            total = total + scaled(later(field, j, group), tap[kind][j])
        send(kind, total)

    value = short(0)
    y_one = causal(0, keep(0, value)) + scaled(value, skip_one)
    gate_one = short(1)
    mid = gate_one * y_one
    y_two = causal(1, keep(1, mid)) + scaled(mid, skip_two)
    gate_two = short(2)
    send(3, gate_two * y_two)
    d_product = pick(fields_ref, 3, received)
    grad_two = d_product * gate_two
    d_gate_two = d_product * y_two
    keep(6, d_gate_two)
    send_back(2, d_gate_two)
    d_mid = anticausal(1, keep(3, grad_two)) + scaled(grad_two, skip_two)
    grad_one = d_mid * gate_one
    d_gate_one = d_mid * y_one
    keep(5, d_gate_one)
    send_back(1, d_gate_one)
    d_value = anticausal(0, keep(2, grad_one)) + scaled(grad_one, skip_one)
    keep(4, d_value)
    send_back(0, d_value)


def places(gathered):
    m = len(gathered) // 2
    me = lax.axis_index("seq")
    row, core = me // 2, lax.rem(me, 2)
    for k in range(m):
        place = 2 * lax.rem(row - k + m, m)
        yield place + core, gathered[k]
        yield place + 1 - core, gathered[m + k]

def weight_kernel(units, *refs):
    sources = (len(refs) - 2) // 2
    series = refs[:sources]
    cot = refs[sources : 2 * sources]
    sent_ref, out_ref = refs[2 * sources :]
    width = out_ref.shape[1]
    group = width // units
    parts = sent_ref.shape[1] // 4 // group

    def weights(kinds, gathered):
        left, right = [], []
        for place, block in places(gathered):
            right.append(block[...])
            for p in range(parts):
                at = [(kind * parts + p) * group for kind in kinds]
                left.append(jnp.concatenate([sent_ref[place, i : i + group, :] for i in at], axis=0))
        return dot(jnp.concatenate(left, axis=1), jnp.concatenate(right, axis=0))

    total = jnp.concatenate([weights((0, 1, 2), series), weights((3,), cot)], axis=0)
    out_ref[...] = total.astype(BF16)


def gradient_kernel(units, fields_ref, kept_ref, low_ref, pad_ref, corr_ref, out_ref):
    sources, received, _ = fields_ref.shape
    _, rows, _ = kept_ref.shape
    _, length = corr_ref.shape
    width = out_ref.shape[1]
    blocks = length // W
    group = rows // blocks
    half = W // 2
    u = lax.rem(lax.axis_index("seq"), units)
    mine = own_lanes(u, group, width)
    lines = length // width

    pad_ref[rows : 2 * rows, :] = jnp.zeros((rows, W), BF16)
    row8 = lax.broadcasted_iota(jnp.int32, (8, length), 0)
    b = lax.broadcasted_iota(jnp.int32, (W, W), 0)
    r = lax.broadcasted_iota(jnp.int32, (W, W), 1)
    for order in range(2):
        pad_ref[0:rows, :] = kept_ref[2 + order]
        right = jnp.concatenate(
            [pad_ref[group * d : rows + group * d, :] for d in range(blocks)], axis=1
        )
        held = kept_ref[order].astype(F32).T.astype(BF16)
        corr_ref[...] = dot(held, right)
        corr_ref[:, 0:W] = jnp.where(r >= b, corr_ref[:, 0:W], 0.0)
        total = None
        for q in range(half // 8):
            upper = corr_ref[half + 8 * q : half + 8 * q + 8, :]
            upper = jnp.concatenate([upper[:, half:], jnp.zeros((8, half), F32)], axis=1)
            both = corr_ref[8 * q : 8 * q + 8, :] + upper
            if q:
                both = pltpu.roll(both, length - 8 * q, 1)
            total = both if total is None else total + both
        for bit in (1, 2, 4):
            total = jnp.where((row8 & bit) != 0, pltpu.roll(total, length - bit, 1), total)
        line = jnp.sum(total, axis=0, keepdims=True)
        for q in range(lines):
            at = order * lines + q
            out_ref[at : at + 1, :] = line[:, q * width : (q + 1) * width]

    def spread(products):
        by_channel = jnp.sum(products.reshape(blocks, group, W), axis=0)
        col = jnp.sum(by_channel, axis=1, keepdims=True)
        return jnp.sum(jnp.where(mine, col, 0.0), axis=0, keepdims=True)

    small = []
    for j in range(3):
        for kind in range(3):
            field = pick(fields_ref, kind, 4 * rows // sources)
            small.append(spread(kept_ref[4 + kind].astype(F32) * earlier(field, j, group)))
    for order in range(2):
        small.append(spread(kept_ref[2 + order].astype(F32) * kept_ref[order].astype(F32)))
    out_ref[2 * lines :, :] = jnp.concatenate(
        small + [jnp.zeros((16 - len(small), width), F32)], axis=0
    )
    low_ref[...] = out_ref[...].astype(BF16)


def spread_kernel(copies, *refs):
    weight_refs, rest_refs = refs[:copies], refs[copies : 2 * copies]
    out_ref, sum_ref = refs[2 * copies :]
    targets, _, width = out_ref.shape

    def total(parts):
        result = parts[0][...].astype(F32)
        for ref in parts[1:]:
            result = result + ref[...].astype(F32)
        return result

    weights = total(weight_refs).astype(BF16)
    base = weights.shape[0]
    sum_ref[...] = total(rest_refs)
    lines = (sum_ref.shape[0] - 16) // 2
    each = lines // targets
    for s in range(targets):
        out_ref[s, 0:base, :] = weights
        out_ref[s, base:, :] = jnp.concatenate(
            [
                sum_ref[s * each : (s + 1) * each, :],
                sum_ref[lines + s * each : lines + (s + 1) * each, :],
                sum_ref[2 * lines :, :],
                jnp.zeros((16 - 2 * each, width), F32),
            ],
            axis=0,
        ).astype(BF16)


def parameter_kernel(
    units, scale, in_ref, w_in_ref, w_out_ref, taps_ref, skip_one_ref, skip_two_ref, one_ref, two_ref
):
    sources, _, width = in_ref.shape
    group = width // units
    count = sources // units
    each = one_ref.shape[1] // width

    def total(first, last):
        parts = [in_ref[e * units : (e + 1) * units, first:last, :] for e in range(count)]
        result = parts[0].astype(F32)
        for part in parts[1:]:
            result = result + part.astype(F32)
        return result

    blocks = total(0, 4 * group) * scale
    for kind in range(3):
        rows = blocks[:, kind * group : (kind + 1) * group, :].reshape(width, width)
        w_in_ref[:, kind * width : (kind + 1) * width] = rows.T
    w_out_ref[...] = blocks[:, 3 * group : 4 * group, :].reshape(width, width)
    rest = total(4 * group, in_ref.shape[1]) * scale
    filters = one_ref.shape[0]
    for q in range(each):
        for ref, at in ((one_ref, q), (two_ref, each + q)):
            by_unit = rest[:, at, :].reshape(filters, units // filters, width)
            ref[:, q * width : (q + 1) * width] = jnp.sum(by_unit, axis=1)
    small = jnp.sum(rest[:, 2 * each : 2 * each + 16, :], axis=0)
    for j in range(3):
        for kind in range(3):
            n = 3 * j + kind
            taps_ref[j : j + 1, kind * width : (kind + 1) * width] = small[n : n + 1]
    skip_one_ref[...] = small[9:10]
    skip_two_ref[...] = small[10:11]


def output_kernel(units, in_ref, w_in_ref, w_out_ref, out_ref, d_series_ref):
    count, block, width = out_ref.shape
    group = width // units
    parts = block // W
    w_in = w_in_ref[...]
    w_out_t = w_out_ref[...].T

    def field(e, kind, part):
        at = (kind * parts + part) * group
        return in_ref[e * units : (e + 1) * units, at : at + group, :].reshape(width, W)

    for e in range(count):
        for part in range(parts):
            rows = pl.ds(part * W, W)
            out_ref[e, rows, :] = dot(w_out_t, field(e, 3, part)).T.astype(BF16)
            grads = jnp.concatenate([field(e, kind, part) for kind in range(3)], axis=0)
            d_series_ref[e, rows, :] = dot(w_in, grads).T.astype(BF16)


def all_to_all(blocks, axis):
    return lax.all_to_all(blocks, axis, split_axis=0, concat_axis=0, tiled=True)


def exchange(block, axis, routes):
    devices = lax.axis_size(axis)
    return [lax.ppermute(block, axis, [(i, route(i) % devices) for i in range(devices)]) for route in routes]


def onward(block):
    return exchange(block, "seq", [lambda i: i + 2])[0]


def swap(block):
    return exchange(block, "seq", [lambda i: i ^ 1])[0]


after = lax.optimization_barrier


def shards(series, cotangent, w_in, w_out, taps, skip_one, skip_two, filter_one, filter_two):
    count, block, width = series.shape
    filters = filter_one.shape[0]
    sources = lax.axis_size("seq")
    copies = lax.axis_size("dp")
    length = block * sources
    units = sources // count
    group = width // units
    assert count == 1 and units % filters == 0 and block % W == 0
    blocks = length // W
    rows = blocks * group
    scale = 1.0 / math.sqrt(count * copies * length)
    shape = jax.ShapeDtypeStruct
    m = sources // 2

    packed = 4 * (block // W) * group
    fields = call(
        functools.partial(project_kernel, units),
        shape((sources, packed + 16, W), BF16),
        flops=2 * count * block * width * 4 * width,
        moved=8 * count * block * width * 4,
    )(series, cotangent, w_in, w_out, filter_one, filter_two)
    fields = all_to_all(fields, "seq")

    own_series, own_cot = [series.reshape(block, width)], [cotangent.reshape(block, width)]

    def turn():
        own_series.append(onward(own_series[-1]))
        own_cot.append(onward(own_cot[-1]))

    turn()
    tied = after((own_series[-1], own_cot[-1], fields))
    own_series[-1], own_cot[-1], fields = tied
    turn()

    sent, kept = call(
        functools.partial(operator_kernel, units),
        (shape((sources, packed, W), BF16), shape((7, rows, W), BF16)),
        [
            pltpu.VMEM((3 * rows, W), BF16),
            pltpu.VMEM((2, blocks, W, W), BF16),
            pltpu.VMEM((8, length), F32),
        ],
        flops=4 * 2 * rows * length * W,
        moved=2 * W * length * 2 * 2,
    )(fields, taps, skip_one.reshape(1, width), skip_two.reshape(1, width))

    tied = after((own_series[-1], own_cot[-1], sent))
    own_series[-1], own_cot[-1], sent = tied
    while len(own_series) < m:
        turn()
    all_series = own_series + [swap(part) for part in own_series]
    all_cot = own_cot + [swap(part) for part in own_cot]
    back = all_to_all(sent, "seq")

    around = [lambda i, d=d: i + d for d in range(1, copies)]
    rest_rows = 2 * (length // width) + 16
    rest = call(
        functools.partial(gradient_kernel, units),
        shape((rest_rows, width), BF16),
        [
            pltpu.VMEM((2 * rows, W), BF16),
            pltpu.VMEM((W, length), F32),
            pltpu.VMEM((rest_rows, width), F32),
        ],
        flops=2 * 2 * rows * length * W,
        moved=2 * length * width * 2,
    )(fields, kept)
    rests = [rest] + exchange(rest, "dp", around)
    weights = call(
        functools.partial(weight_kernel, units),
        shape((4 * group, width), BF16),
        flops=2 * length * width * 4 * group,
        moved=2 * length * width * 2,
    )(*all_series, *all_cot, sent)
    weights = [weights] + exchange(weights, "dp", around)

    spread_rows = 4 * group + 32
    sums = call(
        functools.partial(spread_kernel, copies),
        shape((sources, spread_rows, width), BF16),
        [pltpu.VMEM((rest_rows, width), F32)],
        flops=copies * spread_rows * width,
        moved=2 * sources * spread_rows * width,
    )(*weights, *rests)
    sums, back = after((sums, back))
    sums = all_to_all(sums, "seq")

    output, d_series = call(
        functools.partial(output_kernel, units),
        (shape(series.shape, BF16), shape(series.shape, BF16)),
        flops=2 * count * block * width * 4 * width,
        moved=2 * count * block * width * 6,
    )(back, w_in, w_out)

    grads = call(
        functools.partial(parameter_kernel, units, scale),
        (
            shape(w_in.shape, F32),
            shape(w_out.shape, F32),
            shape(taps.shape, F32),
            shape((1, width), F32),
            shape((1, width), F32),
            shape(filter_one.shape, F32),
            shape(filter_two.shape, F32),
        ),
        flops=sources * spread_rows * width,
        moved=2 * sources * spread_rows * width,
    )(sums)
    grad_w_in, grad_w_out, grad_taps, grad_skip_one, grad_skip_two, grad_one, grad_two = grads
    return (
        output,
        d_series,
        grad_w_in,
        grad_w_out,
        grad_taps,
        grad_skip_one.reshape(width),
        grad_skip_two.reshape(width),
        grad_one,
        grad_two,
    )


def solution(mesh):
    specs = (
        P("dp", "seq", None),
        P("dp", "seq", None),
        P(),
        P(),
        P(),
        P(),
        P(),
        P(None, "seq"),
        P(None, "seq"),
    )
    return jax.shard_map(shards, mesh=mesh, in_specs=specs, out_specs=specs, check_vma=False)
```

```python
import functools
import math

import jax
import jax.numpy as jnp
from jax import lax
from jax.experimental import pallas as pl
from jax.experimental.pallas import tpu as pltpu
from jax.sharding import PartitionSpec as P

W = 256
F32 = jnp.float32
BF16 = jnp.bfloat16
NT = (((1,), (1,)), ((), ()))
VMEM_LIMIT = 56 * 1024 * 1024


def call(body, out_shape, scratch=(), flops=0, moved=0):
    return pl.pallas_call(
        body,
        out_shape=out_shape,
        scratch_shapes=list(scratch),
        compiler_params=pltpu.CompilerParams(vmem_limit_bytes=VMEM_LIMIT),
        cost_estimate=pl.CostEstimate(flops=flops, bytes_accessed=moved, transcendentals=0),
    )


def dot(a, b):
    return jnp.dot(a, b, preferred_element_type=F32)


def dot_nt(a, b):
    return lax.dot_general(a, b, NT, preferred_element_type=F32)


def lanes_of(field):
    return lax.broadcasted_iota(jnp.int32, field.shape, field.ndim - 1)


def turned(field, shift):
    return pltpu.roll(field, shift, field.ndim - 1)


def earlier_parts(parts, j, before):
    result = []
    for held in parts:
        result.append(jnp.where(lanes_of(held) < j, turned(before, j), turned(held, j)))
        before = held
    return result


def later_parts(parts, j, behind):
    result = []
    for held, following in zip(parts, parts[1:] + [behind]):
        edge = lanes_of(held) >= W - j
        result.append(jnp.where(edge, turned(following, W - j), turned(held, W - j)))
    return result


def gate_taps(taps_ref):
    width = taps_ref.shape[1] // 3
    rows = jnp.concatenate([taps_ref[:, 2 * width :], jnp.zeros((5, width), F32)], axis=0)
    cols = jnp.concatenate([rows] * (width // 8), axis=0).T
    return [cols[:, j : j + 1] for j in range(3)]


def gate_local(second, cols):
    zeros = jnp.zeros_like(second[0])
    total = [cols[0] * held for held in second]
    for j in (1, 2):
        moved = earlier_parts(second, j, zeros)
        total = [have + cols[j] * held for have, held in zip(total, moved)]
    return total


def project_kernel(units, series_ref, cot_ref, w_in_ref, w_out_ref, taps_ref, one_ref, two_ref, out_ref):
    _, block, width = series_ref.shape
    group = width // units
    parts = block // W
    w_in_t = w_in_ref[...].T
    w_out = w_out_ref[...]
    proj = [dot_nt(w_in_t, series_ref[0, p * W : (p + 1) * W, :]) for p in range(parts)]
    d_prod = [dot_nt(w_out, cot_ref[0, p * W : (p + 1) * W, :]) for p in range(parts)]
    second = [held[2 * width :] for held in proj]
    gate = gate_local(second, gate_taps(taps_ref))
    for p in range(parts):
        fields = [proj[p][:width], proj[p][width : 2 * width], d_prod[p] * gate[p]]
        for kind, field in enumerate(fields):
            at = (kind * parts + p) * group
            out_ref[:, at : at + group, :] = field.astype(BF16).reshape(units, group, W)

    lane = lanes_of(second[0])
    edges = jnp.where((lane >= 128) & (lane < 130), turned(second[-1], 130), 0.0)
    edges = jnp.where((lane >= 130) & (lane < 132), turned(d_prod[0], 130), edges)
    lines = [
        ref[:, q * width : (q + 1) * width]
        for ref in (one_ref, two_ref)
        for q in range(block // width)
    ]
    repeat = units // one_ref.shape[0]
    for u in range(units):
        row = u // repeat
        held = jnp.concatenate([line[row : row + 1] for line in lines], axis=0)
        held = jnp.concatenate([held, jnp.zeros((held.shape[0], W - width), F32)], axis=1)
        held = jnp.concatenate([held, jnp.zeros((16 - held.shape[0], W), F32)], axis=0)
        edge = edges[u * group : (u + 1) * group]
        if group < 16:
            edge = jnp.concatenate([edge, jnp.zeros((16 - group, W), F32)], axis=0)
        out_ref[u, 3 * parts * group :, :] = (held + edge).astype(BF16)


def gate_kernel(series_ref, cot_ref, w_in_ref, w_out_ref, taps_ref, out_ref):
    _, block, width = series_ref.shape
    parts = block // W
    w_two_t = w_in_ref[:, 2 * width :].T
    w_out = w_out_ref[...]
    second = [dot_nt(w_two_t, series_ref[0, p * W : (p + 1) * W, :]) for p in range(parts)]
    gate = gate_local(second, gate_taps(taps_ref))
    for p in range(parts):
        out_ref[0, p] = second[p]
        out_ref[1, p] = gate[p]
        out_ref[2, p] = dot_nt(w_out, cot_ref[0, p * W : (p + 1) * W, :])


def build_toeplitz(fields_ref, start, toep_ref, base_ref):
    sources = fields_ref.shape[0]
    _, blocks, _, _ = toep_ref.shape
    width = W // 2
    slots = blocks // sources * W // width
    length = blocks * W
    half = W // 2
    row = lax.broadcasted_iota(jnp.int32, (8, length), 0)
    lane = lax.broadcasted_iota(jnp.int32, (16, W), 1)
    channel = lax.broadcasted_iota(jnp.int32, (16, W), 0)
    for m in range(2):
        for s in range(sources):
            lines = fields_ref[s, start : start + 16, :].astype(F32)
            for q in range(slots):
                at = (s * slots + q) * width
                base_ref[:, at : at + width] = jnp.broadcast_to(
                    lines[m * slots + q : m * slots + q + 1, :width], (8, width)
                )
        base = base_ref[...]
        for bit in (1, 2, 4):
            base = jnp.where((row & bit) != 0, pltpu.roll(base, bit, 1), base)
        for q in range(half // 16):
            low = pltpu.roll(base, 16 * q, 1) if q else base
            both = jnp.concatenate([low, pltpu.roll(base, 16 * q + 8, 1)], axis=0)
            first = jnp.where(lane >= channel + 16 * q, both[:, :W], 0.0)
            both = jnp.concatenate([first, both[:, W:]], axis=1).astype(BF16)
            at = 16 * q
            moved = jnp.concatenate([jnp.zeros((16, half), BF16), both[:, :-half]], axis=1)
            for d in range(blocks):
                toep_ref[m, d, at : at + 16, :] = both[:, d * W : (d + 1) * W]
                toep_ref[m, d, half + at : half + at + 16, :] = moved[:, d * W : (d + 1) * W]


def earlier(field, j, group):
    if j == 0:
        return field
    turned = pltpu.roll(field, j, 1)
    above = jnp.concatenate([jnp.zeros((group, W), F32), turned[:-group]], axis=0)
    lane = lax.broadcasted_iota(jnp.int32, field.shape, 1)
    return jnp.where(lane < j, above, turned)


def later(field, j, group):
    if j == 0:
        return field
    turned = pltpu.roll(field, W - j, 1)
    below = jnp.concatenate([turned[group:], jnp.zeros((group, W), F32)], axis=0)
    lane = lax.broadcasted_iota(jnp.int32, field.shape, 1)
    return jnp.where(lane >= W - j, below, turned)


def own_lanes(f, group, width):
    lane = lax.broadcasted_iota(jnp.int32, (group, width), 1)
    channel = lax.broadcasted_iota(jnp.int32, (group, width), 0)
    return lane == f * group + channel


def pick(ref, kind, received):
    rows = received
    field = ref[:, kind * rows : (kind + 1) * rows, :]
    return field.reshape(field.shape[0] * rows, W).astype(F32)


def operator_kernel(
    units,
    fields_ref,
    taps_ref,
    skip_one_ref,
    skip_two_ref,
    out_ref,
    kept_ref,
    pad_ref,
    toep_ref,
    base_ref,
):
    sources, _, _ = out_ref.shape
    _, rows, _ = kept_ref.shape
    each = rows // sources
    start = 3 * each
    build_toeplitz(fields_ref, start, toep_ref, base_ref)
    width = taps_ref.shape[1] // 3
    group = width // units
    blocks = rows // group
    u = lax.rem(lax.axis_index("seq"), units)
    mine = own_lanes(u, group, width)

    def column(values):
        col = jnp.sum(jnp.where(mine, values, 0.0), axis=1, keepdims=True)
        return jnp.broadcast_to(col, (group, W))

    def scaled(field, col):
        return (field.reshape(blocks, group, W) * col[None]).reshape(rows, W)

    zeros = jnp.zeros((rows, W), BF16)
    pad_ref[0:rows, :] = zeros
    pad_ref[2 * rows : 3 * rows, :] = zeros

    def causal(m, field):
        pad_ref[rows : 2 * rows, :] = field
        left = jnp.concatenate(
            [pad_ref[rows - group * d : 2 * rows - group * d, :] for d in range(blocks)], axis=1
        )
        return dot(left, toep_ref[m].reshape(blocks * W, W))

    def anticausal(m, field):
        pad_ref[rows : 2 * rows, :] = field
        left = jnp.concatenate(
            [pad_ref[rows + group * d : 2 * rows + group * d, :] for d in range(blocks)], axis=1
        )
        right = jnp.concatenate([toep_ref[m, d] for d in range(blocks)], axis=1)
        return dot_nt(left, right)

    tap = [
        [
            column(taps_ref[j : j + 1, kind * width : (kind + 1) * width])
            for j in range(3)
        ]
        for kind in range(3)
    ]
    skip_one = column(skip_one_ref[...])
    skip_two = column(skip_two_ref[...])

    def short(kind):
        field = pick(fields_ref, kind, each)
        total = scaled(field, tap[kind][0])
        for j in (1, 2):
            total = total + scaled(earlier(field, j, group), tap[kind][j])
        return total

    def keep(slot, field):
        low = field.astype(BF16)
        kept_ref[slot] = low
        return low

    def send(kind, field):
        out_ref[:, kind * each : (kind + 1) * each, :] = field.astype(BF16).reshape(sources, each, W)

    def send_back(kind, field):
        total = scaled(field, tap[kind][0])
        for j in (1, 2):
            total = total + scaled(later(field, j, group), tap[kind][j])
        send(kind, total)

    edges = fields_ref[:, start : start + 16, :].astype(F32)[:, :group]
    none = jnp.zeros((1, group, W), F32)
    before = jnp.concatenate([none, edges[:-1]], axis=0)
    following = jnp.concatenate([edges[1:], none], axis=0)
    lane = lanes_of(edges)
    reach = tap[2][2] * turned(before, 128)
    reach = reach + jnp.where(lane < 1, tap[2][1] * turned(before, 127), 0.0)
    reach = jnp.where(lane < 2, turned(edges, 126) * reach, 0.0)
    grad_two = pick(fields_ref, 2, each).reshape(sources, each, W)
    grad_two = jnp.concatenate([grad_two[:, :group] + reach, grad_two[:, group:]], axis=1)
    grad_two = grad_two.reshape(rows, W)

    value = short(0)
    y_one = causal(0, keep(0, value)) + scaled(value, skip_one)
    gate_one = short(1)
    mid = gate_one * y_one
    y_two = causal(1, keep(1, mid)) + scaled(mid, skip_two)
    send(2, y_two)
    heads = y_two.reshape(sources, each, W)[1:, :group]
    heads = jnp.concatenate([heads, none], axis=0)
    edges = jnp.where(lane < 4, turned(following, 128) * turned(heads, 2), 0.0)
    edges = jnp.where(lane < 2, turned(before, 128), edges)
    if group < 16:
        edges = jnp.concatenate([edges, jnp.zeros((sources, 16 - group, W), F32)], axis=1)
    out_ref[:, start:, :] = edges.astype(BF16)
    d_mid = anticausal(1, keep(3, grad_two)) + scaled(grad_two, skip_two)
    grad_one = d_mid * gate_one
    d_gate_one = d_mid * y_one
    keep(5, d_gate_one)
    send_back(1, d_gate_one)
    d_value = anticausal(0, keep(2, grad_one)) + scaled(grad_one, skip_one)
    keep(4, d_value)
    send_back(0, d_value)


def gradient_kernel(units, fields_ref, kept_ref, out_ref, pad_ref, corr_ref):
    sources, _, _ = fields_ref.shape
    _, rows, _ = kept_ref.shape
    _, length = corr_ref.shape
    width = out_ref.shape[1]
    blocks = length // W
    group = rows // blocks
    each = rows // sources
    half = W // 2
    lines = length // width

    pad_ref[rows : 2 * rows, :] = jnp.zeros((rows, W), BF16)
    row8 = lax.broadcasted_iota(jnp.int32, (8, length), 0)
    b = lax.broadcasted_iota(jnp.int32, (W, W), 0)
    r = lax.broadcasted_iota(jnp.int32, (W, W), 1)
    for m in range(2):
        pad_ref[0:rows, :] = kept_ref[2 + m]
        right = jnp.concatenate(
            [pad_ref[group * d : rows + group * d, :] for d in range(blocks)], axis=1
        )
        held = kept_ref[m].astype(F32).T.astype(BF16)
        corr_ref[...] = dot(held, right)
        corr_ref[:, 0:W] = jnp.where(r >= b, corr_ref[:, 0:W], 0.0)
        total = None
        for q in range(half // 8):
            upper = corr_ref[half + 8 * q : half + 8 * q + 8, :]
            upper = jnp.concatenate([upper[:, half:], jnp.zeros((8, half), F32)], axis=1)
            both = corr_ref[8 * q : 8 * q + 8, :] + upper
            if q:
                both = pltpu.roll(both, length - 8 * q, 1)
            total = both if total is None else total + both
        for bit in (1, 2, 4):
            total = jnp.where((row8 & bit) != 0, pltpu.roll(total, length - bit, 1), total)
        line = jnp.sum(total, axis=0, keepdims=True)
        for q in range(lines):
            at = m * lines + q
            out_ref[at : at + 1, :] = line[:, q * width : (q + 1) * width]

    lane = lax.broadcasted_iota(jnp.int32, (group, width), 1)
    channel = lax.broadcasted_iota(jnp.int32, (group, width), 0)
    small = [jnp.zeros((1, width), F32)] * 16

    def put(n, products):
        by_channel = jnp.sum(products.reshape(blocks, group, W), axis=0)
        col = jnp.sum(by_channel, axis=1, keepdims=True)
        mine = lane == n % units * group + channel
        small[n // units] += jnp.sum(jnp.where(mine, col, 0.0), axis=0, keepdims=True)

    for j in range(3):
        for kind in range(2):
            field = pick(fields_ref, kind, each)
            put(2 * j + kind, kept_ref[4 + kind].astype(F32) * earlier(field, j, group))
    for m in range(2):
        put(6 + m, kept_ref[2 + m].astype(F32) * kept_ref[m].astype(F32))
    out_ref[2 * lines : 2 * lines + 16, :] = jnp.concatenate(small, axis=0)


def received_field(in_ref, units, group, parts, kind, part):
    at = (kind * parts + part) * group
    return in_ref[:, at : at + group, :].reshape(units * group, W)


def partial_kernel(
    units, in_ref, held_ref, taps_ref, series_ref, cot_ref, own_ref, part_ref, product_ref, grads_ref
):
    _, block, width = series_ref.shape
    group = width // units
    parts = block // W
    cols = gate_taps(taps_ref)
    edges = in_ref[:, 3 * parts * group :, :].astype(F32)[:, :group].reshape(width, W)
    lane = lanes_of(edges)
    second = [held_ref[0, p] for p in range(parts)]
    gate = [held_ref[1, p] for p in range(parts)]
    gate[0] += jnp.where(lane < 2, cols[2] * edges, 0.0)
    gate[0] += jnp.where(lane < 1, cols[1] * turned(edges, W - 1), 0.0)
    around = turned(edges, W - 2)
    y_two = [received_field(in_ref, units, group, parts, 2, p).astype(F32) for p in range(parts)]
    d_gate = [held_ref[2, p] * y_two[p] for p in range(parts)]
    grads = [cols[0] * held for held in d_gate]
    for j in (1, 2):
        grads = [
            have + cols[j] * held for have, held in zip(grads, later_parts(d_gate, j, around))
        ]
    w_in_part = 0.0
    w_out_part = 0.0
    for p in range(parts):
        rows = pl.ds(p * W, W)
        product = (gate[p] * y_two[p]).astype(BF16)
        product_ref[p] = product
        low = grads[p].astype(BF16)
        grads_ref[p] = low
        field = [received_field(in_ref, units, group, parts, k, p) for k in range(2)] + [low]
        w_in_part += dot(jnp.concatenate(field, axis=0), series_ref[0, rows, :])
        w_out_part += dot(product, cot_ref[0, rows, :])

    small = jnp.zeros((width, width), F32)
    for j in range(3):
        moved = earlier_parts(second, j, around) if j else second
        col = sum(jnp.sum(d * held, axis=1, keepdims=True) for d, held in zip(d_gate, moved))
        small = jnp.where(lanes_of(small) == j, col, small)
    small = small.T[0:3]

    weights = jnp.concatenate([w_in_part, w_out_part], axis=0)
    targets, sent, _ = part_ref.shape
    each = weights.shape[0] // targets
    sources = in_ref.shape[0]
    lines = (own_ref.shape[0] - 16) // 2
    slots = lines // sources
    rest = sent - each - 2 * slots - 4
    spare = [jnp.zeros((rest, width), F32)] if rest else []
    for g in range(targets):
        s = g % sources
        part_ref[g] = jnp.concatenate(
            [
                weights[g * each : (g + 1) * each],
                own_ref[s * slots : (s + 1) * slots, :],
                own_ref[lines + s * slots : lines + (s + 1) * slots, :],
                own_ref[2 * lines : 2 * lines + 1, :],
                small,
            ]
            + spare,
            axis=0,
        ).astype(BF16)


def output_kernel(units, in_ref, product_ref, grads_ref, w_in_ref, w_out_ref, out_ref, d_series_ref):
    _, block, width = out_ref.shape
    group = width // units
    parts = block // W
    w_in = w_in_ref[...]
    w_out_t = w_out_ref[...].T
    for p in range(parts):
        rows = pl.ds(p * W, W)
        out_ref[0, rows, :] = dot(w_out_t, product_ref[p]).T.astype(BF16)
        field = [received_field(in_ref, units, group, parts, k, p) for k in range(2)]
        grads = jnp.concatenate(field + [grads_ref[p]], axis=0)
        d_series_ref[0, rows, :] = dot(w_in, grads).T.astype(BF16)


def sum_kernel(in_ref, out_ref):
    targets, each, _ = out_ref.shape
    total = in_ref[0, 0:each, :].astype(F32)
    for g in range(1, targets):
        total = total + in_ref[g, 0:each, :].astype(F32)
    total = total.astype(BF16)
    for g in range(targets):
        out_ref[g] = total


def small_kernel(units, each, scale, in_ref, one_ref, two_ref, taps_ref, skip_one_ref, skip_two_ref):
    targets, _, width = in_ref.shape
    filters, block = one_ref.shape
    slots = block // width
    group = width // units
    by_unit = []
    for u in range(units):
        sums = 0.0
        for g in range(u, targets, units):
            sums += in_ref[g, each:, :].astype(F32)
        by_unit.append(sums * scale)
    repeat = units // filters
    for f in range(filters):
        sums = by_unit[f * repeat]
        for u in range(f * repeat + 1, (f + 1) * repeat):
            sums = sums + by_unit[u]
        for q in range(slots):
            one_ref[f : f + 1, q * width : (q + 1) * width] = sums[q : q + 1]
            two_ref[f : f + 1, q * width : (q + 1) * width] = sums[slots + q : slots + q + 1]

    row = lax.broadcasted_iota(jnp.int32, (units, width), 0)
    lane = lax.broadcasted_iota(jnp.int32, (units, width), 1)
    held = jnp.concatenate([sums[2 * slots : 2 * slots + 1] for sums in by_unit], axis=0)
    small = 0.0
    for shift in range(units):
        moved = pltpu.roll(held, shift * group, 1) if shift else held
        moved = jnp.where(lane // group == row, moved, 0.0)
        small += pltpu.roll(moved, units - shift, 0) if shift else moved
    gate = sum(by_unit)[2 * slots + 1 : 2 * slots + 4]
    for j in range(3):
        for kind in range(2):
            n = 2 * j + kind
            taps_ref[j : j + 1, kind * width : (kind + 1) * width] = small[n : n + 1]
    taps_ref[:, 2 * width :] = gate
    skip_one_ref[...] = small[6:7]
    skip_two_ref[...] = small[7:8]


def weight_kernel(scale, in_ref, w_in_ref, w_out_ref):
    targets, each, width = in_ref.shape
    weights = jnp.concatenate([in_ref[g].astype(F32) for g in range(targets)], axis=0) * scale
    for kind in range(3):
        w_in_ref[:, kind * width : (kind + 1) * width] = weights[kind * width : (kind + 1) * width].T
    w_out_ref[...] = weights[3 * width :]


def all_to_all(blocks, axis):
    return lax.all_to_all(blocks, axis, split_axis=0, concat_axis=0, tiled=True)


def shards(series, cotangent, w_in, w_out, taps, skip_one, skip_two, filter_one, filter_two):
    count, block, width = series.shape
    filters = filter_one.shape[0]
    sources = lax.axis_size("seq")
    copies = lax.axis_size("dp")
    length = block * sources
    units = sources // count
    group = width // units
    assert count == 1 and units >= 8 and 2 * block // width <= 16 and units % filters == 0 and block % W == 0
    blocks = length // W
    rows = blocks * group
    scale = 1.0 / math.sqrt(count * copies * length)
    shape = jax.ShapeDtypeStruct

    devices = sources * copies
    packed = 3 * (block // W) * group + 16
    fields = call(
        functools.partial(project_kernel, units),
        shape((sources, packed, W), BF16),
        flops=2 * block * width * 4 * width,
        moved=8 * block * width * 4,
    )(series, cotangent, w_in, w_out, taps, filter_one, filter_two)
    fields = all_to_all(fields, "seq")
    held = call(
        gate_kernel,
        shape((3, block // W, width, W), F32),
        flops=2 * block * width * 2 * width,
        moved=4 * 4 * block * width,
    )(series, cotangent, w_in, w_out, taps)

    sent, kept = call(
        functools.partial(operator_kernel, units),
        (shape((sources, packed, W), BF16), shape((7, rows, W), BF16)),
        [
            pltpu.VMEM((3 * rows, W), BF16),
            pltpu.VMEM((2, blocks, W, W), BF16),
            pltpu.VMEM((8, length), F32),
        ],
        flops=4 * 2 * rows * length * W,
        moved=2 * W * length * 2 * 2,
    )(fields, taps, skip_one.reshape(1, width), skip_two.reshape(1, width))

    back = all_to_all(sent, "seq")

    own = call(
        functools.partial(gradient_kernel, units),
        shape((2 * (length // width) + 16, width), F32),
        [pltpu.VMEM((2 * rows, W), BF16), pltpu.VMEM((W, length), F32)],
        flops=2 * 2 * rows * length * W,
        moved=2 * length * width * 2,
    )(fields, kept)

    each = 4 * width // devices
    sent_rows = -(-(each + 2 * (block // width) + 4) // 16) * 16
    partial, product, grads = call(
        functools.partial(partial_kernel, units),
        (
            shape((devices, sent_rows, width), BF16),
            shape((block // W, width, W), BF16),
            shape((block // W, width, W), BF16),
        ),
        flops=2 * block * width * 4 * width,
        moved=2 * block * width * 6,
    )(back, held, taps, series, cotangent, own)
    partial = all_to_all(partial, ("dp", "seq"))

    output, d_series = call(
        functools.partial(output_kernel, units),
        (shape(series.shape, BF16), shape(series.shape, BF16)),
        flops=2 * block * width * 4 * width,
        moved=2 * block * width * 6,
    )(back, product, grads, w_in, w_out)

    sums = call(
        sum_kernel,
        shape((devices, each, width), BF16),
        flops=devices * each * width,
        moved=4 * devices * each * width,
    )(partial)
    sums = all_to_all(sums, ("dp", "seq"))

    grad_one, grad_two, grad_taps, grad_skip_one, grad_skip_two = call(
        functools.partial(small_kernel, units, each, scale),
        (
            shape(filter_one.shape, F32),
            shape(filter_two.shape, F32),
            shape(taps.shape, F32),
            shape((1, width), F32),
            shape((1, width), F32),
        ),
        flops=devices * sent_rows * width,
        moved=4 * devices * sent_rows * width,
    )(partial)
    grad_w_in, grad_w_out = call(
        functools.partial(weight_kernel, scale),
        (shape(w_in.shape, F32), shape(w_out.shape, F32)),
        flops=devices * each * width,
        moved=2 * devices * each * width,
    )(sums)
    return (
        output,
        d_series,
        grad_w_in,
        grad_w_out,
        grad_taps,
        grad_skip_one.reshape(width),
        grad_skip_two.reshape(width),
        grad_one,
        grad_two,
    )


def solution(mesh):
    specs = (
        P("dp", "seq", None),
        P("dp", "seq", None),
        P(),
        P(),
        P(),
        P(),
        P(),
        P(None, "seq"),
        P(None, "seq"),
    )
    return jax.shard_map(shards, mesh=mesh, in_specs=specs, out_specs=specs, check_vma=False)
```

```python
import functools
import math

import jax
import jax.numpy as jnp
from jax import lax
from jax.experimental import pallas as pl
from jax.experimental.pallas import tpu as pltpu
from jax.sharding import PartitionSpec as P

W = 256
TILE = 128
F32 = jnp.float32
BF16 = jnp.bfloat16
NT = (((1,), (1,)), ((), ()))
VMEM_LIMIT = 56 * 1024 * 1024


def call(body, out_shape, scratch=(), flops=0, moved=0):
    return pl.pallas_call(
        body,
        out_shape=out_shape,
        scratch_shapes=list(scratch),
        compiler_params=pltpu.CompilerParams(vmem_limit_bytes=VMEM_LIMIT),
        cost_estimate=pl.CostEstimate(flops=flops, bytes_accessed=moved, transcendentals=0),
    )


def dot(a, b):
    return jnp.dot(a, b, preferred_element_type=F32)


def dot_nt(a, b):
    return lax.dot_general(a, b, NT, preferred_element_type=F32)


def lanes_of(field):
    return lax.broadcasted_iota(jnp.int32, field.shape, field.ndim - 1)


def turned(field, shift):
    return pltpu.roll(field, shift, field.ndim - 1)


def tiles_of(parts):
    return [held[:, at : at + TILE] for held in parts for at in range(0, W, TILE)]


def parts_of(tiles):
    each = W // TILE
    return [jnp.concatenate(tiles[at : at + each], axis=1) for at in range(0, len(tiles), each)]


def earlier_parts(parts, j, before):
    moved = [turned(tile, j) for tile in tiles_of([before] + parts)]
    moved = moved[W // TILE - 1 :]
    edge = lanes_of(moved[0]) < j
    return parts_of([jnp.where(edge, ahead, tile) for ahead, tile in zip(moved, moved[1:])])


def later_parts(parts, j, behind):
    moved = [turned(tile, TILE - j) for tile in tiles_of(parts + [behind])]
    moved = moved[: len(moved) - W // TILE + 1]
    edge = lanes_of(moved[0]) >= TILE - j
    return parts_of([jnp.where(edge, following, tile) for tile, following in zip(moved, moved[1:])])


def gate_taps(taps_ref):
    width = taps_ref.shape[1] // 3
    rows = jnp.concatenate([taps_ref[:, 2 * width :], jnp.zeros((5, width), F32)], axis=0)
    cols = jnp.concatenate([rows] * (width // 8), axis=0).T
    return [cols[:, j : j + 1] for j in range(3)]


def gate_local(second, cols):
    zeros = jnp.zeros_like(second[0])
    total = [cols[0] * held for held in second]
    for j in (1, 2):
        moved = earlier_parts(second, j, zeros)
        total = [have + cols[j] * held for have, held in zip(total, moved)]
    return total


def project_kernel(units, series_ref, cot_ref, w_in_ref, w_out_ref, taps_ref, one_ref, two_ref, out_ref):
    _, block, width = series_ref.shape
    group = width // units
    parts = block // W
    w_in_t = w_in_ref[...].T
    w_out = w_out_ref[...]
    proj = [dot_nt(w_in_t, series_ref[0, p * W : (p + 1) * W, :]) for p in range(parts)]
    d_prod = [dot_nt(w_out, cot_ref[0, p * W : (p + 1) * W, :]) for p in range(parts)]
    second = [held[2 * width :] for held in proj]
    gate = gate_local(second, gate_taps(taps_ref))
    for p in range(parts):
        fields = [proj[p][:width], proj[p][width : 2 * width], d_prod[p] * gate[p]]
        for kind, field in enumerate(fields):
            at = (kind * parts + p) * group
            out_ref[:, at : at + group, :] = field.astype(BF16).reshape(units, group, W)

    lane = lanes_of(second[0])
    edges = jnp.where((lane >= 128) & (lane < 130), turned(second[-1], 130), 0.0)
    edges = jnp.where((lane >= 130) & (lane < 132), turned(d_prod[0], 130), edges)
    lines = [
        ref[:, q * width : (q + 1) * width]
        for ref in (one_ref, two_ref)
        for q in range(block // width)
    ]
    repeat = units // one_ref.shape[0]
    for u in range(units):
        row = u // repeat
        held = jnp.concatenate([line[row : row + 1] for line in lines], axis=0)
        held = jnp.concatenate([held, jnp.zeros((held.shape[0], W - width), F32)], axis=1)
        held = jnp.concatenate([held, jnp.zeros((16 - held.shape[0], W), F32)], axis=0)
        edge = edges[u * group : (u + 1) * group]
        if group < 16:
            edge = jnp.concatenate([edge, jnp.zeros((16 - group, W), F32)], axis=0)
        out_ref[u, 3 * parts * group :, :] = (held + edge).astype(BF16)


def gate_kernel(series_ref, cot_ref, w_in_ref, w_out_ref, taps_ref, out_ref):
    _, block, width = series_ref.shape
    parts = block // W
    w_two_t = w_in_ref[:, 2 * width :].T
    w_out = w_out_ref[...]
    second = [dot_nt(w_two_t, series_ref[0, p * W : (p + 1) * W, :]) for p in range(parts)]
    gate = gate_local(second, gate_taps(taps_ref))
    for p in range(parts):
        out_ref[0, p] = second[p]
        out_ref[1, p] = gate[p]
        out_ref[2, p] = dot_nt(w_out, cot_ref[0, p * W : (p + 1) * W, :])


def build_toeplitz(fields_ref, start, toep_ref, base_ref):
    sources = fields_ref.shape[0]
    _, blocks, _, _ = toep_ref.shape
    slots = blocks // sources * (W // TILE)
    tiles = sources * slots
    lane = lax.broadcasted_iota(jnp.int32, (tiles * 16, TILE), 1)
    row = lax.rem(lax.broadcasted_iota(jnp.int32, (tiles * 16, TILE), 0), 16)
    for m in range(2):
        for s in range(sources):
            lines = fields_ref[s, start : start + 16, :].astype(F32)
            for q in range(slots):
                line = lines[m * slots + q : m * slots + q + 1, :TILE]
                at = (s * slots + q) * 16
                base_ref[at : at + 16, :] = jnp.broadcast_to(line, (16, TILE))
        base = base_ref[...].astype(BF16)
        none = jnp.zeros((16, TILE), BF16)
        for bit in (1, 2, 4, 8):
            moved = pltpu.roll(base, bit, 1)
            ahead = jnp.concatenate([none, moved[:-16]], axis=0)
            moved = jnp.where(lane < bit, ahead, moved)
            base = jnp.where((row & bit) != 0, moved, base)
        for q in range(TILE // 16):
            moved = base
            if q:
                moved = pltpu.roll(base, 16 * q, 1)
                ahead = jnp.concatenate([none, moved[:-16]], axis=0)
                moved = jnp.where(lane < 16 * q, ahead, moved)
            moved = moved.reshape(blocks, 2, 16, TILE)
            at = 16 * q
            low = moved[:, 0]
            high = moved[:, 1]
            shifted = jnp.concatenate([jnp.zeros((1, 16, TILE), BF16), high[:-1]], axis=0)
            toep_ref[m, :, at : at + 16, 0:TILE] = low
            toep_ref[m, :, at : at + 16, TILE:] = high
            toep_ref[m, :, TILE + at : TILE + at + 16, 0:TILE] = shifted
            toep_ref[m, :, TILE + at : TILE + at + 16, TILE:] = low


def earlier(field, j, group):
    if j == 0:
        return field
    low, high = pltpu.roll(field[:, :TILE], j, 1), pltpu.roll(field[:, TILE:], j, 1)
    above = jnp.concatenate([jnp.zeros((group, TILE), F32), high[:-group]], axis=0)
    edge = lanes_of(low) < j
    return jnp.concatenate([jnp.where(edge, above, low), jnp.where(edge, low, high)], axis=1)


def later(field, j, group):
    if j == 0:
        return field
    low, high = pltpu.roll(field[:, :TILE], TILE - j, 1), pltpu.roll(field[:, TILE:], TILE - j, 1)
    below = jnp.concatenate([low[group:], jnp.zeros((group, TILE), F32)], axis=0)
    edge = lanes_of(low) >= TILE - j
    return jnp.concatenate([jnp.where(edge, high, low), jnp.where(edge, below, high)], axis=1)


def own_lanes(f, group, width):
    lane = lax.broadcasted_iota(jnp.int32, (group, width), 1)
    channel = lax.broadcasted_iota(jnp.int32, (group, width), 0)
    return lane == f * group + channel


def pick(ref, kind, received):
    rows = received
    field = ref[:, kind * rows : (kind + 1) * rows, :]
    return field.reshape(field.shape[0] * rows, W).astype(F32)


def operator_kernel(
    units,
    fields_ref,
    taps_ref,
    skip_one_ref,
    skip_two_ref,
    out_ref,
    kept_ref,
    pad_ref,
    toep_ref,
    base_ref,
):
    sources, _, _ = out_ref.shape
    _, rows, _ = kept_ref.shape
    each = rows // sources
    start = 3 * each
    build_toeplitz(fields_ref, start, toep_ref, base_ref)
    width = taps_ref.shape[1] // 3
    group = width // units
    blocks = rows // group
    u = lax.rem(lax.axis_index("seq"), units)
    mine = own_lanes(u, group, width)

    def column(values):
        col = jnp.sum(jnp.where(mine, values, 0.0), axis=1, keepdims=True)
        return jnp.broadcast_to(col, (group, W))

    def scaled(field, col):
        return (field.reshape(blocks, group, W) * col[None]).reshape(rows, W)

    zeros = jnp.zeros((rows, W), BF16)
    pad_ref[0:rows, :] = zeros
    pad_ref[2 * rows : 3 * rows, :] = zeros

    def causal(m, field):
        pad_ref[rows : 2 * rows, :] = field
        left = jnp.concatenate(
            [pad_ref[rows - group * d : 2 * rows - group * d, :] for d in range(blocks)], axis=1
        )
        return dot(left, toep_ref[m].reshape(blocks * W, W))

    def anticausal(m, field):
        pad_ref[rows : 2 * rows, :] = field
        left = jnp.concatenate(
            [pad_ref[rows + group * d : 2 * rows + group * d, :] for d in range(blocks)], axis=1
        )
        right = jnp.concatenate([toep_ref[m, d] for d in range(blocks)], axis=1)
        return dot_nt(left, right)

    tap = [
        [
            column(taps_ref[j : j + 1, kind * width : (kind + 1) * width])
            for j in range(3)
        ]
        for kind in range(3)
    ]
    skip_one = column(skip_one_ref[...])
    skip_two = column(skip_two_ref[...])

    def short(kind):
        field = pick(fields_ref, kind, each)
        total = scaled(field, tap[kind][0])
        for j in (1, 2):
            total = total + scaled(earlier(field, j, group), tap[kind][j])
        return total

    def keep(slot, field):
        low = field.astype(BF16)
        kept_ref[slot] = low
        return low

    def send(kind, field):
        out_ref[:, kind * each : (kind + 1) * each, :] = field.astype(BF16).reshape(sources, each, W)

    def send_back(kind, field):
        total = scaled(field, tap[kind][0])
        for j in (1, 2):
            total = total + scaled(later(field, j, group), tap[kind][j])
        send(kind, total)

    edges = fields_ref[:, start : start + 16, :].astype(F32)[:, :group]
    none = jnp.zeros((1, group, W), F32)
    before = jnp.concatenate([none, edges[:-1]], axis=0)
    following = jnp.concatenate([edges[1:], none], axis=0)
    lane = lanes_of(edges)
    reach = tap[2][2] * turned(before, 128)
    reach = reach + jnp.where(lane < 1, tap[2][1] * turned(before, 127), 0.0)
    reach = jnp.where(lane < 2, turned(edges, 126) * reach, 0.0)
    grad_two = pick(fields_ref, 2, each).reshape(sources, each, W)
    grad_two = jnp.concatenate([grad_two[:, :group] + reach, grad_two[:, group:]], axis=1)
    grad_two = grad_two.reshape(rows, W)

    value = short(0)
    y_one = causal(0, keep(0, value)) + scaled(value, skip_one)
    gate_one = short(1)
    mid = gate_one * y_one
    y_two = causal(1, keep(1, mid)) + scaled(mid, skip_two)
    send(2, y_two)
    heads = y_two.reshape(sources, each, W)[1:, :group]
    heads = jnp.concatenate([heads, none], axis=0)
    edges = jnp.where(lane < 4, turned(following, 128) * turned(heads, 2), 0.0)
    edges = jnp.where(lane < 2, turned(before, 128), edges)
    if group < 16:
        edges = jnp.concatenate([edges, jnp.zeros((sources, 16 - group, W), F32)], axis=1)
    out_ref[:, start:, :] = edges.astype(BF16)
    d_mid = anticausal(1, keep(3, grad_two)) + scaled(grad_two, skip_two)
    grad_one = d_mid * gate_one
    d_gate_one = d_mid * y_one
    keep(5, d_gate_one)
    send_back(1, d_gate_one)
    d_value = anticausal(0, keep(2, grad_one)) + scaled(grad_one, skip_one)
    keep(4, d_value)
    send_back(0, d_value)


def gradient_kernel(units, fields_ref, kept_ref, out_ref, pad_ref, corr_ref):
    sources, _, _ = fields_ref.shape
    _, rows, _ = kept_ref.shape
    _, length = corr_ref.shape
    width = out_ref.shape[1]
    blocks = length // W
    group = rows // blocks
    each = rows // sources
    half = W // 2
    lines = length // width

    pad_ref[rows : 2 * rows, :] = jnp.zeros((rows, W), BF16)
    row8 = lax.broadcasted_iota(jnp.int32, (8, length), 0)
    b = lax.broadcasted_iota(jnp.int32, (W, W), 0)
    r = lax.broadcasted_iota(jnp.int32, (W, W), 1)
    for m in range(2):
        pad_ref[0:rows, :] = kept_ref[2 + m]
        right = jnp.concatenate(
            [pad_ref[group * d : rows + group * d, :] for d in range(blocks)], axis=1
        )
        held = kept_ref[m].astype(F32).T.astype(BF16)
        corr_ref[...] = dot(held, right)
        corr_ref[:, 0:W] = jnp.where(r >= b, corr_ref[:, 0:W], 0.0)
        total = None
        for q in range(half // 8):
            upper = corr_ref[half + 8 * q : half + 8 * q + 8, :]
            upper = jnp.concatenate([upper[:, half:], jnp.zeros((8, half), F32)], axis=1)
            both = corr_ref[8 * q : 8 * q + 8, :] + upper
            if q:
                both = pltpu.roll(both, length - 8 * q, 1)
            total = both if total is None else total + both
        for bit in (1, 2, 4):
            total = jnp.where((row8 & bit) != 0, pltpu.roll(total, length - bit, 1), total)
        line = jnp.sum(total, axis=0, keepdims=True)
        for q in range(lines):
            at = m * lines + q
            out_ref[at : at + 1, :] = line[:, q * width : (q + 1) * width]

    lane = lax.broadcasted_iota(jnp.int32, (group, width), 1)
    channel = lax.broadcasted_iota(jnp.int32, (group, width), 0)
    small = [jnp.zeros((1, width), F32)] * 16

    def put(n, products):
        by_channel = jnp.sum(products.reshape(blocks, group, W), axis=0)
        col = jnp.sum(by_channel, axis=1, keepdims=True)
        mine = lane == n % units * group + channel
        small[n // units] += jnp.sum(jnp.where(mine, col, 0.0), axis=0, keepdims=True)

    for j in range(3):
        for kind in range(2):
            field = pick(fields_ref, kind, each)
            put(2 * j + kind, kept_ref[4 + kind].astype(F32) * earlier(field, j, group))
    for m in range(2):
        put(6 + m, kept_ref[2 + m].astype(F32) * kept_ref[m].astype(F32))
    out_ref[2 * lines : 2 * lines + 16, :] = jnp.concatenate(small, axis=0)


def received_field(in_ref, units, group, parts, kind, part):
    at = (kind * parts + part) * group
    return in_ref[:, at : at + group, :].reshape(units * group, W)


def partial_kernel(
    units, in_ref, held_ref, taps_ref, series_ref, cot_ref, own_ref, part_ref, product_ref, grads_ref
):
    _, block, width = series_ref.shape
    group = width // units
    parts = block // W
    cols = gate_taps(taps_ref)
    edges = in_ref[:, 3 * parts * group :, :].astype(F32)[:, :group].reshape(width, W)
    lane = lanes_of(edges)
    second = [held_ref[0, p] for p in range(parts)]
    gate = [held_ref[1, p] for p in range(parts)]
    gate[0] += jnp.where(lane < 2, cols[2] * edges, 0.0)
    gate[0] += jnp.where(lane < 1, cols[1] * turned(edges, W - 1), 0.0)
    around = turned(edges, W - 2)
    y_two = [received_field(in_ref, units, group, parts, 2, p).astype(F32) for p in range(parts)]
    d_gate = [held_ref[2, p] * y_two[p] for p in range(parts)]
    grads = [cols[0] * held for held in d_gate]
    for j in (1, 2):
        grads = [
            have + cols[j] * held for have, held in zip(grads, later_parts(d_gate, j, around))
        ]
    w_in_part = 0.0
    w_out_part = 0.0
    for p in range(parts):
        rows = pl.ds(p * W, W)
        product = (gate[p] * y_two[p]).astype(BF16)
        product_ref[p] = product
        low = grads[p].astype(BF16)
        grads_ref[p] = low
        field = [received_field(in_ref, units, group, parts, k, p) for k in range(2)] + [low]
        w_in_part += dot(jnp.concatenate(field, axis=0), series_ref[0, rows, :])
        w_out_part += dot(product, cot_ref[0, rows, :])

    small = jnp.zeros((width, width), F32)
    for j in range(3):
        moved = earlier_parts(second, j, around) if j else second
        col = sum(jnp.sum(d * held, axis=1, keepdims=True) for d, held in zip(d_gate, moved))
        small = jnp.where(lanes_of(small) == j, col, small)
    small = small.T[0:3]

    weights = jnp.concatenate([w_in_part, w_out_part], axis=0)
    targets, sent, _ = part_ref.shape
    each = weights.shape[0] // targets
    sources = in_ref.shape[0]
    lines = (own_ref.shape[0] - 16) // 2
    slots = lines // sources
    rest = sent - each - 2 * slots - 4
    spare = [jnp.zeros((rest, width), F32)] if rest else []
    for g in range(targets):
        s = g % sources
        part_ref[g] = jnp.concatenate(
            [
                weights[g * each : (g + 1) * each],
                own_ref[s * slots : (s + 1) * slots, :],
                own_ref[lines + s * slots : lines + (s + 1) * slots, :],
                own_ref[2 * lines : 2 * lines + 1, :],
                small,
            ]
            + spare,
            axis=0,
        ).astype(BF16)


def output_kernel(units, in_ref, product_ref, grads_ref, w_in_ref, w_out_ref, out_ref, d_series_ref):
    _, block, width = out_ref.shape
    group = width // units
    parts = block // W
    w_in = w_in_ref[...]
    w_out_t = w_out_ref[...].T
    for p in range(parts):
        rows = pl.ds(p * W, W)
        out_ref[0, rows, :] = dot(w_out_t, product_ref[p]).T.astype(BF16)
        field = [received_field(in_ref, units, group, parts, k, p) for k in range(2)]
        grads = jnp.concatenate(field + [grads_ref[p]], axis=0)
        d_series_ref[0, rows, :] = dot(w_in, grads).T.astype(BF16)


def sum_kernel(in_ref, out_ref):
    targets, each, _ = out_ref.shape
    total = in_ref[0, 0:each, :].astype(F32)
    for g in range(1, targets):
        total = total + in_ref[g, 0:each, :].astype(F32)
    total = total.astype(BF16)
    for g in range(targets):
        out_ref[g] = total


def small_kernel(units, each, scale, in_ref, one_ref, two_ref, taps_ref, skip_one_ref, skip_two_ref):
    targets, _, width = in_ref.shape
    filters, block = one_ref.shape
    slots = block // width
    group = width // units
    by_unit = []
    for u in range(units):
        sums = 0.0
        for g in range(u, targets, units):
            sums += in_ref[g, each:, :].astype(F32)
        by_unit.append(sums * scale)
    repeat = units // filters
    for f in range(filters):
        sums = by_unit[f * repeat]
        for u in range(f * repeat + 1, (f + 1) * repeat):
            sums = sums + by_unit[u]
        for q in range(slots):
            one_ref[f : f + 1, q * width : (q + 1) * width] = sums[q : q + 1]
            two_ref[f : f + 1, q * width : (q + 1) * width] = sums[slots + q : slots + q + 1]

    row = lax.broadcasted_iota(jnp.int32, (units, width), 0)
    lane = lax.broadcasted_iota(jnp.int32, (units, width), 1)
    held = jnp.concatenate([sums[2 * slots : 2 * slots + 1] for sums in by_unit], axis=0)
    small = 0.0
    for shift in range(units):
        moved = pltpu.roll(held, shift * group, 1) if shift else held
        moved = jnp.where(lane // group == row, moved, 0.0)
        small += pltpu.roll(moved, units - shift, 0) if shift else moved
    gate = sum(by_unit)[2 * slots + 1 : 2 * slots + 4]
    for j in range(3):
        for kind in range(2):
            n = 2 * j + kind
            taps_ref[j : j + 1, kind * width : (kind + 1) * width] = small[n : n + 1]
    taps_ref[:, 2 * width :] = gate
    skip_one_ref[...] = small[6:7]
    skip_two_ref[...] = small[7:8]


def weight_kernel(scale, in_ref, w_in_ref, w_out_ref):
    targets, each, width = in_ref.shape
    weights = jnp.concatenate([in_ref[g].astype(F32) for g in range(targets)], axis=0) * scale
    for kind in range(3):
        w_in_ref[:, kind * width : (kind + 1) * width] = weights[kind * width : (kind + 1) * width].T
    w_out_ref[...] = weights[3 * width :]


def all_to_all(blocks, axis):
    return lax.all_to_all(blocks, axis, split_axis=0, concat_axis=0, tiled=True)


def shards(series, cotangent, w_in, w_out, taps, skip_one, skip_two, filter_one, filter_two):
    count, block, width = series.shape
    filters = filter_one.shape[0]
    sources = lax.axis_size("seq")
    copies = lax.axis_size("dp")
    length = block * sources
    units = sources // count
    group = width // units
    assert count == 1 and units >= 8 and 2 * block // width <= 16 and units % filters == 0 and block % W == 0
    blocks = length // W
    rows = blocks * group
    scale = 1.0 / math.sqrt(count * copies * length)
    shape = jax.ShapeDtypeStruct

    devices = sources * copies
    packed = 3 * (block // W) * group + 16
    fields = call(
        functools.partial(project_kernel, units),
        shape((sources, packed, W), BF16),
        flops=2 * block * width * 4 * width,
        moved=8 * block * width * 4,
    )(series, cotangent, w_in, w_out, taps, filter_one, filter_two)
    fields = all_to_all(fields, "seq")
    held = call(
        gate_kernel,
        shape((3, block // W, width, W), F32),
        flops=2 * block * width * 2 * width,
        moved=4 * 4 * block * width,
    )(series, cotangent, w_in, w_out, taps)

    sent, kept = call(
        functools.partial(operator_kernel, units),
        (shape((sources, packed, W), BF16), shape((7, rows, W), BF16)),
        [
            pltpu.VMEM((3 * rows, W), BF16),
            pltpu.VMEM((2, blocks, W, W), BF16),
            pltpu.VMEM((length // TILE * 16, TILE), F32),
        ],
        flops=4 * 2 * rows * length * W,
        moved=2 * W * length * 2 * 2,
    )(fields, taps, skip_one.reshape(1, width), skip_two.reshape(1, width))

    back = all_to_all(sent, "seq")

    own = call(
        functools.partial(gradient_kernel, units),
        shape((2 * (length // width) + 16, width), F32),
        [pltpu.VMEM((2 * rows, W), BF16), pltpu.VMEM((W, length), F32)],
        flops=2 * 2 * rows * length * W,
        moved=2 * length * width * 2,
    )(fields, kept)

    each = 4 * width // devices
    sent_rows = -(-(each + 2 * (block // width) + 4) // 16) * 16
    partial, product, grads = call(
        functools.partial(partial_kernel, units),
        (
            shape((devices, sent_rows, width), BF16),
            shape((block // W, width, W), BF16),
            shape((block // W, width, W), BF16),
        ),
        flops=2 * block * width * 4 * width,
        moved=2 * block * width * 6,
    )(back, held, taps, series, cotangent, own)
    partial = all_to_all(partial, ("dp", "seq"))

    output, d_series = call(
        functools.partial(output_kernel, units),
        (shape(series.shape, BF16), shape(series.shape, BF16)),
        flops=2 * block * width * 4 * width,
        moved=2 * block * width * 6,
    )(back, product, grads, w_in, w_out)

    sums = call(
        sum_kernel,
        shape((devices, each, width), BF16),
        flops=devices * each * width,
        moved=4 * devices * each * width,
    )(partial)
    sums = all_to_all(sums, ("dp", "seq"))

    grad_one, grad_two, grad_taps, grad_skip_one, grad_skip_two = call(
        functools.partial(small_kernel, units, each, scale),
        (
            shape(filter_one.shape, F32),
            shape(filter_two.shape, F32),
            shape(taps.shape, F32),
            shape((1, width), F32),
            shape((1, width), F32),
        ),
        flops=devices * sent_rows * width,
        moved=4 * devices * sent_rows * width,
    )(partial)
    grad_w_in, grad_w_out = call(
        functools.partial(weight_kernel, scale),
        (shape(w_in.shape, F32), shape(w_out.shape, F32)),
        flops=devices * each * width,
        moved=2 * devices * each * width,
    )(sums)
    return (
        output,
        d_series,
        grad_w_in,
        grad_w_out,
        grad_taps,
        grad_skip_one.reshape(width),
        grad_skip_two.reshape(width),
        grad_one,
        grad_two,
    )


def solution(mesh):
    specs = (
        P("dp", "seq", None),
        P("dp", "seq", None),
        P(),
        P(),
        P(),
        P(),
        P(),
        P(None, "seq"),
        P(None, "seq"),
    )
    return jax.shard_map(shards, mesh=mesh, in_specs=specs, out_specs=specs, check_vma=False)
```

```python
import functools
import math

import jax
import jax.numpy as jnp
from jax import lax
from jax.experimental import pallas as pl
from jax.experimental.pallas import tpu as pltpu
from jax.sharding import PartitionSpec as P

W = 256
TILE = 128
F32 = jnp.float32
BF16 = jnp.bfloat16
NT = (((1,), (1,)), ((), ()))
VMEM_LIMIT = 56 * 1024 * 1024


def call(body, out_shape, scratch=(), flops=0, moved=0):
    return pl.pallas_call(
        body,
        out_shape=out_shape,
        scratch_shapes=list(scratch),
        compiler_params=pltpu.CompilerParams(vmem_limit_bytes=VMEM_LIMIT),
        cost_estimate=pl.CostEstimate(flops=flops, bytes_accessed=moved, transcendentals=0),
    )


def dot(a, b):
    return jnp.dot(a, b, preferred_element_type=F32)


def dot_nt(a, b):
    return lax.dot_general(a, b, NT, preferred_element_type=F32)


def lanes_of(field):
    return lax.broadcasted_iota(jnp.int32, field.shape, field.ndim - 1)


def turned(field, shift):
    return pltpu.roll(field, shift, field.ndim - 1)


def tiles_of(parts):
    return [held[:, at : at + TILE] for held in parts for at in range(0, W, TILE)]


def parts_of(tiles):
    each = W // TILE
    return [jnp.concatenate(tiles[at : at + each], axis=1) for at in range(0, len(tiles), each)]


def earlier_parts(parts, j, before):
    moved = [turned(tile, j) for tile in tiles_of([before] + parts)]
    moved = moved[W // TILE - 1 :]
    edge = lanes_of(moved[0]) < j
    return parts_of([jnp.where(edge, ahead, tile) for ahead, tile in zip(moved, moved[1:])])


def later_parts(parts, j, behind):
    moved = [turned(tile, TILE - j) for tile in tiles_of(parts + [behind])]
    moved = moved[: len(moved) - W // TILE + 1]
    edge = lanes_of(moved[0]) >= TILE - j
    return parts_of([jnp.where(edge, following, tile) for tile, following in zip(moved, moved[1:])])


def gate_taps(taps_ref):
    width = taps_ref.shape[1] // 3
    rows = jnp.concatenate([taps_ref[:, 2 * width :], jnp.zeros((5, width), F32)], axis=0)
    cols = jnp.concatenate([rows] * (width // 8), axis=0).T
    return [cols[:, j : j + 1] for j in range(3)]


def gate_local(second, cols):
    zeros = jnp.zeros_like(second[0])
    total = [cols[0] * held for held in second]
    for j in (1, 2):
        moved = earlier_parts(second, j, zeros)
        total = [have + cols[j] * held for have, held in zip(total, moved)]
    return total


def project_kernel(units, series_ref, cot_ref, w_in_ref, w_out_ref, taps_ref, one_ref, two_ref, out_ref):
    _, block, width = series_ref.shape
    group = width // units
    parts = block // W
    w_in_t = w_in_ref[...].T
    w_out = w_out_ref[...]
    proj = [dot_nt(w_in_t, series_ref[0, p * W : (p + 1) * W, :]) for p in range(parts)]
    d_prod = [dot_nt(w_out, cot_ref[0, p * W : (p + 1) * W, :]) for p in range(parts)]
    second = [held[2 * width :] for held in proj]
    gate = gate_local(second, gate_taps(taps_ref))
    for p in range(parts):
        fields = [proj[p][:width], proj[p][width : 2 * width], d_prod[p] * gate[p]]
        for kind, field in enumerate(fields):
            at = (kind * parts + p) * group
            out_ref[:, at : at + group, :] = field.astype(BF16).reshape(units, group, W)

    lane = lanes_of(second[0])
    edges = jnp.where((lane >= 128) & (lane < 130), turned(second[-1], 130), 0.0)
    edges = jnp.where((lane >= 130) & (lane < 132), turned(d_prod[0], 130), edges)
    lines = [
        ref[:, q * width : (q + 1) * width]
        for ref in (one_ref, two_ref)
        for q in range(block // width)
    ]
    repeat = units // one_ref.shape[0]
    for u in range(units):
        row = u // repeat
        held = jnp.concatenate([line[row : row + 1] for line in lines], axis=0)
        held = jnp.concatenate([held, jnp.zeros((held.shape[0], W - width), F32)], axis=1)
        held = jnp.concatenate([held, jnp.zeros((16 - held.shape[0], W), F32)], axis=0)
        edge = edges[u * group : (u + 1) * group]
        if group < 16:
            edge = jnp.concatenate([edge, jnp.zeros((16 - group, W), F32)], axis=0)
        out_ref[u, 3 * parts * group :, :] = (held + edge).astype(BF16)


def gate_kernel(series_ref, cot_ref, w_in_ref, w_out_ref, taps_ref, out_ref):
    _, block, width = series_ref.shape
    parts = block // W
    w_two_t = w_in_ref[:, 2 * width :].T
    w_out = w_out_ref[...]
    second = [dot_nt(w_two_t, series_ref[0, p * W : (p + 1) * W, :]) for p in range(parts)]
    gate = gate_local(second, gate_taps(taps_ref))
    for p in range(parts):
        out_ref[0, p] = second[p]
        out_ref[1, p] = gate[p]
        out_ref[2, p] = dot_nt(w_out, cot_ref[0, p * W : (p + 1) * W, :])


def build_toeplitz(fields_ref, start, toep_ref):
    sources = fields_ref.shape[0]
    _, blocks, _, _ = toep_ref.shape
    slots = blocks // sources * (W // TILE)
    lane = lax.broadcasted_iota(jnp.int32, (16, TILE), 1)
    row = lax.broadcasted_iota(jnp.int32, (16, TILE), 0)
    none = jnp.zeros((16, TILE), F32)
    for m in range(2):
        behind = {}

        def shifted(tile, shift):
            moved = pltpu.roll(tile, shift, 1) if shift else tile
            ahead, behind[shift] = behind.get(shift, none), moved
            return jnp.where(lane < shift, ahead, moved) if shift else moved

        for q in range(TILE // 16):
            at = TILE + 16 * q
            toep_ref[m, 0, at : at + 16, 0:TILE] = none.astype(BF16)
        held = {}
        for s in range(sources):
            lines = fields_ref[s, start : start + 16, :].astype(F32)
            for i in range(slots):
                d, part = divmod(s * slots + i, W // TILE)
                line = lines[m * slots + i : m * slots + i + 1, :TILE]
                tile = jnp.broadcast_to(line, (16, TILE))
                for bit in (1, 2, 4, 8):
                    moved = pltpu.roll(tile, bit, 1)
                    ahead, held[bit] = held.get(bit, none), moved
                    tile = jnp.where((row & bit) != 0, jnp.where(lane < bit, ahead, moved), tile)
                for q in range(TILE // 16):
                    low = shifted(tile, 16 * q).astype(BF16)
                    at = 16 * q
                    toep_ref[m, d, at : at + 16, part * TILE : (part + 1) * TILE] = low
                    if part == 0:
                        toep_ref[m, d, TILE + at : TILE + at + 16, TILE:] = low
                    elif d + 1 < blocks:
                        toep_ref[m, d + 1, TILE + at : TILE + at + 16, 0:TILE] = low


def earlier(field, j, group):
    if j == 0:
        return field
    low, high = pltpu.roll(field[:, :TILE], j, 1), pltpu.roll(field[:, TILE:], j, 1)
    above = jnp.concatenate([jnp.zeros((group, TILE), F32), high[:-group]], axis=0)
    edge = lanes_of(low) < j
    return jnp.concatenate([jnp.where(edge, above, low), jnp.where(edge, low, high)], axis=1)


def own_lanes(f, group, width):
    lane = lax.broadcasted_iota(jnp.int32, (group, width), 1)
    channel = lax.broadcasted_iota(jnp.int32, (group, width), 0)
    return lane == f * group + channel


def pick(ref, kind, received):
    rows = received
    field = ref[:, kind * rows : (kind + 1) * rows, :]
    return field.reshape(field.shape[0] * rows, W).astype(F32)


def operator_kernel(
    units,
    fields_ref,
    taps_ref,
    skip_one_ref,
    skip_two_ref,
    out_ref,
    kept_ref,
    pad_ref,
    back_ref,
    toep_ref,
    wide_ref,
):
    sources, _, _ = out_ref.shape
    _, rows, _ = kept_ref.shape
    each = rows // sources
    start = 3 * each
    build_toeplitz(fields_ref, start, toep_ref)
    width = taps_ref.shape[1] // 3
    group = width // units
    blocks = rows // group
    u = lax.rem(lax.axis_index("seq"), units)
    mine = own_lanes(u, group, width)
    value_ref, gate_ref, y_ref, mid_ref, grad_ref, first_ref, second_ref = [
        wide_ref.at[i] for i in range(7)
    ]

    def column(values):
        col = jnp.sum(jnp.where(mine, values, 0.0), axis=1, keepdims=True)
        return jnp.broadcast_to(col, (group, W))

    def scaled(field, col):
        return (field.reshape(-1, group, W) * col[None]).reshape(field.shape)

    tap = [
        [
            column(taps_ref[j : j + 1, kind * width : (kind + 1) * width])
            for j in range(3)
        ]
        for kind in range(3)
    ]
    skip_one = column(skip_one_ref[...])
    skip_two = column(skip_two_ref[...])
    chunks = [slice(s * each, (s + 1) * each) for s in range(sources)]

    zeros = jnp.zeros((rows, W), BF16)
    pad_ref[0:rows, :] = zeros
    back_ref[rows : 2 * rows, :] = zeros

    def causal(order, into_ref):
        left = jnp.concatenate(
            [pad_ref[rows - group * d : 2 * rows - group * d, :] for d in range(blocks)], axis=1
        )
        into_ref[...] = dot(left, toep_ref[order].reshape(blocks * W, W))

    def anticausal(order, into_ref):
        left = jnp.concatenate(
            [back_ref[group * d : rows + group * d, :] for d in range(blocks)], axis=1
        )
        right = jnp.concatenate([toep_ref[order, d] for d in range(blocks)], axis=1)
        into_ref[...] = dot_nt(left, right)

    def put(slot, s, field, into_ref=None, at=0):
        low = field.astype(BF16)
        kept_ref[slot, chunks[s], :] = low
        if into_ref is not None:
            into_ref[at + s * each : at + (s + 1) * each, :] = low

    def short(kind, s):
        held = fields_ref[s, kind * each : (kind + 1) * each, :].astype(F32)
        if s:
            last = fields_ref[s - 1, (kind + 1) * each - group : (kind + 1) * each, :].astype(F32)
        else:
            last = jnp.zeros((group, W), F32)
        total = scaled(held, tap[kind][0])
        low, high = held[:, :TILE], held[:, TILE:]
        for j in (1, 2):
            low_j, high_j = pltpu.roll(low, j, 1), pltpu.roll(high, j, 1)
            above = jnp.concatenate([pltpu.roll(last[:, TILE:], j, 1), high_j[:-group]], axis=0)
            edge = lanes_of(low) < j
            moved = [jnp.where(edge, above, low_j), jnp.where(edge, low_j, high_j)]
            total = total + scaled(jnp.concatenate(moved, axis=1), tap[kind][j])
        return total

    edges = fields_ref[:, start : start + 16, :].astype(F32)[:, :group]
    none = jnp.zeros((1, group, W), F32)
    before = jnp.concatenate([none, edges[:-1]], axis=0)
    following = jnp.concatenate([edges[1:], none], axis=0)
    lane = lanes_of(edges)
    reach = tap[2][2] * turned(before, 128)
    reach = reach + jnp.where(lane < 1, tap[2][1] * turned(before, 127), 0.0)
    reach = jnp.where(lane < 2, turned(edges, 126) * reach, 0.0)
    for s in range(sources):
        held = fields_ref[s, 2 * each : 3 * each, :].astype(F32)
        held = jnp.concatenate([held[:group] + reach[s], held[group:]], axis=0)
        grad_ref[chunks[s], :] = held
        put(3, s, held, back_ref)
        value = short(0, s)
        value_ref[chunks[s], :] = value
        put(0, s, value, pad_ref, rows)
        gate_ref[chunks[s], :] = short(1, s)

    causal(0, first_ref)
    anticausal(1, second_ref)
    for s in range(sources):
        at = chunks[s]
        y_one = first_ref[at, :] + scaled(value_ref[at, :], skip_one)
        y_ref[at, :] = y_one
        mid = gate_ref[at, :] * y_one
        mid_ref[at, :] = mid
        put(1, s, mid, pad_ref, rows)
    causal(1, first_ref)
    for s in range(sources):
        at = chunks[s]
        d_mid = second_ref[at, :] + scaled(grad_ref[at, :], skip_two)
        grad_one = d_mid * gate_ref[at, :]
        grad_ref[at, :] = grad_one
        put(2, s, grad_one, back_ref)
        d_gate = d_mid * y_ref[at, :]
        y_ref[at, :] = d_gate
        put(5, s, d_gate)
    anticausal(0, second_ref)
    heads = []
    for s in range(sources):
        at = chunks[s]
        y_two = first_ref[at, :] + scaled(mid_ref[at, :], skip_two)
        out_ref[s, 2 * each : 3 * each, :] = y_two.astype(BF16)
        heads.append(y_two[:group])
    heads = jnp.stack(heads[1:] + [none[0]])
    edges = jnp.where(lane < 4, turned(following, 128) * turned(heads, 2), 0.0)
    edges = jnp.where(lane < 2, turned(before, 128), edges)
    if group < 16:
        edges = jnp.concatenate([edges, jnp.zeros((sources, 16 - group, W), F32)], axis=1)
    out_ref[:, start:, :] = edges.astype(BF16)
    for s in range(sources):
        at = chunks[s]
        d_value = second_ref[at, :] + scaled(grad_ref[at, :], skip_one)
        value_ref[at, :] = d_value
        put(4, s, d_value)

    for s in range(sources):
        for kind, ref in ((0, value_ref), (1, y_ref)):
            held = ref[chunks[s], :]
            if s + 1 < sources:
                first = ref[(s + 1) * each : (s + 1) * each + group, :]
            else:
                first = jnp.zeros((group, W), F32)
            total = scaled(held, tap[kind][0])
            low, high = held[:, :TILE], held[:, TILE:]
            for j in (1, 2):
                low_j, high_j = pltpu.roll(low, TILE - j, 1), pltpu.roll(high, TILE - j, 1)
                below = jnp.concatenate([low_j[group:], pltpu.roll(first[:, :TILE], TILE - j, 1)], axis=0)
                edge = lanes_of(low) >= TILE - j
                moved = [jnp.where(edge, high_j, low_j), jnp.where(edge, below, high_j)]
                total = total + scaled(jnp.concatenate(moved, axis=1), tap[kind][j])
            out_ref[s, kind * each : (kind + 1) * each, :] = total.astype(BF16)


def gradient_kernel(units, fields_ref, kept_ref, out_ref, pad_ref, corr_ref):
    sources, _, _ = fields_ref.shape
    _, rows, _ = kept_ref.shape
    _, length = corr_ref.shape
    width = out_ref.shape[1]
    blocks = length // W
    group = rows // blocks
    each = rows // sources
    half = W // 2
    lines = length // width

    pad_ref[rows : 2 * rows, :] = jnp.zeros((rows, W), BF16)
    row8 = lax.broadcasted_iota(jnp.int32, (8, length), 0)
    b = lax.broadcasted_iota(jnp.int32, (W, W), 0)
    r = lax.broadcasted_iota(jnp.int32, (W, W), 1)
    for m in range(2):
        pad_ref[0:rows, :] = kept_ref[2 + m]
        right = jnp.concatenate(
            [pad_ref[group * d : rows + group * d, :] for d in range(blocks)], axis=1
        )
        held = kept_ref[m].astype(F32).T.astype(BF16)
        corr_ref[...] = dot(held, right)
        corr_ref[:, 0:W] = jnp.where(r >= b, corr_ref[:, 0:W], 0.0)
        total = None
        for q in range(half // 8):
            upper = corr_ref[half + 8 * q : half + 8 * q + 8, :]
            upper = jnp.concatenate([upper[:, half:], jnp.zeros((8, half), F32)], axis=1)
            both = corr_ref[8 * q : 8 * q + 8, :] + upper
            if q:
                both = pltpu.roll(both, length - 8 * q, 1)
            total = both if total is None else total + both
        for bit in (1, 2, 4):
            total = jnp.where((row8 & bit) != 0, pltpu.roll(total, length - bit, 1), total)
        line = jnp.sum(total, axis=0, keepdims=True)
        for q in range(lines):
            at = m * lines + q
            out_ref[at : at + 1, :] = line[:, q * width : (q + 1) * width]

    lane = lax.broadcasted_iota(jnp.int32, (group, width), 1)
    channel = lax.broadcasted_iota(jnp.int32, (group, width), 0)
    small = [jnp.zeros((1, width), F32)] * 16

    def put(n, products):
        by_channel = jnp.sum(products.reshape(blocks, group, W), axis=0)
        col = jnp.sum(by_channel, axis=1, keepdims=True)
        mine = lane == n % units * group + channel
        small[n // units] += jnp.sum(jnp.where(mine, col, 0.0), axis=0, keepdims=True)

    for j in range(3):
        for kind in range(2):
            field = pick(fields_ref, kind, each)
            put(2 * j + kind, kept_ref[4 + kind].astype(F32) * earlier(field, j, group))
    for m in range(2):
        put(6 + m, kept_ref[2 + m].astype(F32) * kept_ref[m].astype(F32))
    out_ref[2 * lines : 2 * lines + 16, :] = jnp.concatenate(small, axis=0)


def received_field(in_ref, units, group, parts, kind, part):
    at = (kind * parts + part) * group
    return in_ref[:, at : at + group, :].reshape(units * group, W)


def partial_kernel(
    units, in_ref, held_ref, taps_ref, series_ref, cot_ref, own_ref, part_ref, product_ref, grads_ref
):
    _, block, width = series_ref.shape
    group = width // units
    parts = block // W
    cols = gate_taps(taps_ref)
    edges = in_ref[:, 3 * parts * group :, :].astype(F32)[:, :group].reshape(width, W)
    lane = lanes_of(edges)
    second = [held_ref[0, p] for p in range(parts)]
    gate = [held_ref[1, p] for p in range(parts)]
    gate[0] += jnp.where(lane < 2, cols[2] * edges, 0.0)
    gate[0] += jnp.where(lane < 1, cols[1] * turned(edges, W - 1), 0.0)
    around = turned(edges, W - 2)
    y_two = [received_field(in_ref, units, group, parts, 2, p).astype(F32) for p in range(parts)]
    d_gate = [held_ref[2, p] * y_two[p] for p in range(parts)]
    grads = [cols[0] * held for held in d_gate]
    for j in (1, 2):
        grads = [
            have + cols[j] * held for have, held in zip(grads, later_parts(d_gate, j, around))
        ]
    w_in_part = 0.0
    w_out_part = 0.0
    for p in range(parts):
        rows = pl.ds(p * W, W)
        product = (gate[p] * y_two[p]).astype(BF16)
        product_ref[p] = product
        low = grads[p].astype(BF16)
        grads_ref[p] = low
        field = [received_field(in_ref, units, group, parts, k, p) for k in range(2)] + [low]
        w_in_part += dot(jnp.concatenate(field, axis=0), series_ref[0, rows, :])
        w_out_part += dot(product, cot_ref[0, rows, :])

    small = jnp.zeros((width, width), F32)
    for j in range(3):
        moved = earlier_parts(second, j, around) if j else second
        col = sum(jnp.sum(d * held, axis=1, keepdims=True) for d, held in zip(d_gate, moved))
        small = jnp.where(lanes_of(small) == j, col, small)
    small = small.T[0:3]

    weights = jnp.concatenate([w_in_part, w_out_part], axis=0)
    targets, sent, _ = part_ref.shape
    each = weights.shape[0] // targets
    sources = in_ref.shape[0]
    lines = (own_ref.shape[0] - 16) // 2
    slots = lines // sources
    spare = sent - each - 2 * slots - 4
    spare = [jnp.zeros((spare, width), F32)] if spare else []
    rests = []
    for s in range(sources):
        rows = [
            own_ref[s * slots : (s + 1) * slots, :],
            own_ref[lines + s * slots : lines + (s + 1) * slots, :],
            own_ref[2 * lines : 2 * lines + 1, :],
            small,
        ]
        rests.append(jnp.concatenate(rows + spare, axis=0))
    for g in range(targets):
        block = [weights[g * each : (g + 1) * each], rests[g % sources]]
        part_ref[g] = jnp.concatenate(block, axis=0).astype(BF16)


def output_kernel(units, in_ref, product_ref, grads_ref, w_in_ref, w_out_ref, out_ref, d_series_ref):
    _, block, width = out_ref.shape
    group = width // units
    parts = block // W
    w_in = w_in_ref[...]
    w_out_t = w_out_ref[...].T
    for p in range(parts):
        rows = pl.ds(p * W, W)
        out_ref[0, rows, :] = dot(w_out_t, product_ref[p]).T.astype(BF16)
        field = [received_field(in_ref, units, group, parts, k, p) for k in range(2)]
        grads = jnp.concatenate(field + [grads_ref[p]], axis=0)
        d_series_ref[0, rows, :] = dot(w_in, grads).T.astype(BF16)


def sum_kernel(in_ref, out_ref):
    targets, each, _ = out_ref.shape
    total = in_ref[0, 0:each, :].astype(F32)
    for g in range(1, targets):
        total = total + in_ref[g, 0:each, :].astype(F32)
    total = total.astype(BF16)
    for g in range(targets):
        out_ref[g] = total


def small_kernel(units, each, scale, in_ref, one_ref, two_ref, taps_ref, skip_one_ref, skip_two_ref):
    targets, _, width = in_ref.shape
    filters, block = one_ref.shape
    slots = block // width
    group = width // units
    by_unit = []
    for u in range(units):
        sums = 0.0
        for g in range(u, targets, units):
            sums += in_ref[g, each:, :].astype(F32)
        by_unit.append(sums * scale)
    repeat = units // filters
    for f in range(filters):
        sums = by_unit[f * repeat]
        for u in range(f * repeat + 1, (f + 1) * repeat):
            sums = sums + by_unit[u]
        for q in range(slots):
            one_ref[f : f + 1, q * width : (q + 1) * width] = sums[q : q + 1]
            two_ref[f : f + 1, q * width : (q + 1) * width] = sums[slots + q : slots + q + 1]

    row = lax.broadcasted_iota(jnp.int32, (units, width), 0)
    lane = lax.broadcasted_iota(jnp.int32, (units, width), 1)
    held = jnp.concatenate([sums[2 * slots : 2 * slots + 1] for sums in by_unit], axis=0)
    small = 0.0
    for shift in range(units):
        moved = pltpu.roll(held, shift * group, 1) if shift else held
        moved = jnp.where(lane // group == row, moved, 0.0)
        small += pltpu.roll(moved, units - shift, 0) if shift else moved
    gate = sum(by_unit)[2 * slots + 1 : 2 * slots + 4]
    for j in range(3):
        for kind in range(2):
            n = 2 * j + kind
            taps_ref[j : j + 1, kind * width : (kind + 1) * width] = small[n : n + 1]
    taps_ref[:, 2 * width :] = gate
    skip_one_ref[...] = small[6:7]
    skip_two_ref[...] = small[7:8]


def weight_kernel(scale, in_ref, w_in_ref, w_out_ref):
    targets, each, width = in_ref.shape
    weights = jnp.concatenate([in_ref[g].astype(F32) for g in range(targets)], axis=0) * scale
    for kind in range(3):
        w_in_ref[:, kind * width : (kind + 1) * width] = weights[kind * width : (kind + 1) * width].T
    w_out_ref[...] = weights[3 * width :]


def all_to_all(blocks, axis):
    return lax.all_to_all(blocks, axis, split_axis=0, concat_axis=0, tiled=True)


def shards(series, cotangent, w_in, w_out, taps, skip_one, skip_two, filter_one, filter_two):
    count, block, width = series.shape
    filters = filter_one.shape[0]
    sources = lax.axis_size("seq")
    copies = lax.axis_size("dp")
    length = block * sources
    units = sources // count
    group = width // units
    assert count == 1 and units >= 8 and 2 * block // width <= 16 and units % filters == 0 and block % W == 0
    blocks = length // W
    rows = blocks * group
    scale = 1.0 / math.sqrt(count * copies * length)
    shape = jax.ShapeDtypeStruct

    devices = sources * copies
    packed = 3 * (block // W) * group + 16
    fields = call(
        functools.partial(project_kernel, units),
        shape((sources, packed, W), BF16),
        flops=2 * block * width * 4 * width,
        moved=8 * block * width * 4,
    )(series, cotangent, w_in, w_out, taps, filter_one, filter_two)
    fields = all_to_all(fields, "seq")
    held = call(
        gate_kernel,
        shape((3, block // W, width, W), F32),
        flops=2 * block * width * 2 * width,
        moved=4 * 4 * block * width,
    )(series, cotangent, w_in, w_out, taps)

    sent, kept = call(
        functools.partial(operator_kernel, units),
        (shape((sources, packed, W), BF16), shape((7, rows, W), BF16)),
        [
            pltpu.VMEM((2 * rows, W), BF16),
            pltpu.VMEM((2 * rows, W), BF16),
            pltpu.VMEM((2, blocks, W, W), BF16),
            pltpu.VMEM((7, rows, W), F32),
        ],
        flops=4 * 2 * rows * length * W,
        moved=2 * W * length * 2 * 2,
    )(fields, taps, skip_one.reshape(1, width), skip_two.reshape(1, width))

    back = all_to_all(sent, "seq")

    own = call(
        functools.partial(gradient_kernel, units),
        shape((2 * (length // width) + 16, width), F32),
        [pltpu.VMEM((2 * rows, W), BF16), pltpu.VMEM((W, length), F32)],
        flops=2 * 2 * rows * length * W,
        moved=2 * length * width * 2,
    )(fields, kept)

    each = 4 * width // devices
    sent_rows = -(-(each + 2 * (block // width) + 4) // 16) * 16
    partial, product, grads = call(
        functools.partial(partial_kernel, units),
        (
            shape((devices, sent_rows, width), BF16),
            shape((block // W, width, W), BF16),
            shape((block // W, width, W), BF16),
        ),
        flops=2 * block * width * 4 * width,
        moved=2 * block * width * 6,
    )(back, held, taps, series, cotangent, own)
    partial = all_to_all(partial, ("dp", "seq"))

    output, d_series = call(
        functools.partial(output_kernel, units),
        (shape(series.shape, BF16), shape(series.shape, BF16)),
        flops=2 * block * width * 4 * width,
        moved=2 * block * width * 6,
    )(back, product, grads, w_in, w_out)

    sums = call(
        sum_kernel,
        shape((devices, each, width), BF16),
        flops=devices * each * width,
        moved=4 * devices * each * width,
    )(partial)
    sums = all_to_all(sums, ("dp", "seq"))

    grad_one, grad_two, grad_taps, grad_skip_one, grad_skip_two = call(
        functools.partial(small_kernel, units, each, scale),
        (
            shape(filter_one.shape, F32),
            shape(filter_two.shape, F32),
            shape(taps.shape, F32),
            shape((1, width), F32),
            shape((1, width), F32),
        ),
        flops=devices * sent_rows * width,
        moved=4 * devices * sent_rows * width,
    )(partial)
    grad_w_in, grad_w_out = call(
        functools.partial(weight_kernel, scale),
        (shape(w_in.shape, F32), shape(w_out.shape, F32)),
        flops=devices * each * width,
        moved=2 * devices * each * width,
    )(sums)
    return (
        output,
        d_series,
        grad_w_in,
        grad_w_out,
        grad_taps,
        grad_skip_one.reshape(width),
        grad_skip_two.reshape(width),
        grad_one,
        grad_two,
    )


def solution(mesh):
    specs = (
        P("dp", "seq", None),
        P("dp", "seq", None),
        P(),
        P(),
        P(),
        P(),
        P(),
        P(None, "seq"),
        P(None, "seq"),
    )
    return jax.shard_map(shards, mesh=mesh, in_specs=specs, out_specs=specs, check_vma=False)
```

```python
import functools
import math

import jax
import jax.numpy as jnp
from jax import lax
from jax.experimental import pallas as pl
from jax.experimental.pallas import tpu as pltpu
from jax.sharding import PartitionSpec as P

W = 256
TILE = 128
F32 = jnp.float32
BF16 = jnp.bfloat16
NT = (((1,), (1,)), ((), ()))
VMEM_LIMIT = 24 * 1024 * 1024


def call(body, out_shape, scratch=(), flops=0, moved=0):
    return pl.pallas_call(
        body,
        out_shape=out_shape,
        scratch_shapes=list(scratch),
        compiler_params=pltpu.CompilerParams(vmem_limit_bytes=VMEM_LIMIT),
        cost_estimate=pl.CostEstimate(flops=flops, bytes_accessed=moved, transcendentals=0),
    )


def dot(a, b):
    return jnp.dot(a, b, preferred_element_type=F32)


def dot_nt(a, b):
    return lax.dot_general(a, b, NT, preferred_element_type=F32)


def lanes_of(field):
    return lax.broadcasted_iota(jnp.int32, field.shape, field.ndim - 1)


def turned(field, shift):
    return pltpu.roll(field, shift, field.ndim - 1)


def tiles_of(parts):
    return [held[:, at : at + TILE] for held in parts for at in range(0, W, TILE)]


def parts_of(tiles):
    each = W // TILE
    return [jnp.concatenate(tiles[at : at + each], axis=1) for at in range(0, len(tiles), each)]


def earlier_parts(parts, j, before):
    moved = [turned(tile, j) for tile in tiles_of([before] + parts)]
    moved = moved[W // TILE - 1 :]
    edge = lanes_of(moved[0]) < j
    return parts_of([jnp.where(edge, ahead, tile) for ahead, tile in zip(moved, moved[1:])])


def later_parts(parts, j, behind):
    moved = [turned(tile, TILE - j) for tile in tiles_of(parts + [behind])]
    moved = moved[: len(moved) - W // TILE + 1]
    edge = lanes_of(moved[0]) >= TILE - j
    return parts_of([jnp.where(edge, following, tile) for tile, following in zip(moved, moved[1:])])


def gate_taps(taps_ref):
    width = taps_ref.shape[1] // 3
    rows = jnp.concatenate([taps_ref[:, 2 * width :], jnp.zeros((5, width), F32)], axis=0)
    cols = jnp.concatenate([rows] * (width // 8), axis=0).T
    return [cols[:, j : j + 1] for j in range(3)]


def gate_local(second, cols):
    zeros = jnp.zeros_like(second[0])
    total = [cols[0] * held for held in second]
    for j in (1, 2):
        moved = earlier_parts(second, j, zeros)
        total = [have + cols[j] * held for have, held in zip(total, moved)]
    return total


def project_kernel(units, series_ref, cot_ref, w_in_ref, w_out_ref, taps_ref, one_ref, two_ref, out_ref):
    _, block, width = series_ref.shape
    group = width // units
    parts = block // W
    w_in_t = w_in_ref[...].T
    w_out = w_out_ref[...]
    proj = [dot_nt(w_in_t, series_ref[0, p * W : (p + 1) * W, :]) for p in range(parts)]
    d_prod = [dot_nt(w_out, cot_ref[0, p * W : (p + 1) * W, :]) for p in range(parts)]
    second = [held[2 * width :] for held in proj]
    gate = gate_local(second, gate_taps(taps_ref))
    for p in range(parts):
        fields = [proj[p][:width], proj[p][width : 2 * width], d_prod[p] * gate[p]]
        for kind, field in enumerate(fields):
            at = (kind * parts + p) * group
            out_ref[:, at : at + group, :] = field.astype(BF16).reshape(units, group, W)

    lane = lanes_of(second[0])
    edges = jnp.where((lane >= 128) & (lane < 130), turned(second[-1], 130), 0.0)
    edges = jnp.where((lane >= 130) & (lane < 132), turned(d_prod[0], 130), edges)
    lines = [
        ref[:, q * width : (q + 1) * width]
        for ref in (one_ref, two_ref)
        for q in range(block // width)
    ]
    repeat = units // one_ref.shape[0]
    for u in range(units):
        row = u // repeat
        held = jnp.concatenate([line[row : row + 1] for line in lines], axis=0)
        held = jnp.concatenate([held, jnp.zeros((held.shape[0], W - width), F32)], axis=1)
        held = jnp.concatenate([held, jnp.zeros((16 - held.shape[0], W), F32)], axis=0)
        edge = edges[u * group : (u + 1) * group]
        if group < 16:
            edge = jnp.concatenate([edge, jnp.zeros((16 - group, W), F32)], axis=0)
        out_ref[u, 3 * parts * group :, :] = (held + edge).astype(BF16)


def gate_kernel(series_ref, cot_ref, w_in_ref, w_out_ref, taps_ref, out_ref):
    _, block, width = series_ref.shape
    parts = block // W
    w_two_t = w_in_ref[:, 2 * width :].T
    w_out = w_out_ref[...]
    second = [dot_nt(w_two_t, series_ref[0, p * W : (p + 1) * W, :]) for p in range(parts)]
    gate = gate_local(second, gate_taps(taps_ref))
    for p in range(parts):
        out_ref[0, p] = second[p]
        out_ref[1, p] = gate[p]
        out_ref[2, p] = dot_nt(w_out, cot_ref[0, p * W : (p + 1) * W, :])


def build_toeplitz(fields_ref, start, toep_ref):
    sources = fields_ref.shape[0]
    _, blocks, _, _ = toep_ref.shape
    slots = blocks // sources * (W // TILE)
    lane = lax.broadcasted_iota(jnp.int32, (16, TILE), 1)
    row = lax.broadcasted_iota(jnp.int32, (16, TILE), 0)
    none = jnp.zeros((16, TILE), F32)
    for m in range(2):
        behind = {}

        def shifted(tile, shift):
            moved = pltpu.roll(tile, shift, 1) if shift else tile
            ahead, behind[shift] = behind.get(shift, none), moved
            return jnp.where(lane < shift, ahead, moved) if shift else moved

        for q in range(TILE // 16):
            at = TILE + 16 * q
            toep_ref[m, 0, at : at + 16, 0:TILE] = none.astype(BF16)
        held = {}
        for s in range(sources):
            lines = fields_ref[s, start : start + 16, :].astype(F32)
            for i in range(slots):
                d, part = divmod(s * slots + i, W // TILE)
                line = lines[m * slots + i : m * slots + i + 1, :TILE]
                tile = jnp.broadcast_to(line, (16, TILE))
                for bit in (1, 2, 4, 8):
                    moved = pltpu.roll(tile, bit, 1)
                    ahead, held[bit] = held.get(bit, none), moved
                    tile = jnp.where((row & bit) != 0, jnp.where(lane < bit, ahead, moved), tile)
                for q in range(TILE // 16):
                    low = shifted(tile, 16 * q).astype(BF16)
                    at = 16 * q
                    toep_ref[m, d, at : at + 16, part * TILE : (part + 1) * TILE] = low
                    if part == 0:
                        toep_ref[m, d, TILE + at : TILE + at + 16, TILE:] = low
                    elif d + 1 < blocks:
                        toep_ref[m, d + 1, TILE + at : TILE + at + 16, 0:TILE] = low


def earlier(field, j, group):
    if j == 0:
        return field
    low, high = pltpu.roll(field[:, :TILE], j, 1), pltpu.roll(field[:, TILE:], j, 1)
    above = jnp.concatenate([jnp.zeros((group, TILE), F32), high[:-group]], axis=0)
    edge = lanes_of(low) < j
    return jnp.concatenate([jnp.where(edge, above, low), jnp.where(edge, low, high)], axis=1)


def own_lanes(f, group, width):
    lane = lax.broadcasted_iota(jnp.int32, (group, width), 1)
    channel = lax.broadcasted_iota(jnp.int32, (group, width), 0)
    return lane == f * group + channel


def pick(ref, kind, received):
    rows = received
    field = ref[:, kind * rows : (kind + 1) * rows, :]
    return field.reshape(field.shape[0] * rows, W).astype(F32)


def operator_kernel(
    units,
    fields_ref,
    taps_ref,
    skip_one_ref,
    skip_two_ref,
    out_ref,
    kept_ref,
    pad_ref,
    back_ref,
    toep_ref,
    wide_ref,
):
    sources, _, _ = out_ref.shape
    _, rows, _ = kept_ref.shape
    each = rows // sources
    start = 3 * each
    build_toeplitz(fields_ref, start, toep_ref)
    width = taps_ref.shape[1] // 3
    group = width // units
    blocks = rows // group
    u = lax.rem(lax.axis_index("seq"), units)
    mine = own_lanes(u, group, width)
    value_ref, gate_ref, y_ref, mid_ref, grad_ref, first_ref, second_ref = [
        wide_ref.at[i] for i in range(7)
    ]

    def column(values):
        col = jnp.sum(jnp.where(mine, values, 0.0), axis=1, keepdims=True)
        return jnp.broadcast_to(col, (group, W))

    def scaled(field, col):
        return (field.reshape(-1, group, W) * col[None]).reshape(field.shape)

    tap = [
        [
            column(taps_ref[j : j + 1, kind * width : (kind + 1) * width])
            for j in range(3)
        ]
        for kind in range(3)
    ]
    skip_one = column(skip_one_ref[...])
    skip_two = column(skip_two_ref[...])
    chunks = [slice(s * each, (s + 1) * each) for s in range(sources)]

    zeros = jnp.zeros((rows, W), BF16)
    pad_ref[0:rows, :] = zeros
    back_ref[rows : 2 * rows, :] = zeros

    def causal(order, into_ref):
        left = jnp.concatenate(
            [pad_ref[rows - group * d : 2 * rows - group * d, :] for d in range(blocks)], axis=1
        )
        into_ref[...] = dot(left, toep_ref[order].reshape(blocks * W, W))

    def anticausal(order, into_ref):
        left = jnp.concatenate(
            [back_ref[group * d : rows + group * d, :] for d in range(blocks)], axis=1
        )
        right = jnp.concatenate([toep_ref[order, d] for d in range(blocks)], axis=1)
        into_ref[...] = dot_nt(left, right)

    def put(slot, s, field, into_ref=None, at=0):
        low = field.astype(BF16)
        kept_ref[slot, chunks[s], :] = low
        if into_ref is not None:
            into_ref[at + s * each : at + (s + 1) * each, :] = low

    def short(kind, s):
        held = fields_ref[s, kind * each : (kind + 1) * each, :].astype(F32)
        if s:
            last = fields_ref[s - 1, (kind + 1) * each - group : (kind + 1) * each, :].astype(F32)
        else:
            last = jnp.zeros((group, W), F32)
        total = scaled(held, tap[kind][0])
        low, high = held[:, :TILE], held[:, TILE:]
        for j in (1, 2):
            low_j, high_j = pltpu.roll(low, j, 1), pltpu.roll(high, j, 1)
            above = jnp.concatenate([pltpu.roll(last[:, TILE:], j, 1), high_j[:-group]], axis=0)
            edge = lanes_of(low) < j
            moved = [jnp.where(edge, above, low_j), jnp.where(edge, low_j, high_j)]
            total = total + scaled(jnp.concatenate(moved, axis=1), tap[kind][j])
        return total

    edges = fields_ref[:, start : start + 16, :].astype(F32)[:, :group]
    none = jnp.zeros((1, group, W), F32)
    before = jnp.concatenate([none, edges[:-1]], axis=0)
    following = jnp.concatenate([edges[1:], none], axis=0)
    lane = lanes_of(edges)
    reach = tap[2][2] * turned(before, 128)
    reach = reach + jnp.where(lane < 1, tap[2][1] * turned(before, 127), 0.0)
    reach = jnp.where(lane < 2, turned(edges, 126) * reach, 0.0)
    for s in range(sources):
        held = fields_ref[s, 2 * each : 3 * each, :].astype(F32)
        held = jnp.concatenate([held[:group] + reach[s], held[group:]], axis=0)
        grad_ref[chunks[s], :] = held
        put(3, s, held, back_ref)
        value = short(0, s)
        value_ref[chunks[s], :] = value
        put(0, s, value, pad_ref, rows)
        gate_ref[chunks[s], :] = short(1, s)

    causal(0, first_ref)
    anticausal(1, second_ref)
    for s in range(sources):
        at = chunks[s]
        y_one = first_ref[at, :] + scaled(value_ref[at, :], skip_one)
        y_ref[at, :] = y_one
        mid = gate_ref[at, :] * y_one
        mid_ref[at, :] = mid
        put(1, s, mid, pad_ref, rows)
    causal(1, first_ref)
    for s in range(sources):
        at = chunks[s]
        d_mid = second_ref[at, :] + scaled(grad_ref[at, :], skip_two)
        grad_one = d_mid * gate_ref[at, :]
        grad_ref[at, :] = grad_one
        put(2, s, grad_one, back_ref)
        d_gate = d_mid * y_ref[at, :]
        y_ref[at, :] = d_gate
        put(5, s, d_gate)
    anticausal(0, second_ref)
    heads = []
    for s in range(sources):
        at = chunks[s]
        y_two = first_ref[at, :] + scaled(mid_ref[at, :], skip_two)
        out_ref[s, 2 * each : 3 * each, :] = y_two.astype(BF16)
        heads.append(y_two[:group])
    heads = jnp.stack(heads[1:] + [none[0]])
    edges = jnp.where(lane < 4, turned(following, 128) * turned(heads, 2), 0.0)
    edges = jnp.where(lane < 2, turned(before, 128), edges)
    if group < 16:
        edges = jnp.concatenate([edges, jnp.zeros((sources, 16 - group, W), F32)], axis=1)
    out_ref[:, start:, :] = edges.astype(BF16)
    for s in range(sources):
        at = chunks[s]
        d_value = second_ref[at, :] + scaled(grad_ref[at, :], skip_one)
        value_ref[at, :] = d_value
        put(4, s, d_value)

    for s in range(sources):
        for kind, ref in ((0, value_ref), (1, y_ref)):
            held = ref[chunks[s], :]
            if s + 1 < sources:
                first = ref[(s + 1) * each : (s + 1) * each + group, :]
            else:
                first = jnp.zeros((group, W), F32)
            total = scaled(held, tap[kind][0])
            low, high = held[:, :TILE], held[:, TILE:]
            for j in (1, 2):
                low_j, high_j = pltpu.roll(low, TILE - j, 1), pltpu.roll(high, TILE - j, 1)
                below = jnp.concatenate([low_j[group:], pltpu.roll(first[:, :TILE], TILE - j, 1)], axis=0)
                edge = lanes_of(low) >= TILE - j
                moved = [jnp.where(edge, high_j, low_j), jnp.where(edge, below, high_j)]
                total = total + scaled(jnp.concatenate(moved, axis=1), tap[kind][j])
            out_ref[s, kind * each : (kind + 1) * each, :] = total.astype(BF16)


def gradient_kernel(units, fields_ref, kept_ref, out_ref, pad_ref, corr_ref):
    sources, _, _ = fields_ref.shape
    _, rows, _ = kept_ref.shape
    _, length = corr_ref.shape
    width = out_ref.shape[1]
    blocks = length // W
    group = rows // blocks
    each = rows // sources
    half = W // 2
    lines = length // width

    pad_ref[rows : 2 * rows, :] = jnp.zeros((rows, W), BF16)
    row8 = lax.broadcasted_iota(jnp.int32, (8, length), 0)
    b = lax.broadcasted_iota(jnp.int32, (W, W), 0)
    r = lax.broadcasted_iota(jnp.int32, (W, W), 1)
    for m in range(2):
        pad_ref[0:rows, :] = kept_ref[2 + m]
        right = jnp.concatenate(
            [pad_ref[group * d : rows + group * d, :] for d in range(blocks)], axis=1
        )
        held = kept_ref[m].astype(F32).T.astype(BF16)
        corr_ref[...] = dot(held, right)
        corr_ref[:, 0:W] = jnp.where(r >= b, corr_ref[:, 0:W], 0.0)
        total = None
        for q in range(half // 8):
            upper = corr_ref[half + 8 * q : half + 8 * q + 8, :]
            upper = jnp.concatenate([upper[:, half:], jnp.zeros((8, half), F32)], axis=1)
            both = corr_ref[8 * q : 8 * q + 8, :] + upper
            if q:
                both = pltpu.roll(both, length - 8 * q, 1)
            total = both if total is None else total + both
        for bit in (1, 2, 4):
            total = jnp.where((row8 & bit) != 0, pltpu.roll(total, length - bit, 1), total)
        line = jnp.sum(total, axis=0, keepdims=True)
        for q in range(lines):
            at = m * lines + q
            out_ref[at : at + 1, :] = line[:, q * width : (q + 1) * width]

    lane = lax.broadcasted_iota(jnp.int32, (group, width), 1)
    channel = lax.broadcasted_iota(jnp.int32, (group, width), 0)
    small = [jnp.zeros((1, width), F32)] * 16

    def put(n, products):
        by_channel = jnp.sum(products.reshape(blocks, group, W), axis=0)
        col = jnp.sum(by_channel, axis=1, keepdims=True)
        mine = lane == n % units * group + channel
        small[n // units] += jnp.sum(jnp.where(mine, col, 0.0), axis=0, keepdims=True)

    for j in range(3):
        for kind in range(2):
            field = pick(fields_ref, kind, each)
            put(2 * j + kind, kept_ref[4 + kind].astype(F32) * earlier(field, j, group))
    for m in range(2):
        put(6 + m, kept_ref[2 + m].astype(F32) * kept_ref[m].astype(F32))
    out_ref[2 * lines : 2 * lines + 16, :] = jnp.concatenate(small, axis=0)


def received_field(in_ref, units, group, parts, kind, part):
    at = (kind * parts + part) * group
    return in_ref[:, at : at + group, :].reshape(units * group, W)


def partial_kernel(
    units, in_ref, held_ref, taps_ref, series_ref, cot_ref, own_ref, part_ref, product_ref, grads_ref
):
    _, block, width = series_ref.shape
    group = width // units
    parts = block // W
    cols = gate_taps(taps_ref)
    edges = in_ref[:, 3 * parts * group :, :].astype(F32)[:, :group].reshape(width, W)
    lane = lanes_of(edges)
    second = [held_ref[0, p] for p in range(parts)]
    gate = [held_ref[1, p] for p in range(parts)]
    gate[0] += jnp.where(lane < 2, cols[2] * edges, 0.0)
    gate[0] += jnp.where(lane < 1, cols[1] * turned(edges, W - 1), 0.0)
    around = turned(edges, W - 2)
    y_two = [received_field(in_ref, units, group, parts, 2, p).astype(F32) for p in range(parts)]
    d_gate = [held_ref[2, p] * y_two[p] for p in range(parts)]
    grads = [cols[0] * held for held in d_gate]
    for j in (1, 2):
        grads = [
            have + cols[j] * held for have, held in zip(grads, later_parts(d_gate, j, around))
        ]
    w_in_part = 0.0
    w_out_part = 0.0
    for p in range(parts):
        rows = pl.ds(p * W, W)
        product = (gate[p] * y_two[p]).astype(BF16)
        product_ref[p] = product
        low = grads[p].astype(BF16)
        grads_ref[p] = low
        field = [received_field(in_ref, units, group, parts, k, p) for k in range(2)] + [low]
        w_in_part += dot(jnp.concatenate(field, axis=0), series_ref[0, rows, :])
        w_out_part += dot(product, cot_ref[0, rows, :])

    small = jnp.zeros((width, width), F32)
    for j in range(3):
        moved = earlier_parts(second, j, around) if j else second
        col = sum(jnp.sum(d * held, axis=1, keepdims=True) for d, held in zip(d_gate, moved))
        small = jnp.where(lanes_of(small) == j, col, small)
    small = small.T[0:3]

    weights = jnp.concatenate([w_in_part, w_out_part], axis=0)
    targets, sent, _ = part_ref.shape
    each = weights.shape[0] // targets
    sources = in_ref.shape[0]
    lines = (own_ref.shape[0] - 16) // 2
    slots = lines // sources
    spare = sent - each - 2 * slots - 4
    spare = [jnp.zeros((spare, width), F32)] if spare else []
    rests = []
    for s in range(sources):
        rows = [
            own_ref[s * slots : (s + 1) * slots, :],
            own_ref[lines + s * slots : lines + (s + 1) * slots, :],
            own_ref[2 * lines : 2 * lines + 1, :],
            small,
        ]
        rests.append(jnp.concatenate(rows + spare, axis=0))
    for g in range(targets):
        block = [weights[g * each : (g + 1) * each], rests[g % sources]]
        part_ref[g] = jnp.concatenate(block, axis=0).astype(BF16)


def output_kernel(units, in_ref, product_ref, grads_ref, w_in_ref, w_out_ref, out_ref, d_series_ref):
    _, block, width = out_ref.shape
    group = width // units
    parts = block // W
    w_in = w_in_ref[...]
    w_out_t = w_out_ref[...].T
    for p in range(parts):
        rows = pl.ds(p * W, W)
        out_ref[0, rows, :] = dot(w_out_t, product_ref[p]).T.astype(BF16)
        field = [received_field(in_ref, units, group, parts, k, p) for k in range(2)]
        grads = jnp.concatenate(field + [grads_ref[p]], axis=0)
        d_series_ref[0, rows, :] = dot(w_in, grads).T.astype(BF16)


def sum_kernel(in_ref, out_ref):
    targets, each, _ = out_ref.shape
    total = in_ref[0, 0:each, :].astype(F32)
    for g in range(1, targets):
        total = total + in_ref[g, 0:each, :].astype(F32)
    total = total.astype(BF16)
    for g in range(targets):
        out_ref[g] = total


def small_kernel(units, each, scale, in_ref, one_ref, two_ref, taps_ref, skip_one_ref, skip_two_ref):
    targets, _, width = in_ref.shape
    filters, block = one_ref.shape
    slots = block // width
    group = width // units
    by_unit = []
    for u in range(units):
        sums = 0.0
        for g in range(u, targets, units):
            sums += in_ref[g, each:, :].astype(F32)
        by_unit.append(sums * scale)
    repeat = units // filters
    for f in range(filters):
        sums = by_unit[f * repeat]
        for u in range(f * repeat + 1, (f + 1) * repeat):
            sums = sums + by_unit[u]
        for q in range(slots):
            one_ref[f : f + 1, q * width : (q + 1) * width] = sums[q : q + 1]
            two_ref[f : f + 1, q * width : (q + 1) * width] = sums[slots + q : slots + q + 1]

    row = lax.broadcasted_iota(jnp.int32, (units, width), 0)
    lane = lax.broadcasted_iota(jnp.int32, (units, width), 1)
    held = jnp.concatenate([sums[2 * slots : 2 * slots + 1] for sums in by_unit], axis=0)
    small = 0.0
    for shift in range(units):
        moved = pltpu.roll(held, shift * group, 1) if shift else held
        moved = jnp.where(lane // group == row, moved, 0.0)
        small += pltpu.roll(moved, units - shift, 0) if shift else moved
    gate = sum(by_unit)[2 * slots + 1 : 2 * slots + 4]
    for j in range(3):
        for kind in range(2):
            n = 2 * j + kind
            taps_ref[j : j + 1, kind * width : (kind + 1) * width] = small[n : n + 1]
    taps_ref[:, 2 * width :] = gate
    skip_one_ref[...] = small[6:7]
    skip_two_ref[...] = small[7:8]


def weight_kernel(scale, in_ref, w_in_ref, w_out_ref):
    targets, each, width = in_ref.shape
    weights = jnp.concatenate([in_ref[g].astype(F32) for g in range(targets)], axis=0) * scale
    for kind in range(3):
        w_in_ref[:, kind * width : (kind + 1) * width] = weights[kind * width : (kind + 1) * width].T
    w_out_ref[...] = weights[3 * width :]


def all_to_all(blocks, axis):
    return lax.all_to_all(blocks, axis, split_axis=0, concat_axis=0, tiled=True)


def shards(series, cotangent, w_in, w_out, taps, skip_one, skip_two, filter_one, filter_two):
    count, block, width = series.shape
    filters = filter_one.shape[0]
    sources = lax.axis_size("seq")
    copies = lax.axis_size("dp")
    length = block * sources
    units = sources // count
    group = width // units
    assert count == 1 and units >= 8 and 2 * block // width <= 16 and units % filters == 0 and block % W == 0
    blocks = length // W
    rows = blocks * group
    scale = 1.0 / math.sqrt(count * copies * length)
    shape = jax.ShapeDtypeStruct

    devices = sources * copies
    packed = 3 * (block // W) * group + 16
    fields = call(
        functools.partial(project_kernel, units),
        shape((sources, packed, W), BF16),
        flops=2 * block * width * 4 * width,
        moved=8 * block * width * 4,
    )(series, cotangent, w_in, w_out, taps, filter_one, filter_two)
    fields = all_to_all(fields, "seq")
    held = call(
        gate_kernel,
        shape((3, block // W, width, W), F32),
        flops=2 * block * width * 2 * width,
        moved=4 * 4 * block * width,
    )(series, cotangent, w_in, w_out, taps)

    sent, kept = call(
        functools.partial(operator_kernel, units),
        (shape((sources, packed, W), BF16), shape((7, rows, W), BF16)),
        [
            pltpu.VMEM((2 * rows, W), BF16),
            pltpu.VMEM((2 * rows, W), BF16),
            pltpu.VMEM((2, blocks, W, W), BF16),
            pltpu.VMEM((7, rows, W), F32),
        ],
        flops=4 * 2 * rows * length * W,
        moved=2 * W * length * 2 * 2,
    )(fields, taps, skip_one.reshape(1, width), skip_two.reshape(1, width))

    back = all_to_all(sent, "seq")

    own = call(
        functools.partial(gradient_kernel, units),
        shape((2 * (length // width) + 16, width), F32),
        [pltpu.VMEM((2 * rows, W), BF16), pltpu.VMEM((W, length), F32)],
        flops=2 * 2 * rows * length * W,
        moved=2 * length * width * 2,
    )(fields, kept)

    each = 4 * width // devices
    sent_rows = -(-(each + 2 * (block // width) + 4) // 16) * 16
    partial, product, grads = call(
        functools.partial(partial_kernel, units),
        (
            shape((devices, sent_rows, width), BF16),
            shape((block // W, width, W), BF16),
            shape((block // W, width, W), BF16),
        ),
        flops=2 * block * width * 4 * width,
        moved=2 * block * width * 6,
    )(back, held, taps, series, cotangent, own)
    partial = all_to_all(partial, ("dp", "seq"))

    output, d_series = call(
        functools.partial(output_kernel, units),
        (shape(series.shape, BF16), shape(series.shape, BF16)),
        flops=2 * block * width * 4 * width,
        moved=2 * block * width * 6,
    )(back, product, grads, w_in, w_out)

    sums = call(
        sum_kernel,
        shape((devices, each, width), BF16),
        flops=devices * each * width,
        moved=4 * devices * each * width,
    )(partial)
    sums = all_to_all(sums, ("dp", "seq"))

    grad_one, grad_two, grad_taps, grad_skip_one, grad_skip_two = call(
        functools.partial(small_kernel, units, each, scale),
        (
            shape(filter_one.shape, F32),
            shape(filter_two.shape, F32),
            shape(taps.shape, F32),
            shape((1, width), F32),
            shape((1, width), F32),
        ),
        flops=devices * sent_rows * width,
        moved=4 * devices * sent_rows * width,
    )(partial)
    grad_w_in, grad_w_out = call(
        functools.partial(weight_kernel, scale),
        (shape(w_in.shape, F32), shape(w_out.shape, F32)),
        flops=devices * each * width,
        moved=2 * devices * each * width,
    )(sums)
    return (
        output,
        d_series,
        grad_w_in,
        grad_w_out,
        grad_taps,
        grad_skip_one.reshape(width),
        grad_skip_two.reshape(width),
        grad_one,
        grad_two,
    )


def solution(mesh):
    specs = (
        P("dp", "seq", None),
        P("dp", "seq", None),
        P(),
        P(),
        P(),
        P(),
        P(),
        P(None, "seq"),
        P(None, "seq"),
    )
    return jax.shard_map(shards, mesh=mesh, in_specs=specs, out_specs=specs, check_vma=False)
```

```python
import functools
import math

import jax
import jax.numpy as jnp
from jax import lax
from jax.experimental import pallas as pl
from jax.experimental.pallas import tpu as pltpu
from jax.sharding import PartitionSpec as P

W = 256
TILE = 128
F32 = jnp.float32
BF16 = jnp.bfloat16
NT = (((1,), (1,)), ((), ()))
VMEM_LIMIT = 24 * 1024 * 1024
VMEM_ALL = 56 * 1024 * 1024


def call(body, out_shape, scratch=(), flops=0, moved=0, limit=VMEM_LIMIT):
    return pl.pallas_call(
        body,
        out_shape=out_shape,
        scratch_shapes=list(scratch),
        compiler_params=pltpu.CompilerParams(vmem_limit_bytes=limit),
        cost_estimate=pl.CostEstimate(flops=flops, bytes_accessed=moved, transcendentals=0),
    )


def dot(a, b):
    return jnp.dot(a, b, preferred_element_type=F32)


def dot_nt(a, b):
    return lax.dot_general(a, b, NT, preferred_element_type=F32)


def lanes_of(field):
    return lax.broadcasted_iota(jnp.int32, field.shape, field.ndim - 1)


def turned(field, shift):
    return pltpu.roll(field, shift, field.ndim - 1)


def tiles_of(parts):
    return [held[:, at : at + TILE] for held in parts for at in range(0, W, TILE)]


def parts_of(tiles):
    each = W // TILE
    return [jnp.concatenate(tiles[at : at + each], axis=1) for at in range(0, len(tiles), each)]


def earlier_parts(parts, j, before):
    moved = [turned(tile, j) for tile in tiles_of([before] + parts)]
    moved = moved[W // TILE - 1 :]
    edge = lanes_of(moved[0]) < j
    return parts_of([jnp.where(edge, ahead, tile) for ahead, tile in zip(moved, moved[1:])])


def later_parts(parts, j, behind):
    moved = [turned(tile, TILE - j) for tile in tiles_of(parts + [behind])]
    moved = moved[: len(moved) - W // TILE + 1]
    edge = lanes_of(moved[0]) >= TILE - j
    return parts_of([jnp.where(edge, following, tile) for tile, following in zip(moved, moved[1:])])


def gate_taps(taps_ref):
    width = taps_ref.shape[1] // 3
    rows = jnp.concatenate([taps_ref[0:3, 2 * width :], jnp.zeros((5, width), F32)], axis=0)
    cols = jnp.concatenate([rows] * (width // 8), axis=0).T
    return [cols[:, j : j + 1] for j in range(3)]


def gate_local(second, cols):
    zeros = jnp.zeros_like(second[0])
    total = [cols[0] * held for held in second]
    for j in (1, 2):
        moved = earlier_parts(second, j, zeros)
        total = [have + cols[j] * held for have, held in zip(total, moved)]
    return total


def project_kernel(
    units,
    series_ref,
    cot_ref,
    w_in_ref,
    w_out_ref,
    taps_ref,
    skip_one_ref,
    skip_two_ref,
    one_ref,
    two_ref,
    out_ref,
    params_ref,
):
    _, block, width = series_ref.shape
    group = width // units
    parts = block // W
    params_ref[...] = jnp.zeros(params_ref.shape, F32)
    params_ref[0:3, :] = taps_ref[...]
    params_ref[3:4, 0:width] = skip_one_ref[...]
    params_ref[4:5, 0:width] = skip_two_ref[...]
    w_in_t = w_in_ref[...].T
    w_out = w_out_ref[...]
    proj = [dot_nt(w_in_t, series_ref[0, p * W : (p + 1) * W, :]) for p in range(parts)]
    d_prod = [dot_nt(w_out, cot_ref[0, p * W : (p + 1) * W, :]) for p in range(parts)]
    second = [held[2 * width :] for held in proj]
    gate = gate_local(second, gate_taps(taps_ref))
    for p in range(parts):
        fields = [proj[p][:width], proj[p][width : 2 * width], d_prod[p] * gate[p]]
        for kind, field in enumerate(fields):
            at = (kind * parts + p) * group
            out_ref[:, at : at + group, :] = field.astype(BF16).reshape(units, group, W)

    lane = lanes_of(second[0])
    edges = jnp.where((lane >= 128) & (lane < 130), turned(second[-1], 130), 0.0)
    edges = jnp.where((lane >= 130) & (lane < 132), turned(d_prod[0], 130), edges)
    lines = [
        ref[:, q * width : (q + 1) * width]
        for ref in (one_ref, two_ref)
        for q in range(block // width)
    ]
    repeat = units // one_ref.shape[0]
    for u in range(units):
        row = u // repeat
        held = jnp.concatenate([line[row : row + 1] for line in lines], axis=0)
        held = jnp.concatenate([held, jnp.zeros((held.shape[0], W - width), F32)], axis=1)
        held = jnp.concatenate([held, jnp.zeros((16 - held.shape[0], W), F32)], axis=0)
        edge = edges[u * group : (u + 1) * group]
        if group < 16:
            edge = jnp.concatenate([edge, jnp.zeros((16 - group, W), F32)], axis=0)
        out_ref[u, 3 * parts * group :, :] = (held + edge).astype(BF16)


def gate_kernel(series_ref, cot_ref, w_in_ref, w_out_ref, taps_ref, out_ref):
    _, block, width = series_ref.shape
    parts = block // W
    w_two_t = w_in_ref[:, 2 * width :].T
    w_out = w_out_ref[...]
    second = [dot_nt(w_two_t, series_ref[0, p * W : (p + 1) * W, :]) for p in range(parts)]
    gate = gate_local(second, gate_taps(taps_ref))
    for p in range(parts):
        out_ref[0, p] = second[p]
        out_ref[1, p] = gate[p]
        out_ref[2, p] = dot_nt(w_out, cot_ref[0, p * W : (p + 1) * W, :])


def build_toeplitz(fields_ref, start, toep_ref):
    sources = fields_ref.shape[0]
    _, blocks, _, _ = toep_ref.shape
    slots = blocks // sources * (W // TILE)
    lane = lax.broadcasted_iota(jnp.int32, (16, TILE), 1)
    row = lax.broadcasted_iota(jnp.int32, (16, TILE), 0)
    none = jnp.zeros((16, TILE), F32)
    for m in range(2):
        behind = {}

        def shifted(tile, shift):
            moved = pltpu.roll(tile, shift, 1) if shift else tile
            ahead, behind[shift] = behind.get(shift, none), moved
            return jnp.where(lane < shift, ahead, moved) if shift else moved

        for q in range(TILE // 16):
            at = TILE + 16 * q
            toep_ref[m, 0, at : at + 16, 0:TILE] = none.astype(BF16)
        held = {}
        for s in range(sources):
            lines = fields_ref[s, start : start + 16, :].astype(F32)
            for i in range(slots):
                d, part = divmod(s * slots + i, W // TILE)
                line = lines[m * slots + i : m * slots + i + 1, :TILE]
                tile = jnp.broadcast_to(line, (16, TILE))
                for bit in (1, 2, 4, 8):
                    moved = pltpu.roll(tile, bit, 1)
                    ahead, held[bit] = held.get(bit, none), moved
                    tile = jnp.where((row & bit) != 0, jnp.where(lane < bit, ahead, moved), tile)
                for q in range(TILE // 16):
                    low = shifted(tile, 16 * q).astype(BF16)
                    at = 16 * q
                    toep_ref[m, d, at : at + 16, part * TILE : (part + 1) * TILE] = low
                    if part == 0:
                        toep_ref[m, d, TILE + at : TILE + at + 16, TILE:] = low
                    elif d + 1 < blocks:
                        toep_ref[m, d + 1, TILE + at : TILE + at + 16, 0:TILE] = low


def earlier(field, j, group):
    if j == 0:
        return field
    low, high = pltpu.roll(field[:, :TILE], j, 1), pltpu.roll(field[:, TILE:], j, 1)
    above = jnp.concatenate([jnp.zeros((group, TILE), F32), high[:-group]], axis=0)
    edge = lanes_of(low) < j
    return jnp.concatenate([jnp.where(edge, above, low), jnp.where(edge, low, high)], axis=1)


def own_lanes(f, group, width):
    lane = lax.broadcasted_iota(jnp.int32, (group, width), 1)
    channel = lax.broadcasted_iota(jnp.int32, (group, width), 0)
    return lane == f * group + channel


def pick(ref, kind, received):
    rows = received
    field = ref[:, kind * rows : (kind + 1) * rows, :]
    return field.reshape(field.shape[0] * rows, W).astype(F32)


def operator_kernel(
    units,
    fields_ref,
    taps_ref,
    out_ref,
    kept_ref,
    pad_ref,
    back_ref,
    toep_ref,
    wide_ref,
):
    sources, _, _ = out_ref.shape
    _, rows, _ = kept_ref.shape
    each = rows // sources
    start = 3 * each
    build_toeplitz(fields_ref, start, toep_ref)
    width = taps_ref.shape[1] // 3
    group = width // units
    blocks = rows // group
    u = lax.rem(lax.axis_index("seq"), units)
    mine = own_lanes(u, group, width)
    value_ref, gate_ref, y_ref, mid_ref, grad_ref, first_ref, second_ref = [
        wide_ref.at[i] for i in range(7)
    ]

    def column(values):
        col = jnp.sum(jnp.where(mine, values, 0.0), axis=1, keepdims=True)
        return jnp.broadcast_to(col, (group, W))

    def scaled(field, col):
        return (field.reshape(-1, group, W) * col[None]).reshape(field.shape)

    tap = [
        [
            column(taps_ref[j : j + 1, kind * width : (kind + 1) * width])
            for j in range(3)
        ]
        for kind in range(3)
    ]
    skip_one = column(taps_ref[3:4, 0:width])
    skip_two = column(taps_ref[4:5, 0:width])
    chunks = [slice(s * each, (s + 1) * each) for s in range(sources)]

    zeros = jnp.zeros((rows, W), BF16)
    pad_ref[0:rows, :] = zeros
    back_ref[rows : 2 * rows, :] = zeros

    def causal(order, into_ref):
        left = jnp.concatenate(
            [pad_ref[rows - group * d : 2 * rows - group * d, :] for d in range(blocks)], axis=1
        )
        into_ref[...] = dot(left, toep_ref[order].reshape(blocks * W, W))

    def anticausal(order, into_ref):
        left = jnp.concatenate(
            [back_ref[group * d : rows + group * d, :] for d in range(blocks)], axis=1
        )
        right = jnp.concatenate([toep_ref[order, d] for d in range(blocks)], axis=1)
        into_ref[...] = dot_nt(left, right)

    def put(slot, s, field, into_ref=None, at=0):
        low = field.astype(BF16)
        kept_ref[slot, chunks[s], :] = low
        if into_ref is not None:
            into_ref[at + s * each : at + (s + 1) * each, :] = low

    def short(kind, s):
        held = fields_ref[s, kind * each : (kind + 1) * each, :].astype(F32)
        if s:
            last = fields_ref[s - 1, (kind + 1) * each - group : (kind + 1) * each, :].astype(F32)
        else:
            last = jnp.zeros((group, W), F32)
        total = scaled(held, tap[kind][0])
        low, high = held[:, :TILE], held[:, TILE:]
        for j in (1, 2):
            low_j, high_j = pltpu.roll(low, j, 1), pltpu.roll(high, j, 1)
            above = jnp.concatenate([pltpu.roll(last[:, TILE:], j, 1), high_j[:-group]], axis=0)
            edge = lanes_of(low) < j
            moved = [jnp.where(edge, above, low_j), jnp.where(edge, low_j, high_j)]
            total = total + scaled(jnp.concatenate(moved, axis=1), tap[kind][j])
        return total

    edges = fields_ref[:, start : start + 16, :].astype(F32)[:, :group]
    none = jnp.zeros((1, group, W), F32)
    before = jnp.concatenate([none, edges[:-1]], axis=0)
    following = jnp.concatenate([edges[1:], none], axis=0)
    lane = lanes_of(edges)
    reach = tap[2][2] * turned(before, 128)
    reach = reach + jnp.where(lane < 1, tap[2][1] * turned(before, 127), 0.0)
    reach = jnp.where(lane < 2, turned(edges, 126) * reach, 0.0)
    for s in range(sources):
        held = fields_ref[s, 2 * each : 3 * each, :].astype(F32)
        held = jnp.concatenate([held[:group] + reach[s], held[group:]], axis=0)
        grad_ref[chunks[s], :] = held
        put(3, s, held, back_ref)
        value = short(0, s)
        value_ref[chunks[s], :] = value
        put(0, s, value, pad_ref, rows)
        gate_ref[chunks[s], :] = short(1, s)

    causal(0, first_ref)
    anticausal(1, second_ref)
    for s in range(sources):
        at = chunks[s]
        y_one = first_ref[at, :] + scaled(value_ref[at, :], skip_one)
        y_ref[at, :] = y_one
        mid = gate_ref[at, :] * y_one
        mid_ref[at, :] = mid
        put(1, s, mid, pad_ref, rows)
    causal(1, first_ref)
    for s in range(sources):
        at = chunks[s]
        d_mid = second_ref[at, :] + scaled(grad_ref[at, :], skip_two)
        grad_one = d_mid * gate_ref[at, :]
        grad_ref[at, :] = grad_one
        put(2, s, grad_one, back_ref)
        d_gate = d_mid * y_ref[at, :]
        y_ref[at, :] = d_gate
        put(5, s, d_gate)
    anticausal(0, second_ref)
    heads = []
    for s in range(sources):
        at = chunks[s]
        y_two = first_ref[at, :] + scaled(mid_ref[at, :], skip_two)
        out_ref[s, 2 * each : 3 * each, :] = y_two.astype(BF16)
        heads.append(y_two[:group])
    heads = jnp.stack(heads[1:] + [none[0]])
    edges = jnp.where(lane < 4, turned(following, 128) * turned(heads, 2), 0.0)
    edges = jnp.where(lane < 2, turned(before, 128), edges)
    if group < 16:
        edges = jnp.concatenate([edges, jnp.zeros((sources, 16 - group, W), F32)], axis=1)
    out_ref[:, start:, :] = edges.astype(BF16)
    for s in range(sources):
        at = chunks[s]
        d_value = second_ref[at, :] + scaled(grad_ref[at, :], skip_one)
        value_ref[at, :] = d_value
        put(4, s, d_value)

    for s in range(sources):
        for kind, ref in ((0, value_ref), (1, y_ref)):
            held = ref[chunks[s], :]
            if s + 1 < sources:
                first = ref[(s + 1) * each : (s + 1) * each + group, :]
            else:
                first = jnp.zeros((group, W), F32)
            total = scaled(held, tap[kind][0])
            low, high = held[:, :TILE], held[:, TILE:]
            for j in (1, 2):
                low_j, high_j = pltpu.roll(low, TILE - j, 1), pltpu.roll(high, TILE - j, 1)
                below = jnp.concatenate([low_j[group:], pltpu.roll(first[:, :TILE], TILE - j, 1)], axis=0)
                edge = lanes_of(low) >= TILE - j
                moved = [jnp.where(edge, high_j, low_j), jnp.where(edge, below, high_j)]
                total = total + scaled(jnp.concatenate(moved, axis=1), tap[kind][j])
            out_ref[s, kind * each : (kind + 1) * each, :] = total.astype(BF16)


def gradient_kernel(units, fields_ref, kept_ref, out_ref, pad_ref, corr_ref):
    sources, _, _ = fields_ref.shape
    _, rows, _ = kept_ref.shape
    _, length = corr_ref.shape
    width = out_ref.shape[1]
    blocks = length // W
    group = rows // blocks
    each = rows // sources
    half = W // 2
    lines = length // width

    pad_ref[rows : 2 * rows, :] = jnp.zeros((rows, W), BF16)
    row8 = lax.broadcasted_iota(jnp.int32, (8, length), 0)
    b = lax.broadcasted_iota(jnp.int32, (W, W), 0)
    r = lax.broadcasted_iota(jnp.int32, (W, W), 1)
    for m in range(2):
        pad_ref[0:rows, :] = kept_ref[2 + m]
        right = jnp.concatenate(
            [pad_ref[group * d : rows + group * d, :] for d in range(blocks)], axis=1
        )
        held = kept_ref[m].astype(F32).T.astype(BF16)
        corr_ref[...] = dot(held, right)
        corr_ref[:, 0:W] = jnp.where(r >= b, corr_ref[:, 0:W], 0.0)
        total = None
        for q in range(half // 8):
            upper = corr_ref[half + 8 * q : half + 8 * q + 8, :]
            upper = jnp.concatenate([upper[:, half:], jnp.zeros((8, half), F32)], axis=1)
            both = corr_ref[8 * q : 8 * q + 8, :] + upper
            if q:
                both = pltpu.roll(both, length - 8 * q, 1)
            total = both if total is None else total + both
        for bit in (1, 2, 4):
            total = jnp.where((row8 & bit) != 0, pltpu.roll(total, length - bit, 1), total)
        line = jnp.sum(total, axis=0, keepdims=True)
        for q in range(lines):
            at = m * lines + q
            out_ref[at : at + 1, :] = line[:, q * width : (q + 1) * width]

    lane = lax.broadcasted_iota(jnp.int32, (group, width), 1)
    channel = lax.broadcasted_iota(jnp.int32, (group, width), 0)
    small = [jnp.zeros((1, width), F32)] * 16

    def put(n, products):
        by_channel = jnp.sum(products.reshape(blocks, group, W), axis=0)
        col = jnp.sum(by_channel, axis=1, keepdims=True)
        mine = lane == n % units * group + channel
        small[n // units] += jnp.sum(jnp.where(mine, col, 0.0), axis=0, keepdims=True)

    for j in range(3):
        for kind in range(2):
            field = pick(fields_ref, kind, each)
            put(2 * j + kind, kept_ref[4 + kind].astype(F32) * earlier(field, j, group))
    for m in range(2):
        put(6 + m, kept_ref[2 + m].astype(F32) * kept_ref[m].astype(F32))
    out_ref[2 * lines : 2 * lines + 16, :] = jnp.concatenate(small, axis=0)


def received_field(in_ref, units, group, parts, kind, part):
    at = (kind * parts + part) * group
    return in_ref[:, at : at + group, :].reshape(units * group, W)


def partial_kernel(
    units, in_ref, held_ref, taps_ref, series_ref, cot_ref, own_ref, part_ref, product_ref, grads_ref
):
    _, block, width = series_ref.shape
    group = width // units
    parts = block // W
    cols = gate_taps(taps_ref)
    edges = in_ref[:, 3 * parts * group :, :].astype(F32)[:, :group].reshape(width, W)
    lane = lanes_of(edges)
    second = [held_ref[0, p] for p in range(parts)]
    gate = [held_ref[1, p] for p in range(parts)]
    gate[0] += jnp.where(lane < 2, cols[2] * edges, 0.0)
    gate[0] += jnp.where(lane < 1, cols[1] * turned(edges, W - 1), 0.0)
    around = turned(edges, W - 2)
    y_two = [received_field(in_ref, units, group, parts, 2, p).astype(F32) for p in range(parts)]
    d_gate = [held_ref[2, p] * y_two[p] for p in range(parts)]
    grads = [cols[0] * held for held in d_gate]
    for j in (1, 2):
        grads = [
            have + cols[j] * held for have, held in zip(grads, later_parts(d_gate, j, around))
        ]
    w_in_part = 0.0
    w_out_part = 0.0
    for p in range(parts):
        rows = pl.ds(p * W, W)
        product = (gate[p] * y_two[p]).astype(BF16)
        product_ref[p] = product
        low = grads[p].astype(BF16)
        grads_ref[p] = low
        field = [received_field(in_ref, units, group, parts, k, p) for k in range(2)] + [low]
        w_in_part += dot(jnp.concatenate(field, axis=0), series_ref[0, rows, :])
        w_out_part += dot(product, cot_ref[0, rows, :])

    small = jnp.zeros((width, width), F32)
    for j in range(3):
        moved = earlier_parts(second, j, around) if j else second
        col = sum(jnp.sum(d * held, axis=1, keepdims=True) for d, held in zip(d_gate, moved))
        small = jnp.where(lanes_of(small) == j, col, small)
    small = small.T[0:3]

    weights = jnp.concatenate([w_in_part, w_out_part], axis=0)
    targets, sent, _ = part_ref.shape
    each = weights.shape[0] // targets
    sources = in_ref.shape[0]
    lines = (own_ref.shape[0] - 16) // 2
    slots = lines // sources
    spare = sent - each - 2 * slots - 4
    spare = [jnp.zeros((spare, width), F32)] if spare else []
    rests = []
    for s in range(sources):
        rows = [
            own_ref[s * slots : (s + 1) * slots, :],
            own_ref[lines + s * slots : lines + (s + 1) * slots, :],
            own_ref[2 * lines : 2 * lines + 1, :],
            small,
        ]
        rests.append(jnp.concatenate(rows + spare, axis=0))
    for g in range(targets):
        block = [weights[g * each : (g + 1) * each], rests[g % sources]]
        part_ref[g] = jnp.concatenate(block, axis=0).astype(BF16)


def output_kernel(units, in_ref, product_ref, grads_ref, w_in_ref, w_out_ref, out_ref, d_series_ref):
    _, block, width = out_ref.shape
    group = width // units
    parts = block // W
    w_in = w_in_ref[...]
    w_out_t = w_out_ref[...].T
    for p in range(parts):
        rows = pl.ds(p * W, W)
        out_ref[0, rows, :] = dot(w_out_t, product_ref[p]).T.astype(BF16)
        field = [received_field(in_ref, units, group, parts, k, p) for k in range(2)]
        grads = jnp.concatenate(field + [grads_ref[p]], axis=0)
        d_series_ref[0, rows, :] = dot(w_in, grads).T.astype(BF16)


def sum_kernel(in_ref, out_ref):
    targets, each, _ = out_ref.shape
    total = in_ref[0, 0:each, :].astype(F32)
    for g in range(1, targets):
        total = total + in_ref[g, 0:each, :].astype(F32)
    total = total.astype(BF16)
    for g in range(targets):
        out_ref[g] = total


def small_kernel(units, each, scale, in_ref, one_ref, two_ref, taps_ref, skip_one_ref, skip_two_ref):
    targets, _, width = in_ref.shape
    filters, block = one_ref.shape
    slots = block // width
    group = width // units
    by_unit = []
    for u in range(units):
        sums = 0.0
        for g in range(u, targets, units):
            sums += in_ref[g, each:, :].astype(F32)
        by_unit.append(sums * scale)
    repeat = units // filters
    for f in range(filters):
        sums = by_unit[f * repeat]
        for u in range(f * repeat + 1, (f + 1) * repeat):
            sums = sums + by_unit[u]
        for q in range(slots):
            one_ref[f : f + 1, q * width : (q + 1) * width] = sums[q : q + 1]
            two_ref[f : f + 1, q * width : (q + 1) * width] = sums[slots + q : slots + q + 1]

    row = lax.broadcasted_iota(jnp.int32, (units, width), 0)
    lane = lax.broadcasted_iota(jnp.int32, (units, width), 1)
    held = jnp.concatenate([sums[2 * slots : 2 * slots + 1] for sums in by_unit], axis=0)
    small = 0.0
    for shift in range(units):
        moved = pltpu.roll(held, shift * group, 1) if shift else held
        moved = jnp.where(lane // group == row, moved, 0.0)
        small += pltpu.roll(moved, units - shift, 0) if shift else moved
    gate = sum(by_unit)[2 * slots + 1 : 2 * slots + 4]
    for j in range(3):
        for kind in range(2):
            n = 2 * j + kind
            taps_ref[j : j + 1, kind * width : (kind + 1) * width] = small[n : n + 1]
    taps_ref[:, 2 * width :] = gate
    skip_one_ref[...] = small[6:7]
    skip_two_ref[...] = small[7:8]


def weight_kernel(scale, in_ref, w_in_ref, w_out_ref):
    targets, each, width = in_ref.shape
    weights = jnp.concatenate([in_ref[g].astype(F32) for g in range(targets)], axis=0) * scale
    for kind in range(3):
        w_in_ref[:, kind * width : (kind + 1) * width] = weights[kind * width : (kind + 1) * width].T
    w_out_ref[...] = weights[3 * width :]


def all_to_all(blocks, axis):
    return lax.all_to_all(blocks, axis, split_axis=0, concat_axis=0, tiled=True)


def shards(series, cotangent, w_in, w_out, taps, skip_one, skip_two, filter_one, filter_two):
    count, block, width = series.shape
    filters = filter_one.shape[0]
    sources = lax.axis_size("seq")
    copies = lax.axis_size("dp")
    length = block * sources
    units = sources // count
    group = width // units
    assert count == 1 and units >= 8 and 2 * block // width <= 16 and units % filters == 0 and block % W == 0
    blocks = length // W
    rows = blocks * group
    scale = 1.0 / math.sqrt(count * copies * length)
    shape = jax.ShapeDtypeStruct

    devices = sources * copies
    packed = 3 * (block // W) * group + 16
    skips = (skip_one.reshape(1, width), skip_two.reshape(1, width))
    fields, params = call(
        functools.partial(project_kernel, units),
        (shape((sources, packed, W), BF16), shape((8, 3 * width), F32)),
        flops=2 * block * width * 4 * width,
        moved=8 * block * width * 4,
        limit=VMEM_ALL,
    )(series, cotangent, w_in, w_out, taps, *skips, filter_one, filter_two)
    fields = all_to_all(fields, "seq")
    held = call(
        gate_kernel,
        shape((3, block // W, width, W), F32),
        flops=2 * block * width * 2 * width,
        moved=4 * 4 * block * width,
    )(series, cotangent, w_in, w_out, params)

    sent, kept = call(
        functools.partial(operator_kernel, units),
        (shape((sources, packed, W), BF16), shape((7, rows, W), BF16)),
        [
            pltpu.VMEM((2 * rows, W), BF16),
            pltpu.VMEM((2 * rows, W), BF16),
            pltpu.VMEM((2, blocks, W, W), BF16),
            pltpu.VMEM((7, rows, W), F32),
        ],
        flops=4 * 2 * rows * length * W,
        moved=2 * W * length * 2 * 2,
    )(fields, params)

    back = all_to_all(sent, "seq")

    own = call(
        functools.partial(gradient_kernel, units),
        shape((2 * (length // width) + 16, width), F32),
        [pltpu.VMEM((2 * rows, W), BF16), pltpu.VMEM((W, length), F32)],
        flops=2 * 2 * rows * length * W,
        moved=2 * length * width * 2,
    )(fields, kept)

    each = 4 * width // devices
    sent_rows = -(-(each + 2 * (block // width) + 4) // 16) * 16
    partial, product, grads = call(
        functools.partial(partial_kernel, units),
        (
            shape((devices, sent_rows, width), BF16),
            shape((block // W, width, W), BF16),
            shape((block // W, width, W), BF16),
        ),
        flops=2 * block * width * 4 * width,
        moved=2 * block * width * 6,
    )(back, held, params, series, cotangent, own)
    partial = all_to_all(partial, ("dp", "seq"))

    output, d_series = call(
        functools.partial(output_kernel, units),
        (shape(series.shape, BF16), shape(series.shape, BF16)),
        flops=2 * block * width * 4 * width,
        moved=2 * block * width * 6,
    )(back, product, grads, w_in, w_out)

    sums = call(
        sum_kernel,
        shape((devices, each, width), BF16),
        flops=devices * each * width,
        moved=4 * devices * each * width,
    )(partial)
    sums = all_to_all(sums, ("dp", "seq"))

    grad_one, grad_two, grad_taps, grad_skip_one, grad_skip_two = call(
        functools.partial(small_kernel, units, each, scale),
        (
            shape(filter_one.shape, F32),
            shape(filter_two.shape, F32),
            shape(taps.shape, F32),
            shape((1, width), F32),
            shape((1, width), F32),
        ),
        flops=devices * sent_rows * width,
        moved=4 * devices * sent_rows * width,
    )(partial)
    grad_w_in, grad_w_out = call(
        functools.partial(weight_kernel, scale),
        (shape(w_in.shape, F32), shape(w_out.shape, F32)),
        flops=devices * each * width,
        moved=2 * devices * each * width,
    )(sums)
    return (
        output,
        d_series,
        grad_w_in,
        grad_w_out,
        grad_taps,
        grad_skip_one.reshape(width),
        grad_skip_two.reshape(width),
        grad_one,
        grad_two,
    )


def solution(mesh):
    specs = (
        P("dp", "seq", None),
        P("dp", "seq", None),
        P(),
        P(),
        P(),
        P(),
        P(),
        P(None, "seq"),
        P(None, "seq"),
    )
    return jax.shard_map(shards, mesh=mesh, in_specs=specs, out_specs=specs, check_vma=False)
```

```python
import functools
import math

import jax
import jax.numpy as jnp
from jax import lax
from jax.experimental import pallas as pl
from jax.experimental.pallas import tpu as pltpu
from jax.sharding import PartitionSpec as P

W = 256
TILE = 128
F32 = jnp.float32
BF16 = jnp.bfloat16
NT = (((1,), (1,)), ((), ()))
VMEM_LIMIT = 24 * 1024 * 1024
VMEM_ALL = 56 * 1024 * 1024


def call(body, out_shape, scratch=(), flops=0, moved=0, limit=VMEM_LIMIT):
    return pl.pallas_call(
        body,
        out_shape=out_shape,
        scratch_shapes=list(scratch),
        compiler_params=pltpu.CompilerParams(vmem_limit_bytes=limit),
        cost_estimate=pl.CostEstimate(flops=flops, bytes_accessed=moved, transcendentals=0),
    )


def dot(a, b):
    return jnp.dot(a, b, preferred_element_type=F32)


def dot_nt(a, b):
    return lax.dot_general(a, b, NT, preferred_element_type=F32)


def lanes_of(field):
    return lax.broadcasted_iota(jnp.int32, field.shape, field.ndim - 1)


def turned(field, shift):
    return pltpu.roll(field, shift, field.ndim - 1)


def tiles_of(parts):
    return [held[:, at : at + TILE] for held in parts for at in range(0, W, TILE)]


def parts_of(tiles):
    each = W // TILE
    return [jnp.concatenate(tiles[at : at + each], axis=1) for at in range(0, len(tiles), each)]


def fold(edges):
    total = edges[..., :8, :]
    for k in range(1, edges.shape[-2] // 8):
        total = total + turned(edges[..., 8 * k : 8 * k + 8, :], 64 * k)
    return total


def unfold(edges, group):
    pieces = [edges] + [turned(edges, W - 64 * k) for k in range(1, group // 8)]
    return jnp.concatenate(pieces, axis=edges.ndim - 2)


def earlier_parts(parts, j, before):
    moved = [turned(tile, j) for tile in tiles_of([before] + parts)]
    moved = moved[W // TILE - 1 :]
    edge = lanes_of(moved[0]) < j
    return parts_of([jnp.where(edge, ahead, tile) for ahead, tile in zip(moved, moved[1:])])


def later_parts(parts, j, behind):
    moved = [turned(tile, TILE - j) for tile in tiles_of(parts + [behind])]
    moved = moved[: len(moved) - W // TILE + 1]
    edge = lanes_of(moved[0]) >= TILE - j
    return parts_of([jnp.where(edge, following, tile) for tile, following in zip(moved, moved[1:])])


def gate_taps(taps_ref):
    width = taps_ref.shape[1] // 3
    rows = jnp.concatenate([taps_ref[0:3, 2 * width :], jnp.zeros((5, width), F32)], axis=0)
    cols = jnp.concatenate([rows] * (width // 8), axis=0).T
    return [cols[:, j : j + 1] for j in range(3)]


def gate_local(second, cols):
    zeros = jnp.zeros_like(second[0])
    total = [cols[0] * held for held in second]
    for j in (1, 2):
        moved = earlier_parts(second, j, zeros)
        total = [have + cols[j] * held for have, held in zip(total, moved)]
    return total


def project_kernel(
    units,
    series_ref,
    cot_ref,
    w_in_ref,
    w_out_ref,
    taps_ref,
    skip_one_ref,
    skip_two_ref,
    one_ref,
    two_ref,
    out_ref,
    params_ref,
):
    _, block, width = series_ref.shape
    group = width // units
    parts = block // W
    params_ref[...] = jnp.zeros(params_ref.shape, F32)
    params_ref[0:3, :] = taps_ref[...]
    params_ref[3:4, 0:width] = skip_one_ref[...]
    params_ref[4:5, 0:width] = skip_two_ref[...]
    w_in_t = w_in_ref[...].T
    w_out = w_out_ref[...]
    proj = [dot_nt(w_in_t, series_ref[0, p * W : (p + 1) * W, :]) for p in range(parts)]
    d_prod = [dot_nt(w_out, cot_ref[0, p * W : (p + 1) * W, :]) for p in range(parts)]
    second = [held[2 * width :] for held in proj]
    gate = gate_local(second, gate_taps(taps_ref))
    for p in range(parts):
        fields = [proj[p][:width], proj[p][width : 2 * width], d_prod[p] * gate[p]]
        for kind, field in enumerate(fields):
            at = (kind * parts + p) * group
            out_ref[:, at : at + group, :] = field.astype(BF16).reshape(units, group, W)

    lane = lanes_of(second[0])
    edges = jnp.where((lane >= 128) & (lane < 130), turned(second[-1], 130), 0.0)
    edges = jnp.where((lane >= 130) & (lane < 132), turned(d_prod[0], 130), edges)
    lines = [
        ref[:, q * width : (q + 1) * width]
        for ref in (one_ref, two_ref)
        for q in range(block // width)
    ]
    repeat = units // one_ref.shape[0]
    for u in range(units):
        row = u // repeat
        held = jnp.concatenate([line[row : row + 1] for line in lines], axis=0)
        held = jnp.concatenate([held, jnp.zeros((held.shape[0], W - width), F32)], axis=1)
        edge = fold(edges[u * group : (u + 1) * group])
        out_ref[u, 3 * parts * group :, :] = (held + edge).astype(BF16)


def gate_kernel(series_ref, cot_ref, w_in_ref, w_out_ref, taps_ref, out_ref):
    _, block, width = series_ref.shape
    parts = block // W
    w_two_t = w_in_ref[:, 2 * width :].T
    w_out = w_out_ref[...]
    second = [dot_nt(w_two_t, series_ref[0, p * W : (p + 1) * W, :]) for p in range(parts)]
    gate = gate_local(second, gate_taps(taps_ref))
    for p in range(parts):
        out_ref[0, p] = second[p]
        out_ref[1, p] = gate[p]
        out_ref[2, p] = dot_nt(w_out, cot_ref[0, p * W : (p + 1) * W, :])


def build_toeplitz(fields_ref, start, toep_ref):
    sources = fields_ref.shape[0]
    _, blocks, _, _ = toep_ref.shape
    slots = blocks // sources * (W // TILE)
    lane = lax.broadcasted_iota(jnp.int32, (16, TILE), 1)
    row = lax.broadcasted_iota(jnp.int32, (16, TILE), 0)
    none = jnp.zeros((16, TILE), F32)
    for m in range(2):
        behind = {}

        def shifted(tile, shift):
            moved = pltpu.roll(tile, shift, 1) if shift else tile
            ahead, behind[shift] = behind.get(shift, none), moved
            return jnp.where(lane < shift, ahead, moved) if shift else moved

        for q in range(TILE // 16):
            at = TILE + 16 * q
            toep_ref[m, 0, at : at + 16, 0:TILE] = none.astype(BF16)
        held = {}
        for s in range(sources):
            lines = fields_ref[s, start:, :].astype(F32)
            for i in range(slots):
                d, part = divmod(s * slots + i, W // TILE)
                line = lines[m * slots + i : m * slots + i + 1, :TILE]
                tile = jnp.broadcast_to(line, (16, TILE))
                for bit in (1, 2, 4, 8):
                    moved = pltpu.roll(tile, bit, 1)
                    ahead, held[bit] = held.get(bit, none), moved
                    tile = jnp.where((row & bit) != 0, jnp.where(lane < bit, ahead, moved), tile)
                for q in range(TILE // 16):
                    low = shifted(tile, 16 * q).astype(BF16)
                    at = 16 * q
                    toep_ref[m, d, at : at + 16, part * TILE : (part + 1) * TILE] = low
                    if part == 0:
                        toep_ref[m, d, TILE + at : TILE + at + 16, TILE:] = low
                    elif d + 1 < blocks:
                        toep_ref[m, d + 1, TILE + at : TILE + at + 16, 0:TILE] = low


def earlier(field, j, group):
    if j == 0:
        return field
    low, high = pltpu.roll(field[:, :TILE], j, 1), pltpu.roll(field[:, TILE:], j, 1)
    above = jnp.concatenate([jnp.zeros((group, TILE), F32), high[:-group]], axis=0)
    edge = lanes_of(low) < j
    return jnp.concatenate([jnp.where(edge, above, low), jnp.where(edge, low, high)], axis=1)


def own_lanes(f, group, width):
    lane = lax.broadcasted_iota(jnp.int32, (group, width), 1)
    channel = lax.broadcasted_iota(jnp.int32, (group, width), 0)
    return lane == f * group + channel


def pick(ref, kind, received):
    rows = received
    field = ref[:, kind * rows : (kind + 1) * rows, :]
    return field.reshape(field.shape[0] * rows, W).astype(F32)


def operator_kernel(
    units,
    fields_ref,
    taps_ref,
    out_ref,
    kept_ref,
    pad_ref,
    back_ref,
    toep_ref,
    wide_ref,
):
    sources, _, _ = out_ref.shape
    _, rows, _ = kept_ref.shape
    each = rows // sources
    start = 3 * each
    build_toeplitz(fields_ref, start, toep_ref)
    width = taps_ref.shape[1] // 3
    group = width // units
    blocks = rows // group
    u = lax.rem(lax.axis_index("seq"), units)
    mine = own_lanes(u, group, width)
    value_ref, gate_ref, y_ref, mid_ref, grad_ref, first_ref, second_ref = [
        wide_ref.at[i] for i in range(7)
    ]

    def column(values):
        col = jnp.sum(jnp.where(mine, values, 0.0), axis=1, keepdims=True)
        return jnp.broadcast_to(col, (group, W))

    def scaled(field, col):
        return (field.reshape(-1, group, W) * col[None]).reshape(field.shape)

    tap = [
        [
            column(taps_ref[j : j + 1, kind * width : (kind + 1) * width])
            for j in range(3)
        ]
        for kind in range(3)
    ]
    skip_one = column(taps_ref[3:4, 0:width])
    skip_two = column(taps_ref[4:5, 0:width])
    chunks = [slice(s * each, (s + 1) * each) for s in range(sources)]

    zeros = jnp.zeros((rows, W), BF16)
    pad_ref[0:rows, :] = zeros
    back_ref[rows : 2 * rows, :] = zeros

    def causal(order, into_ref):
        left = jnp.concatenate(
            [pad_ref[rows - group * d : 2 * rows - group * d, :] for d in range(blocks)], axis=1
        )
        into_ref[...] = dot(left, toep_ref[order].reshape(blocks * W, W))

    def anticausal(order, into_ref):
        left = jnp.concatenate(
            [back_ref[group * d : rows + group * d, :] for d in range(blocks)], axis=1
        )
        right = jnp.concatenate([toep_ref[order, d] for d in range(blocks)], axis=1)
        into_ref[...] = dot_nt(left, right)

    def put(slot, s, field, into_ref=None, at=0):
        low = field.astype(BF16)
        kept_ref[slot, chunks[s], :] = low
        if into_ref is not None:
            into_ref[at + s * each : at + (s + 1) * each, :] = low

    def short(kind, s):
        held = fields_ref[s, kind * each : (kind + 1) * each, :].astype(F32)
        if s:
            last = fields_ref[s - 1, (kind + 1) * each - group : (kind + 1) * each, :].astype(F32)
        else:
            last = jnp.zeros((group, W), F32)
        total = scaled(held, tap[kind][0])
        low, high = held[:, :TILE], held[:, TILE:]
        for j in (1, 2):
            low_j, high_j = pltpu.roll(low, j, 1), pltpu.roll(high, j, 1)
            above = jnp.concatenate([pltpu.roll(last[:, TILE:], j, 1), high_j[:-group]], axis=0)
            edge = lanes_of(low) < j
            moved = [jnp.where(edge, above, low_j), jnp.where(edge, low_j, high_j)]
            total = total + scaled(jnp.concatenate(moved, axis=1), tap[kind][j])
        return total

    edges = unfold(fields_ref[:, start:, :].astype(F32), group)
    none = jnp.zeros((1, group, W), F32)
    before = jnp.concatenate([none, edges[:-1]], axis=0)
    following = jnp.concatenate([edges[1:], none], axis=0)
    lane = lanes_of(edges)
    reach = tap[2][2] * turned(before, 128)
    reach = reach + jnp.where(lane < 1, tap[2][1] * turned(before, 127), 0.0)
    reach = jnp.where(lane < 2, turned(edges, 126) * reach, 0.0)
    for s in range(sources):
        held = fields_ref[s, 2 * each : 3 * each, :].astype(F32)
        held = jnp.concatenate([held[:group] + reach[s], held[group:]], axis=0)
        grad_ref[chunks[s], :] = held
        put(3, s, held, back_ref)
        value = short(0, s)
        value_ref[chunks[s], :] = value
        put(0, s, value, pad_ref, rows)
        gate_ref[chunks[s], :] = short(1, s)

    causal(0, first_ref)
    anticausal(1, second_ref)
    for s in range(sources):
        at = chunks[s]
        y_one = first_ref[at, :] + scaled(value_ref[at, :], skip_one)
        y_ref[at, :] = y_one
        mid = gate_ref[at, :] * y_one
        mid_ref[at, :] = mid
        put(1, s, mid, pad_ref, rows)
    causal(1, first_ref)
    for s in range(sources):
        at = chunks[s]
        d_mid = second_ref[at, :] + scaled(grad_ref[at, :], skip_two)
        grad_one = d_mid * gate_ref[at, :]
        grad_ref[at, :] = grad_one
        put(2, s, grad_one, back_ref)
        d_gate = d_mid * y_ref[at, :]
        y_ref[at, :] = d_gate
        put(5, s, d_gate)
    anticausal(0, second_ref)
    heads = []
    for s in range(sources):
        at = chunks[s]
        y_two = first_ref[at, :] + scaled(mid_ref[at, :], skip_two)
        out_ref[s, 2 * each : 3 * each, :] = y_two.astype(BF16)
        heads.append(y_two[:group])
    heads = jnp.stack(heads[1:] + [none[0]])
    edges = jnp.where(lane < 4, turned(following, 128) * turned(heads, 2), 0.0)
    edges = jnp.where(lane < 2, turned(before, 128), edges)
    out_ref[:, start:, :] = fold(edges).astype(BF16)
    for s in range(sources):
        at = chunks[s]
        d_value = second_ref[at, :] + scaled(grad_ref[at, :], skip_one)
        value_ref[at, :] = d_value
        put(4, s, d_value)

    for s in range(sources):
        for kind, ref in ((0, value_ref), (1, y_ref)):
            held = ref[chunks[s], :]
            if s + 1 < sources:
                first = ref[(s + 1) * each : (s + 1) * each + group, :]
            else:
                first = jnp.zeros((group, W), F32)
            total = scaled(held, tap[kind][0])
            low, high = held[:, :TILE], held[:, TILE:]
            for j in (1, 2):
                low_j, high_j = pltpu.roll(low, TILE - j, 1), pltpu.roll(high, TILE - j, 1)
                below = jnp.concatenate([low_j[group:], pltpu.roll(first[:, :TILE], TILE - j, 1)], axis=0)
                edge = lanes_of(low) >= TILE - j
                moved = [jnp.where(edge, high_j, low_j), jnp.where(edge, below, high_j)]
                total = total + scaled(jnp.concatenate(moved, axis=1), tap[kind][j])
            out_ref[s, kind * each : (kind + 1) * each, :] = total.astype(BF16)


def gradient_kernel(units, fields_ref, kept_ref, out_ref, pad_ref, corr_ref):
    sources, _, _ = fields_ref.shape
    _, rows, _ = kept_ref.shape
    _, length = corr_ref.shape
    width = out_ref.shape[1]
    blocks = length // W
    group = rows // blocks
    each = rows // sources
    half = W // 2
    lines = length // width

    pad_ref[rows : 2 * rows, :] = jnp.zeros((rows, W), BF16)
    row8 = lax.broadcasted_iota(jnp.int32, (8, length), 0)
    b = lax.broadcasted_iota(jnp.int32, (W, W), 0)
    r = lax.broadcasted_iota(jnp.int32, (W, W), 1)
    for m in range(2):
        pad_ref[0:rows, :] = kept_ref[2 + m]
        right = jnp.concatenate(
            [pad_ref[group * d : rows + group * d, :] for d in range(blocks)], axis=1
        )
        held = kept_ref[m].astype(F32).T.astype(BF16)
        corr_ref[...] = dot(held, right)
        corr_ref[:, 0:W] = jnp.where(r >= b, corr_ref[:, 0:W], 0.0)
        total = None
        for q in range(half // 8):
            upper = corr_ref[half + 8 * q : half + 8 * q + 8, :]
            upper = jnp.concatenate([upper[:, half:], jnp.zeros((8, half), F32)], axis=1)
            both = corr_ref[8 * q : 8 * q + 8, :] + upper
            if q:
                both = pltpu.roll(both, length - 8 * q, 1)
            total = both if total is None else total + both
        for bit in (1, 2, 4):
            total = jnp.where((row8 & bit) != 0, pltpu.roll(total, length - bit, 1), total)
        line = jnp.sum(total, axis=0, keepdims=True)
        for q in range(lines):
            at = m * lines + q
            out_ref[at : at + 1, :] = line[:, q * width : (q + 1) * width]

    lane = lax.broadcasted_iota(jnp.int32, (group, width), 1)
    channel = lax.broadcasted_iota(jnp.int32, (group, width), 0)
    small = [jnp.zeros((1, width), F32)] * 16

    def put(n, products):
        by_channel = jnp.sum(products.reshape(blocks, group, W), axis=0)
        col = jnp.sum(by_channel, axis=1, keepdims=True)
        mine = lane == n % units * group + channel
        small[n // units] += jnp.sum(jnp.where(mine, col, 0.0), axis=0, keepdims=True)

    for j in range(3):
        for kind in range(2):
            field = pick(fields_ref, kind, each)
            put(2 * j + kind, kept_ref[4 + kind].astype(F32) * earlier(field, j, group))
    for m in range(2):
        put(6 + m, kept_ref[2 + m].astype(F32) * kept_ref[m].astype(F32))
    out_ref[2 * lines : 2 * lines + 16, :] = jnp.concatenate(small, axis=0)


def received_field(in_ref, units, group, parts, kind, part):
    at = (kind * parts + part) * group
    return in_ref[:, at : at + group, :].reshape(units * group, W)


def partial_kernel(
    units, in_ref, held_ref, taps_ref, series_ref, cot_ref, own_ref, part_ref, product_ref, grads_ref
):
    _, block, width = series_ref.shape
    group = width // units
    parts = block // W
    cols = gate_taps(taps_ref)
    edges = unfold(in_ref[:, 3 * parts * group :, :].astype(F32), group).reshape(width, W)
    lane = lanes_of(edges)
    second = [held_ref[0, p] for p in range(parts)]
    gate = [held_ref[1, p] for p in range(parts)]
    gate[0] += jnp.where(lane < 2, cols[2] * edges, 0.0)
    gate[0] += jnp.where(lane < 1, cols[1] * turned(edges, W - 1), 0.0)
    around = turned(edges, W - 2)
    y_two = [received_field(in_ref, units, group, parts, 2, p).astype(F32) for p in range(parts)]
    d_gate = [held_ref[2, p] * y_two[p] for p in range(parts)]
    grads = [cols[0] * held for held in d_gate]
    for j in (1, 2):
        grads = [
            have + cols[j] * held for have, held in zip(grads, later_parts(d_gate, j, around))
        ]
    w_in_part = 0.0
    w_out_part = 0.0
    for p in range(parts):
        rows = pl.ds(p * W, W)
        product = (gate[p] * y_two[p]).astype(BF16)
        product_ref[p] = product
        low = grads[p].astype(BF16)
        grads_ref[p] = low
        field = [received_field(in_ref, units, group, parts, k, p) for k in range(2)] + [low]
        w_in_part += dot(jnp.concatenate(field, axis=0), series_ref[0, rows, :])
        w_out_part += dot(product, cot_ref[0, rows, :])

    small = jnp.zeros((width, width), F32)
    for j in range(3):
        moved = earlier_parts(second, j, around) if j else second
        col = sum(jnp.sum(d * held, axis=1, keepdims=True) for d, held in zip(d_gate, moved))
        small = jnp.where(lanes_of(small) == j, col, small)
    small = small.T[0:3]

    weights = jnp.concatenate([w_in_part, w_out_part], axis=0)
    targets, sent, _ = part_ref.shape
    each = weights.shape[0] // targets
    sources = in_ref.shape[0]
    lines = (own_ref.shape[0] - 16) // 2
    slots = lines // sources
    spare = sent - each - 2 * slots - 4
    spare = [jnp.zeros((spare, width), F32)] if spare else []
    rests = []
    for s in range(sources):
        rows = [
            own_ref[s * slots : (s + 1) * slots, :],
            own_ref[lines + s * slots : lines + (s + 1) * slots, :],
            own_ref[2 * lines : 2 * lines + 1, :],
            small,
        ]
        rests.append(jnp.concatenate(rows + spare, axis=0))
    for g in range(targets):
        block = [weights[g * each : (g + 1) * each], rests[g % sources]]
        part_ref[g] = jnp.concatenate(block, axis=0).astype(BF16)


def output_kernel(units, in_ref, product_ref, grads_ref, w_in_ref, w_out_ref, out_ref, d_series_ref):
    _, block, width = out_ref.shape
    group = width // units
    parts = block // W
    w_in = w_in_ref[...]
    w_out_t = w_out_ref[...].T
    for p in range(parts):
        rows = pl.ds(p * W, W)
        out_ref[0, rows, :] = dot(w_out_t, product_ref[p]).T.astype(BF16)
        field = [received_field(in_ref, units, group, parts, k, p) for k in range(2)]
        grads = jnp.concatenate(field + [grads_ref[p]], axis=0)
        d_series_ref[0, rows, :] = dot(w_in, grads).T.astype(BF16)


def sum_kernel(in_ref, out_ref):
    targets, each, _ = out_ref.shape
    total = in_ref[0, 0:each, :].astype(F32)
    for g in range(1, targets):
        total = total + in_ref[g, 0:each, :].astype(F32)
    total = total.astype(BF16)
    for g in range(targets):
        out_ref[g] = total


def small_kernel(units, each, scale, in_ref, one_ref, two_ref, taps_ref, skip_one_ref, skip_two_ref):
    targets, _, width = in_ref.shape
    filters, block = one_ref.shape
    slots = block // width
    group = width // units
    by_unit = []
    for u in range(units):
        sums = 0.0
        for g in range(u, targets, units):
            sums += in_ref[g, each:, :].astype(F32)
        by_unit.append(sums * scale)
    repeat = units // filters
    for f in range(filters):
        sums = by_unit[f * repeat]
        for u in range(f * repeat + 1, (f + 1) * repeat):
            sums = sums + by_unit[u]
        for q in range(slots):
            one_ref[f : f + 1, q * width : (q + 1) * width] = sums[q : q + 1]
            two_ref[f : f + 1, q * width : (q + 1) * width] = sums[slots + q : slots + q + 1]

    row = lax.broadcasted_iota(jnp.int32, (units, width), 0)
    lane = lax.broadcasted_iota(jnp.int32, (units, width), 1)
    held = jnp.concatenate([sums[2 * slots : 2 * slots + 1] for sums in by_unit], axis=0)
    small = 0.0
    for shift in range(units):
        moved = pltpu.roll(held, shift * group, 1) if shift else held
        moved = jnp.where(lane // group == row, moved, 0.0)
        small += pltpu.roll(moved, units - shift, 0) if shift else moved
    gate = sum(by_unit)[2 * slots + 1 : 2 * slots + 4]
    for j in range(3):
        for kind in range(2):
            n = 2 * j + kind
            taps_ref[j : j + 1, kind * width : (kind + 1) * width] = small[n : n + 1]
    taps_ref[:, 2 * width :] = gate
    skip_one_ref[...] = small[6:7]
    skip_two_ref[...] = small[7:8]


def weight_kernel(scale, in_ref, w_in_ref, w_out_ref):
    targets, each, width = in_ref.shape
    weights = jnp.concatenate([in_ref[g].astype(F32) for g in range(targets)], axis=0) * scale
    for kind in range(3):
        w_in_ref[:, kind * width : (kind + 1) * width] = weights[kind * width : (kind + 1) * width].T
    w_out_ref[...] = weights[3 * width :]


def all_to_all(blocks, axis):
    return lax.all_to_all(blocks, axis, split_axis=0, concat_axis=0, tiled=True)


def shards(series, cotangent, w_in, w_out, taps, skip_one, skip_two, filter_one, filter_two):
    count, block, width = series.shape
    filters = filter_one.shape[0]
    sources = lax.axis_size("seq")
    copies = lax.axis_size("dp")
    length = block * sources
    units = sources // count
    group = width // units
    assert count == 1 and units >= 8 and 2 * block // width <= 16 and units % filters == 0 and block % W == 0
    blocks = length // W
    rows = blocks * group
    scale = 1.0 / math.sqrt(count * copies * length)
    shape = jax.ShapeDtypeStruct

    devices = sources * copies
    assert 2 * block // width == 8 and group in (8, 16)
    packed = 3 * (block // W) * group + 8
    skips = (skip_one.reshape(1, width), skip_two.reshape(1, width))
    fields, params = call(
        functools.partial(project_kernel, units),
        (shape((sources, packed, W), BF16), shape((8, 3 * width), F32)),
        flops=2 * block * width * 4 * width,
        moved=8 * block * width * 4,
        limit=VMEM_ALL,
    )(series, cotangent, w_in, w_out, taps, *skips, filter_one, filter_two)
    fields = all_to_all(fields, "seq")
    held = call(
        gate_kernel,
        shape((3, block // W, width, W), F32),
        flops=2 * block * width * 2 * width,
        moved=4 * 4 * block * width,
    )(series, cotangent, w_in, w_out, params)

    sent, kept = call(
        functools.partial(operator_kernel, units),
        (shape((sources, packed, W), BF16), shape((7, rows, W), BF16)),
        [
            pltpu.VMEM((2 * rows, W), BF16),
            pltpu.VMEM((2 * rows, W), BF16),
            pltpu.VMEM((2, blocks, W, W), BF16),
            pltpu.VMEM((7, rows, W), F32),
        ],
        flops=4 * 2 * rows * length * W,
        moved=2 * W * length * 2 * 2,
    )(fields, params)

    back = all_to_all(sent, "seq")

    own = call(
        functools.partial(gradient_kernel, units),
        shape((2 * (length // width) + 16, width), F32),
        [pltpu.VMEM((2 * rows, W), BF16), pltpu.VMEM((W, length), F32)],
        flops=2 * 2 * rows * length * W,
        moved=2 * length * width * 2,
    )(fields, kept)

    each = 4 * width // devices
    sent_rows = -(-(each + 2 * (block // width) + 4) // 16) * 16
    partial, product, grads = call(
        functools.partial(partial_kernel, units),
        (
            shape((devices, sent_rows, width), BF16),
            shape((block // W, width, W), BF16),
            shape((block // W, width, W), BF16),
        ),
        flops=2 * block * width * 4 * width,
        moved=2 * block * width * 6,
    )(back, held, params, series, cotangent, own)
    partial = all_to_all(partial, ("dp", "seq"))

    output, d_series = call(
        functools.partial(output_kernel, units),
        (shape(series.shape, BF16), shape(series.shape, BF16)),
        flops=2 * block * width * 4 * width,
        moved=2 * block * width * 6,
    )(back, product, grads, w_in, w_out)

    sums = call(
        sum_kernel,
        shape((devices, each, width), BF16),
        flops=devices * each * width,
        moved=4 * devices * each * width,
    )(partial)
    sums = all_to_all(sums, ("dp", "seq"))

    grad_one, grad_two, grad_taps, grad_skip_one, grad_skip_two = call(
        functools.partial(small_kernel, units, each, scale),
        (
            shape(filter_one.shape, F32),
            shape(filter_two.shape, F32),
            shape(taps.shape, F32),
            shape((1, width), F32),
            shape((1, width), F32),
        ),
        flops=devices * sent_rows * width,
        moved=4 * devices * sent_rows * width,
    )(partial)
    grad_w_in, grad_w_out = call(
        functools.partial(weight_kernel, scale),
        (shape(w_in.shape, F32), shape(w_out.shape, F32)),
        flops=devices * each * width,
        moved=2 * devices * each * width,
    )(sums)
    return (
        output,
        d_series,
        grad_w_in,
        grad_w_out,
        grad_taps,
        grad_skip_one.reshape(width),
        grad_skip_two.reshape(width),
        grad_one,
        grad_two,
    )


def solution(mesh):
    specs = (
        P("dp", "seq", None),
        P("dp", "seq", None),
        P(),
        P(),
        P(),
        P(),
        P(),
        P(None, "seq"),
        P(None, "seq"),
    )
    return jax.shard_map(shards, mesh=mesh, in_specs=specs, out_specs=specs, check_vma=False)
```

```python
import functools
import math

import jax
import jax.numpy as jnp
from jax import lax
from jax.experimental import pallas as pl
from jax.experimental.pallas import tpu as pltpu
from jax.sharding import PartitionSpec as P

W = 256
TILE = 128
F32 = jnp.float32
BF16 = jnp.bfloat16
NT = (((1,), (1,)), ((), ()))
VMEM_LIMIT = 24 * 1024 * 1024
VMEM_ALL = 56 * 1024 * 1024


def call(body, out_shape, scratch=(), flops=0, moved=0, limit=VMEM_LIMIT):
    return pl.pallas_call(
        body,
        out_shape=out_shape,
        scratch_shapes=list(scratch),
        compiler_params=pltpu.CompilerParams(vmem_limit_bytes=limit),
        cost_estimate=pl.CostEstimate(flops=flops, bytes_accessed=moved, transcendentals=0),
    )


def dot(a, b):
    return jnp.dot(a, b, preferred_element_type=F32)


def dot_nt(a, b):
    return lax.dot_general(a, b, NT, preferred_element_type=F32)


def lanes_of(field):
    return lax.broadcasted_iota(jnp.int32, field.shape, field.ndim - 1)


def turned(field, shift):
    return pltpu.roll(field, shift, field.ndim - 1)


def tiles_of(parts):
    return [held[:, at : at + TILE] for held in parts for at in range(0, W, TILE)]


def parts_of(tiles):
    each = W // TILE
    return [jnp.concatenate(tiles[at : at + each], axis=1) for at in range(0, len(tiles), each)]


def fold(edges):
    total = edges[..., :8, :]
    for k in range(1, edges.shape[-2] // 8):
        total = total + turned(edges[..., 8 * k : 8 * k + 8, :], 64 * k)
    return total


def unfold(edges, group):
    pieces = [edges] + [turned(edges, W - 64 * k) for k in range(1, group // 8)]
    return jnp.concatenate(pieces, axis=edges.ndim - 2)


def earlier_parts(parts, j, before):
    moved = [turned(tile, j) for tile in tiles_of([before] + parts)]
    moved = moved[W // TILE - 1 :]
    edge = lanes_of(moved[0]) < j
    return parts_of([jnp.where(edge, ahead, tile) for ahead, tile in zip(moved, moved[1:])])


def later_parts(parts, j, behind):
    moved = [turned(tile, TILE - j) for tile in tiles_of(parts + [behind])]
    moved = moved[: len(moved) - W // TILE + 1]
    edge = lanes_of(moved[0]) >= TILE - j
    return parts_of([jnp.where(edge, following, tile) for tile, following in zip(moved, moved[1:])])


def gate_taps(taps_ref):
    width = taps_ref.shape[1] // 3
    rows = jnp.concatenate([taps_ref[0:3, 2 * width :], jnp.zeros((5, width), F32)], axis=0)
    cols = jnp.concatenate([rows] * (width // 8), axis=0).T
    return [cols[:, j : j + 1] for j in range(3)]


def gate_local(second, cols):
    zeros = jnp.zeros_like(second[0])
    total = [cols[0] * held for held in second]
    for j in (1, 2):
        moved = earlier_parts(second, j, zeros)
        total = [have + cols[j] * held for have, held in zip(total, moved)]
    return total


def project_kernel(
    units,
    series_ref,
    cot_ref,
    w_in_ref,
    w_out_ref,
    taps_ref,
    skip_one_ref,
    skip_two_ref,
    one_ref,
    two_ref,
    out_ref,
    params_ref,
):
    _, block, width = series_ref.shape
    group = width // units
    parts = block // W
    params_ref[...] = jnp.zeros(params_ref.shape, F32)
    params_ref[0:3, :] = taps_ref[...]
    params_ref[3:4, 0:width] = skip_one_ref[...]
    params_ref[4:5, 0:width] = skip_two_ref[...]
    w_in_t = w_in_ref[...].T
    w_out = w_out_ref[...]
    proj = [dot_nt(w_in_t, series_ref[0, p * W : (p + 1) * W, :]) for p in range(parts)]
    d_prod = [dot_nt(w_out, cot_ref[0, p * W : (p + 1) * W, :]) for p in range(parts)]
    second = [held[2 * width :] for held in proj]
    gate = gate_local(second, gate_taps(taps_ref))
    for p in range(parts):
        fields = [proj[p][:width], proj[p][width : 2 * width], d_prod[p] * gate[p]]
        for kind, field in enumerate(fields):
            at = (kind * parts + p) * group
            out_ref[:, at : at + group, :] = field.astype(BF16).reshape(units, group, W)

    lane = lanes_of(second[0])
    edges = jnp.where((lane >= 128) & (lane < 130), turned(second[-1], 130), 0.0)
    edges = jnp.where((lane >= 130) & (lane < 132), turned(d_prod[0], 130), edges)
    lines = [
        ref[:, q * width : (q + 1) * width]
        for ref in (one_ref, two_ref)
        for q in range(block // width)
    ]
    repeat = units // one_ref.shape[0]
    for u in range(units):
        row = u // repeat
        held = jnp.concatenate([line[row : row + 1] for line in lines], axis=0)
        held = jnp.concatenate([held, jnp.zeros((held.shape[0], W - width), F32)], axis=1)
        edge = fold(edges[u * group : (u + 1) * group])
        out_ref[u, 3 * parts * group :, :] = (held + edge).astype(BF16)


def gate_kernel(series_ref, cot_ref, w_in_ref, w_out_ref, taps_ref, out_ref):
    _, block, width = series_ref.shape
    parts = block // W
    w_two_t = w_in_ref[:, 2 * width :].T
    w_out = w_out_ref[...]
    second = [dot_nt(w_two_t, series_ref[0, p * W : (p + 1) * W, :]) for p in range(parts)]
    gate = gate_local(second, gate_taps(taps_ref))
    for p in range(parts):
        out_ref[0, p] = second[p]
        out_ref[1, p] = gate[p]
        out_ref[2, p] = dot_nt(w_out, cot_ref[0, p * W : (p + 1) * W, :])


def build_toeplitz(fields_ref, start, toep_ref):
    sources = fields_ref.shape[0]
    _, blocks, _, _ = toep_ref.shape
    slots = blocks // sources * (W // TILE)
    lane = lax.broadcasted_iota(jnp.int32, (16, TILE), 1)
    row = lax.broadcasted_iota(jnp.int32, (16, TILE), 0)
    none = jnp.zeros((16, TILE), F32)
    for m in range(2):
        behind = {}

        def shifted(tile, shift):
            moved = pltpu.roll(tile, shift, 1) if shift else tile
            ahead, behind[shift] = behind.get(shift, none), moved
            return jnp.where(lane < shift, ahead, moved) if shift else moved

        for q in range(TILE // 16):
            at = TILE + 16 * q
            toep_ref[m, 0, at : at + 16, 0:TILE] = none.astype(BF16)
        held = {}
        for s in range(sources):
            lines = fields_ref[s, start:, :].astype(F32)
            for i in range(slots):
                d, part = divmod(s * slots + i, W // TILE)
                line = lines[m * slots + i : m * slots + i + 1, :TILE]
                tile = jnp.broadcast_to(line, (16, TILE))
                for bit in (1, 2, 4, 8):
                    moved = pltpu.roll(tile, bit, 1)
                    ahead, held[bit] = held.get(bit, none), moved
                    tile = jnp.where((row & bit) != 0, jnp.where(lane < bit, ahead, moved), tile)
                for q in range(TILE // 16):
                    low = shifted(tile, 16 * q).astype(BF16)
                    at = 16 * q
                    toep_ref[m, d, at : at + 16, part * TILE : (part + 1) * TILE] = low
                    if part == 0:
                        toep_ref[m, d, TILE + at : TILE + at + 16, TILE:] = low
                    elif d + 1 < blocks:
                        toep_ref[m, d + 1, TILE + at : TILE + at + 16, 0:TILE] = low


def earlier(field, j, group):
    if j == 0:
        return field
    low, high = pltpu.roll(field[:, :TILE], j, 1), pltpu.roll(field[:, TILE:], j, 1)
    above = jnp.concatenate([jnp.zeros((group, TILE), F32), high[:-group]], axis=0)
    edge = lanes_of(low) < j
    return jnp.concatenate([jnp.where(edge, above, low), jnp.where(edge, low, high)], axis=1)


def own_lanes(f, group, width):
    lane = lax.broadcasted_iota(jnp.int32, (group, width), 1)
    channel = lax.broadcasted_iota(jnp.int32, (group, width), 0)
    return lane == f * group + channel


def pick(ref, kind, received):
    rows = received
    field = ref[:, kind * rows : (kind + 1) * rows, :]
    return field.reshape(field.shape[0] * rows, W).astype(F32)


def operator_kernel(
    units,
    fields_ref,
    taps_ref,
    out_ref,
    kept_ref,
    pad_ref,
    back_ref,
    toep_ref,
    wide_ref,
):
    sources, _, _ = out_ref.shape
    _, rows, _ = kept_ref.shape
    each = rows // sources
    start = 3 * each
    build_toeplitz(fields_ref, start, toep_ref)
    width = taps_ref.shape[1] // 3
    group = width // units
    blocks = rows // group
    u = lax.rem(lax.axis_index("seq"), units)
    mine = own_lanes(u, group, width)
    value_ref, gate_ref, y_ref, mid_ref, grad_ref, first_ref, second_ref = [
        wide_ref.at[i] for i in range(7)
    ]

    def column(values):
        col = jnp.sum(jnp.where(mine, values, 0.0), axis=1, keepdims=True)
        return jnp.broadcast_to(col, (group, W))

    def scaled(field, col):
        return (field.reshape(-1, group, W) * col[None]).reshape(field.shape)

    tap = [
        [
            column(taps_ref[j : j + 1, kind * width : (kind + 1) * width])
            for j in range(3)
        ]
        for kind in range(3)
    ]
    skip_one = column(taps_ref[3:4, 0:width])
    skip_two = column(taps_ref[4:5, 0:width])
    chunks = [slice(s * each, (s + 1) * each) for s in range(sources)]

    zeros = jnp.zeros((rows, W), BF16)
    pad_ref[0:rows, :] = zeros
    back_ref[rows : 2 * rows, :] = zeros

    def causal(order, into_ref):
        left = jnp.concatenate(
            [pad_ref[rows - group * d : 2 * rows - group * d, :] for d in range(blocks)], axis=1
        )
        into_ref[...] = dot(left, toep_ref[order].reshape(blocks * W, W))

    def anticausal(order, into_ref):
        left = jnp.concatenate(
            [back_ref[group * d : rows + group * d, :] for d in range(blocks)], axis=1
        )
        right = jnp.concatenate([toep_ref[order, d] for d in range(blocks)], axis=1)
        into_ref[...] = dot_nt(left, right)

    def put(slot, s, field, into_ref=None, at=0):
        low = field.astype(BF16)
        kept_ref[slot, chunks[s], :] = low
        if into_ref is not None:
            into_ref[at + s * each : at + (s + 1) * each, :] = low

    def short(kind, s):
        held = fields_ref[s, kind * each : (kind + 1) * each, :].astype(F32)
        if s:
            last = fields_ref[s - 1, (kind + 1) * each - group : (kind + 1) * each, :].astype(F32)
        else:
            last = jnp.zeros((group, W), F32)
        total = scaled(held, tap[kind][0])
        low, high = held[:, :TILE], held[:, TILE:]
        for j in (1, 2):
            low_j, high_j = pltpu.roll(low, j, 1), pltpu.roll(high, j, 1)
            above = jnp.concatenate([pltpu.roll(last[:, TILE:], j, 1), high_j[:-group]], axis=0)
            edge = lanes_of(low) < j
            moved = [jnp.where(edge, above, low_j), jnp.where(edge, low_j, high_j)]
            total = total + scaled(jnp.concatenate(moved, axis=1), tap[kind][j])
        return total

    edges = unfold(fields_ref[:, start:, :].astype(F32), group)
    none = jnp.zeros((1, group, W), F32)
    before = jnp.concatenate([none, edges[:-1]], axis=0)
    following = jnp.concatenate([edges[1:], none], axis=0)
    lane = lanes_of(edges)
    reach = tap[2][2] * turned(before, 128)
    reach = reach + jnp.where(lane < 1, tap[2][1] * turned(before, 127), 0.0)
    reach = jnp.where(lane < 2, turned(edges, 126) * reach, 0.0)
    for s in range(sources):
        held = fields_ref[s, 2 * each : 3 * each, :].astype(F32)
        held = jnp.concatenate([held[:group] + reach[s], held[group:]], axis=0)
        grad_ref[chunks[s], :] = held
        put(3, s, held, back_ref)
        value = short(0, s)
        value_ref[chunks[s], :] = value
        put(0, s, value, pad_ref, rows)
        gate_ref[chunks[s], :] = short(1, s)

    causal(0, first_ref)
    anticausal(1, second_ref)
    for s in range(sources):
        at = chunks[s]
        y_one = first_ref[at, :] + scaled(value_ref[at, :], skip_one)
        y_ref[at, :] = y_one
        mid = gate_ref[at, :] * y_one
        mid_ref[at, :] = mid
        put(1, s, mid, pad_ref, rows)
    causal(1, first_ref)
    for s in range(sources):
        at = chunks[s]
        d_mid = second_ref[at, :] + scaled(grad_ref[at, :], skip_two)
        grad_one = d_mid * gate_ref[at, :]
        grad_ref[at, :] = grad_one
        put(2, s, grad_one, back_ref)
        d_gate = d_mid * y_ref[at, :]
        y_ref[at, :] = d_gate
        put(5, s, d_gate)
    anticausal(0, second_ref)
    heads = []
    for s in range(sources):
        at = chunks[s]
        y_two = first_ref[at, :] + scaled(mid_ref[at, :], skip_two)
        out_ref[s, 2 * each : 3 * each, :] = y_two.astype(BF16)
        heads.append(y_two[:group])
    heads = jnp.stack(heads[1:] + [none[0]])
    edges = jnp.where(lane < 4, turned(following, 128) * turned(heads, 2), 0.0)
    edges = jnp.where(lane < 2, turned(before, 128), edges)
    out_ref[:, start:, :] = fold(edges).astype(BF16)
    for s in range(sources):
        at = chunks[s]
        d_value = second_ref[at, :] + scaled(grad_ref[at, :], skip_one)
        value_ref[at, :] = d_value
        put(4, s, d_value)

    for s in range(sources):
        for kind, ref in ((0, value_ref), (1, y_ref)):
            held = ref[chunks[s], :]
            if s + 1 < sources:
                first = ref[(s + 1) * each : (s + 1) * each + group, :]
            else:
                first = jnp.zeros((group, W), F32)
            total = scaled(held, tap[kind][0])
            low, high = held[:, :TILE], held[:, TILE:]
            for j in (1, 2):
                low_j, high_j = pltpu.roll(low, TILE - j, 1), pltpu.roll(high, TILE - j, 1)
                below = jnp.concatenate([low_j[group:], pltpu.roll(first[:, :TILE], TILE - j, 1)], axis=0)
                edge = lanes_of(low) >= TILE - j
                moved = [jnp.where(edge, high_j, low_j), jnp.where(edge, below, high_j)]
                total = total + scaled(jnp.concatenate(moved, axis=1), tap[kind][j])
            out_ref[s, kind * each : (kind + 1) * each, :] = total.astype(BF16)


def gradient_kernel(units, fields_ref, kept_ref, low_ref, pad_ref, corr_ref, out_ref):
    sources, _, _ = fields_ref.shape
    _, rows, _ = kept_ref.shape
    _, length = corr_ref.shape
    width = out_ref.shape[1]
    blocks = length // W
    group = rows // blocks
    each = rows // sources
    half = W // 2
    lines = length // width

    pad_ref[rows : 2 * rows, :] = jnp.zeros((rows, W), BF16)
    row8 = lax.broadcasted_iota(jnp.int32, (8, length), 0)
    b = lax.broadcasted_iota(jnp.int32, (W, W), 0)
    r = lax.broadcasted_iota(jnp.int32, (W, W), 1)
    for m in range(2):
        pad_ref[0:rows, :] = kept_ref[2 + m]
        right = jnp.concatenate(
            [pad_ref[group * d : rows + group * d, :] for d in range(blocks)], axis=1
        )
        held = kept_ref[m].astype(F32).T.astype(BF16)
        corr_ref[...] = dot(held, right)
        corr_ref[:, 0:W] = jnp.where(r >= b, corr_ref[:, 0:W], 0.0)
        total = None
        for q in range(half // 8):
            upper = corr_ref[half + 8 * q : half + 8 * q + 8, :]
            upper = jnp.concatenate([upper[:, half:], jnp.zeros((8, half), F32)], axis=1)
            both = corr_ref[8 * q : 8 * q + 8, :] + upper
            if q:
                both = pltpu.roll(both, length - 8 * q, 1)
            total = both if total is None else total + both
        for bit in (1, 2, 4):
            total = jnp.where((row8 & bit) != 0, pltpu.roll(total, length - bit, 1), total)
        line = jnp.sum(total, axis=0, keepdims=True)
        for q in range(lines):
            at = m * lines + q
            out_ref[at : at + 1, :] = line[:, q * width : (q + 1) * width]

    lane = lax.broadcasted_iota(jnp.int32, (group, width), 1)
    channel = lax.broadcasted_iota(jnp.int32, (group, width), 0)
    small = [jnp.zeros((1, width), F32)] * 16

    def put(n, products):
        by_channel = jnp.sum(products.reshape(blocks, group, W), axis=0)
        col = jnp.sum(by_channel, axis=1, keepdims=True)
        mine = lane == n % units * group + channel
        small[n // units] += jnp.sum(jnp.where(mine, col, 0.0), axis=0, keepdims=True)

    for j in range(3):
        for kind in range(2):
            field = pick(fields_ref, kind, each)
            put(2 * j + kind, kept_ref[4 + kind].astype(F32) * earlier(field, j, group))
    for m in range(2):
        put(6 + m, kept_ref[2 + m].astype(F32) * kept_ref[m].astype(F32))
    out_ref[2 * lines : 2 * lines + 16, :] = jnp.concatenate(small, axis=0)
    low_ref[...] = out_ref[...].astype(BF16)


def received_field(in_ref, units, group, parts, kind, part):
    at = (kind * parts + part) * group
    return in_ref[:, at : at + group, :].reshape(units * group, W)


def partial_kernel(units, copies, in_ref, held_ref, taps_ref, series_ref, cot_ref, *refs):
    own_refs, (part_ref, product_ref, grads_ref) = refs[:copies], refs[copies:]
    _, block, width = series_ref.shape
    group = width // units
    parts = block // W
    cols = gate_taps(taps_ref)
    edges = unfold(in_ref[:, 3 * parts * group :, :].astype(F32), group).reshape(width, W)
    lane = lanes_of(edges)
    second = [held_ref[0, p] for p in range(parts)]
    gate = [held_ref[1, p] for p in range(parts)]
    gate[0] += jnp.where(lane < 2, cols[2] * edges, 0.0)
    gate[0] += jnp.where(lane < 1, cols[1] * turned(edges, W - 1), 0.0)
    around = turned(edges, W - 2)
    y_two = [received_field(in_ref, units, group, parts, 2, p).astype(F32) for p in range(parts)]
    d_gate = [held_ref[2, p] * y_two[p] for p in range(parts)]
    grads = [cols[0] * held for held in d_gate]
    for j in (1, 2):
        grads = [
            have + cols[j] * held for have, held in zip(grads, later_parts(d_gate, j, around))
        ]
    w_in_part = 0.0
    w_out_part = 0.0
    for p in range(parts):
        rows = pl.ds(p * W, W)
        product = (gate[p] * y_two[p]).astype(BF16)
        product_ref[p] = product
        low = grads[p].astype(BF16)
        grads_ref[p] = low
        field = [received_field(in_ref, units, group, parts, k, p) for k in range(2)] + [low]
        w_in_part += dot(jnp.concatenate(field, axis=0), series_ref[0, rows, :])
        w_out_part += dot(product, cot_ref[0, rows, :])

    small = jnp.zeros((width, width), F32)
    for j in range(3):
        moved = earlier_parts(second, j, around) if j else second
        col = sum(jnp.sum(d * held, axis=1, keepdims=True) for d, held in zip(d_gate, moved))
        small = jnp.where(lanes_of(small) == j, col, small)
    small = small.T[0:3]

    weights = jnp.concatenate([w_in_part, w_out_part], axis=0)
    own = own_refs[0][...].astype(F32)
    for ref in own_refs[1:]:
        own = own + ref[...].astype(F32)
    targets, sent, _ = part_ref.shape
    each = weights.shape[0] // targets
    sources = in_ref.shape[0]
    lines = (own.shape[0] - 16) // 2
    slots = lines // sources
    share = 2 * slots // copies
    mine = lax.axis_index("dp")
    spare = sent - each - share - 4
    spare = [jnp.zeros((spare, width), F32)] if spare else []
    rests = []
    for s in range(sources):
        rows = [own[order * lines + s * slots + q][None] for order in range(2) for q in range(slots)]
        held = 0.0
        for k in range(copies):
            block = jnp.concatenate(rows[k * share : (k + 1) * share], axis=0)
            held += jnp.where(mine == k, block, 0.0)
        rows = [held, own[2 * lines : 2 * lines + 1], small]
        rests.append(jnp.concatenate(rows + spare, axis=0))
    for g in range(targets):
        block = [weights[g * each : (g + 1) * each], rests[g % sources]]
        part_ref[g] = jnp.concatenate(block, axis=0).astype(BF16)


def output_kernel(units, in_ref, product_ref, grads_ref, w_in_ref, w_out_ref, out_ref, d_series_ref):
    _, block, width = out_ref.shape
    group = width // units
    parts = block // W
    w_in = w_in_ref[...]
    w_out_t = w_out_ref[...].T
    for p in range(parts):
        rows = pl.ds(p * W, W)
        out_ref[0, rows, :] = dot(w_out_t, product_ref[p]).T.astype(BF16)
        field = [received_field(in_ref, units, group, parts, k, p) for k in range(2)]
        grads = jnp.concatenate(field + [grads_ref[p]], axis=0)
        d_series_ref[0, rows, :] = dot(w_in, grads).T.astype(BF16)


def sum_kernel(in_ref, out_ref):
    targets, each, _ = out_ref.shape
    total = in_ref[0, 0:each, :].astype(F32)
    for g in range(1, targets):
        total = total + in_ref[g, 0:each, :].astype(F32)
    total = total.astype(BF16)
    for g in range(targets):
        out_ref[g] = total


def small_kernel(units, each, scale, in_ref, one_ref, two_ref, taps_ref, skip_one_ref, skip_two_ref):
    targets, _, width = in_ref.shape
    filters, block = one_ref.shape
    slots = block // width
    group = width // units
    share = 2 * slots * units // targets
    by_unit = []
    gate = 0.0
    for u in range(units):
        rows = [in_ref[g, each:, :].astype(F32) * scale for g in range(u, targets, units)]
        for held in rows:
            gate += held[share + 1 : share + 4]
        shares = [held[:share] for held in rows]
        by_unit.append(jnp.concatenate(shares + [rows[0][share : share + 1]], axis=0))
    repeat = units // filters
    for f in range(filters):
        sums = by_unit[f * repeat]
        for u in range(f * repeat + 1, (f + 1) * repeat):
            sums = sums + by_unit[u]
        for q in range(slots):
            one_ref[f : f + 1, q * width : (q + 1) * width] = sums[q : q + 1]
            two_ref[f : f + 1, q * width : (q + 1) * width] = sums[slots + q : slots + q + 1]

    row = lax.broadcasted_iota(jnp.int32, (units, width), 0)
    lane = lax.broadcasted_iota(jnp.int32, (units, width), 1)
    held = jnp.concatenate([sums[2 * slots : 2 * slots + 1] for sums in by_unit], axis=0)
    small = 0.0
    for shift in range(units):
        moved = pltpu.roll(held, shift * group, 1) if shift else held
        moved = jnp.where(lane // group == row, moved, 0.0)
        small += pltpu.roll(moved, units - shift, 0) if shift else moved
    for j in range(3):
        for kind in range(2):
            n = 2 * j + kind
            taps_ref[j : j + 1, kind * width : (kind + 1) * width] = small[n : n + 1]
    taps_ref[:, 2 * width :] = gate
    skip_one_ref[...] = small[6:7]
    skip_two_ref[...] = small[7:8]


def weight_kernel(scale, in_ref, w_in_ref, w_out_ref):
    targets, each, width = in_ref.shape
    weights = jnp.concatenate([in_ref[g].astype(F32) for g in range(targets)], axis=0) * scale
    for kind in range(3):
        w_in_ref[:, kind * width : (kind + 1) * width] = weights[kind * width : (kind + 1) * width].T
    w_out_ref[...] = weights[3 * width :]


def all_to_all(blocks, axis):
    return lax.all_to_all(blocks, axis, split_axis=0, concat_axis=0, tiled=True)


def shards(series, cotangent, w_in, w_out, taps, skip_one, skip_two, filter_one, filter_two):
    count, block, width = series.shape
    filters = filter_one.shape[0]
    sources = lax.axis_size("seq")
    copies = lax.axis_size("dp")
    length = block * sources
    units = sources // count
    group = width // units
    assert count == 1 and units >= 8 and 2 * block // width <= 16 and units % filters == 0 and block % W == 0
    blocks = length // W
    rows = blocks * group
    scale = 1.0 / math.sqrt(count * copies * length)
    shape = jax.ShapeDtypeStruct

    devices = sources * copies
    assert 2 * block // width == 8 and group in (8, 16)
    packed = 3 * (block // W) * group + 8
    skips = (skip_one.reshape(1, width), skip_two.reshape(1, width))
    fields, params = call(
        functools.partial(project_kernel, units),
        (shape((sources, packed, W), BF16), shape((8, 3 * width), F32)),
        flops=2 * block * width * 4 * width,
        moved=8 * block * width * 4,
        limit=VMEM_ALL,
    )(series, cotangent, w_in, w_out, taps, *skips, filter_one, filter_two)
    fields = all_to_all(fields, "seq")
    held = call(
        gate_kernel,
        shape((3, block // W, width, W), F32),
        flops=2 * block * width * 2 * width,
        moved=4 * 4 * block * width,
    )(series, cotangent, w_in, w_out, params)

    sent, kept = call(
        functools.partial(operator_kernel, units),
        (shape((sources, packed, W), BF16), shape((7, rows, W), BF16)),
        [
            pltpu.VMEM((2 * rows, W), BF16),
            pltpu.VMEM((2 * rows, W), BF16),
            pltpu.VMEM((2, blocks, W, W), BF16),
            pltpu.VMEM((7, rows, W), F32),
        ],
        flops=4 * 2 * rows * length * W,
        moved=2 * W * length * 2 * 2,
    )(fields, params)

    back = all_to_all(sent, "seq")

    own = call(
        functools.partial(gradient_kernel, units),
        shape((2 * (length // width) + 16, width), BF16),
        [
            pltpu.VMEM((2 * rows, W), BF16),
            pltpu.VMEM((W, length), F32),
            pltpu.VMEM((2 * (length // width) + 16, width), F32),
        ],
        flops=2 * 2 * rows * length * W,
        moved=2 * length * width * 2,
    )(fields, kept)

    each = 4 * width // devices
    around = [[(i, (i + d) % copies) for i in range(copies)] for d in range(1, copies)]
    owns = [own] + [lax.ppermute(own, "dp", route) for route in around]
    assert 2 * (block // width) % copies == 0
    sent_rows = -(-(each + 2 * (block // width) // copies + 4) // 8) * 8
    partial, product, grads = call(
        functools.partial(partial_kernel, units, copies),
        (
            shape((devices, sent_rows, width), BF16),
            shape((block // W, width, W), BF16),
            shape((block // W, width, W), BF16),
        ),
        flops=2 * block * width * 4 * width,
        moved=2 * block * width * 6,
    )(back, held, params, series, cotangent, *owns)
    partial = all_to_all(partial, ("dp", "seq"))

    output, d_series = call(
        functools.partial(output_kernel, units),
        (shape(series.shape, BF16), shape(series.shape, BF16)),
        flops=2 * block * width * 4 * width,
        moved=2 * block * width * 6,
    )(back, product, grads, w_in, w_out)

    sums = call(
        sum_kernel,
        shape((devices, each, width), BF16),
        flops=devices * each * width,
        moved=4 * devices * each * width,
    )(partial)
    sums = all_to_all(sums, ("dp", "seq"))

    grad_one, grad_two, grad_taps, grad_skip_one, grad_skip_two = call(
        functools.partial(small_kernel, units, each, scale),
        (
            shape(filter_one.shape, F32),
            shape(filter_two.shape, F32),
            shape(taps.shape, F32),
            shape((1, width), F32),
            shape((1, width), F32),
        ),
        flops=devices * sent_rows * width,
        moved=4 * devices * sent_rows * width,
    )(partial)
    grad_w_in, grad_w_out = call(
        functools.partial(weight_kernel, scale),
        (shape(w_in.shape, F32), shape(w_out.shape, F32)),
        flops=devices * each * width,
        moved=2 * devices * each * width,
    )(sums)
    return (
        output,
        d_series,
        grad_w_in,
        grad_w_out,
        grad_taps,
        grad_skip_one.reshape(width),
        grad_skip_two.reshape(width),
        grad_one,
        grad_two,
    )


def solution(mesh):
    specs = (
        P("dp", "seq", None),
        P("dp", "seq", None),
        P(),
        P(),
        P(),
        P(),
        P(),
        P(None, "seq"),
        P(None, "seq"),
    )
    return jax.shard_map(shards, mesh=mesh, in_specs=specs, out_specs=specs, check_vma=False)
```

```python
import functools
import math

import jax
import jax.numpy as jnp
from jax import lax
from jax.experimental import pallas as pl
from jax.experimental.pallas import tpu as pltpu
from jax.sharding import PartitionSpec as P

W = 256
TILE = 128
F32 = jnp.float32
BF16 = jnp.bfloat16
NT = (((1,), (1,)), ((), ()))
VMEM_LIMIT = 24 * 1024 * 1024
VMEM_ALL = 56 * 1024 * 1024


def call(body, out_shape, scratch=(), flops=0, moved=0, limit=VMEM_LIMIT, **specs):
    return pl.pallas_call(
        body,
        out_shape=out_shape,
        **specs,
        scratch_shapes=list(scratch),
        compiler_params=pltpu.CompilerParams(vmem_limit_bytes=limit),
        cost_estimate=pl.CostEstimate(flops=flops, bytes_accessed=moved, transcendentals=0),
    )


def dot(a, b):
    return jnp.dot(a, b, preferred_element_type=F32)


def dot_nt(a, b):
    return lax.dot_general(a, b, NT, preferred_element_type=F32)


def lanes_of(field):
    return lax.broadcasted_iota(jnp.int32, field.shape, field.ndim - 1)


def turned(field, shift):
    return pltpu.roll(field, shift, field.ndim - 1)


def tiles_of(parts):
    return [held[:, at : at + TILE] for held in parts for at in range(0, W, TILE)]


def parts_of(tiles):
    each = W // TILE
    return [jnp.concatenate(tiles[at : at + each], axis=1) for at in range(0, len(tiles), each)]


def fold(edges):
    total = edges[..., :8, :]
    for k in range(1, edges.shape[-2] // 8):
        total = total + turned(edges[..., 8 * k : 8 * k + 8, :], 64 * k)
    return total


def unfold(edges, group):
    pieces = [edges] + [turned(edges, W - 64 * k) for k in range(1, group // 8)]
    return jnp.concatenate(pieces, axis=edges.ndim - 2)


def earlier_parts(parts, j, before):
    moved = [turned(tile, j) for tile in tiles_of([before] + parts)]
    moved = moved[W // TILE - 1 :]
    edge = lanes_of(moved[0]) < j
    return parts_of([jnp.where(edge, ahead, tile) for ahead, tile in zip(moved, moved[1:])])


def later_parts(parts, j, behind):
    moved = [turned(tile, TILE - j) for tile in tiles_of(parts + [behind])]
    moved = moved[: len(moved) - W // TILE + 1]
    edge = lanes_of(moved[0]) >= TILE - j
    return parts_of([jnp.where(edge, following, tile) for tile, following in zip(moved, moved[1:])])


def gate_taps(taps_ref):
    width = taps_ref.shape[1] // 3
    rows = jnp.concatenate([taps_ref[0:3, 2 * width :], jnp.zeros((5, width), F32)], axis=0)
    cols = jnp.concatenate([rows] * (width // 8), axis=0).T
    return [cols[:, j : j + 1] for j in range(3)]


def gate_local(second, cols):
    zeros = jnp.zeros_like(second[0])
    total = [cols[0] * held for held in second]
    for j in (1, 2):
        moved = earlier_parts(second, j, zeros)
        total = [have + cols[j] * held for have, held in zip(total, moved)]
    return total


def project_kernel(units, *refs):
    given, (out_ref, params_ref), held, sems = refs[:9], refs[9:11], refs[11:20], refs[20]
    copies = [
        pltpu.make_async_copy(far, near, sems.at[i]) for i, (far, near) in enumerate(zip(given, held))
    ]
    for copy in copies:
        copy.start()
    for copy in copies:
        copy.wait()
    series_ref, cot_ref, w_in_ref, w_out_ref, taps_ref = held[:5]
    skip_one_ref, skip_two_ref, one_ref, two_ref = held[5:]
    _, block, width = series_ref.shape
    group = width // units
    parts = block // W
    params_ref[...] = jnp.zeros(params_ref.shape, F32)
    params_ref[0:3, :] = taps_ref[...]
    params_ref[3:4, 0:width] = skip_one_ref[...]
    params_ref[4:5, 0:width] = skip_two_ref[...]
    w_in_t = w_in_ref[...].T
    w_out = w_out_ref[...]
    proj = [dot_nt(w_in_t, series_ref[0, p * W : (p + 1) * W, :]) for p in range(parts)]
    d_prod = [dot_nt(w_out, cot_ref[0, p * W : (p + 1) * W, :]) for p in range(parts)]
    second = [held[2 * width :] for held in proj]
    gate = gate_local(second, gate_taps(taps_ref))
    for p in range(parts):
        fields = [proj[p][:width], proj[p][width : 2 * width], d_prod[p] * gate[p]]
        for kind, field in enumerate(fields):
            at = (kind * parts + p) * group
            out_ref[:, at : at + group, :] = field.astype(BF16).reshape(units, group, W)

    lane = lanes_of(second[0])
    edges = jnp.where((lane >= 128) & (lane < 130), turned(second[-1], 130), 0.0)
    edges = jnp.where((lane >= 130) & (lane < 132), turned(d_prod[0], 130), edges)
    lines = [
        ref[:, q * width : (q + 1) * width]
        for ref in (one_ref, two_ref)
        for q in range(block // width)
    ]
    repeat = units // one_ref.shape[0]
    for u in range(units):
        row = u // repeat
        held = jnp.concatenate([line[row : row + 1] for line in lines], axis=0)
        held = jnp.concatenate([held, jnp.zeros((held.shape[0], W - width), F32)], axis=1)
        edge = fold(edges[u * group : (u + 1) * group])
        out_ref[u, 3 * parts * group :, :] = (held + edge).astype(BF16)


def gate_kernel(series_ref, cot_ref, w_in_ref, w_out_ref, taps_ref, out_ref):
    _, block, width = series_ref.shape
    parts = block // W
    w_two_t = w_in_ref[:, 2 * width :].T
    w_out = w_out_ref[...]
    second = [dot_nt(w_two_t, series_ref[0, p * W : (p + 1) * W, :]) for p in range(parts)]
    gate = gate_local(second, gate_taps(taps_ref))
    for p in range(parts):
        out_ref[0, p] = second[p]
        out_ref[1, p] = gate[p]
        out_ref[2, p] = dot_nt(w_out, cot_ref[0, p * W : (p + 1) * W, :])


def build_toeplitz(fields_ref, start, toep_ref):
    sources = fields_ref.shape[0]
    _, blocks, _, _ = toep_ref.shape
    slots = blocks // sources * (W // TILE)
    lane = lax.broadcasted_iota(jnp.int32, (16, TILE), 1)
    row = lax.broadcasted_iota(jnp.int32, (16, TILE), 0)
    none = jnp.zeros((16, TILE), F32)
    for m in range(2):
        behind = {}

        def shifted(tile, shift):
            moved = pltpu.roll(tile, shift, 1) if shift else tile
            ahead, behind[shift] = behind.get(shift, none), moved
            return jnp.where(lane < shift, ahead, moved) if shift else moved

        for q in range(TILE // 16):
            at = TILE + 16 * q
            toep_ref[m, 0, at : at + 16, 0:TILE] = none.astype(BF16)
        held = {}
        for s in range(sources):
            lines = fields_ref[s, start:, :].astype(F32)
            for i in range(slots):
                d, part = divmod(s * slots + i, W // TILE)
                line = lines[m * slots + i : m * slots + i + 1, :TILE]
                tile = jnp.broadcast_to(line, (16, TILE))
                for bit in (1, 2, 4, 8):
                    moved = pltpu.roll(tile, bit, 1)
                    ahead, held[bit] = held.get(bit, none), moved
                    tile = jnp.where((row & bit) != 0, jnp.where(lane < bit, ahead, moved), tile)
                for q in range(TILE // 16):
                    low = shifted(tile, 16 * q).astype(BF16)
                    at = 16 * q
                    toep_ref[m, d, at : at + 16, part * TILE : (part + 1) * TILE] = low
                    if part == 0:
                        toep_ref[m, d, TILE + at : TILE + at + 16, TILE:] = low
                    elif d + 1 < blocks:
                        toep_ref[m, d + 1, TILE + at : TILE + at + 16, 0:TILE] = low


def earlier(field, j, group):
    if j == 0:
        return field
    low, high = pltpu.roll(field[:, :TILE], j, 1), pltpu.roll(field[:, TILE:], j, 1)
    above = jnp.concatenate([jnp.zeros((group, TILE), F32), high[:-group]], axis=0)
    edge = lanes_of(low) < j
    return jnp.concatenate([jnp.where(edge, above, low), jnp.where(edge, low, high)], axis=1)


def own_lanes(f, group, width):
    lane = lax.broadcasted_iota(jnp.int32, (group, width), 1)
    channel = lax.broadcasted_iota(jnp.int32, (group, width), 0)
    return lane == f * group + channel


def pick(ref, kind, received):
    rows = received
    field = ref[:, kind * rows : (kind + 1) * rows, :]
    return field.reshape(field.shape[0] * rows, W).astype(F32)


def operator_kernel(
    units,
    fields_ref,
    taps_ref,
    out_ref,
    kept_ref,
    pad_ref,
    back_ref,
    toep_ref,
    wide_ref,
):
    sources, _, _ = out_ref.shape
    _, rows, _ = kept_ref.shape
    each = rows // sources
    start = 3 * each
    build_toeplitz(fields_ref, start, toep_ref)
    width = taps_ref.shape[1] // 3
    group = width // units
    blocks = rows // group
    u = lax.rem(lax.axis_index("seq"), units)
    mine = own_lanes(u, group, width)
    value_ref, gate_ref, y_ref, mid_ref, grad_ref, first_ref, second_ref = [
        wide_ref.at[i] for i in range(7)
    ]

    def column(values):
        col = jnp.sum(jnp.where(mine, values, 0.0), axis=1, keepdims=True)
        return jnp.broadcast_to(col, (group, W))

    def scaled(field, col):
        return (field.reshape(-1, group, W) * col[None]).reshape(field.shape)

    tap = [
        [
            column(taps_ref[j : j + 1, kind * width : (kind + 1) * width])
            for j in range(3)
        ]
        for kind in range(3)
    ]
    skip_one = column(taps_ref[3:4, 0:width])
    skip_two = column(taps_ref[4:5, 0:width])
    chunks = [slice(s * each, (s + 1) * each) for s in range(sources)]

    zeros = jnp.zeros((rows, W), BF16)
    pad_ref[0:rows, :] = zeros
    back_ref[rows : 2 * rows, :] = zeros

    def causal(order, into_ref):
        left = jnp.concatenate(
            [pad_ref[rows - group * d : 2 * rows - group * d, :] for d in range(blocks)], axis=1
        )
        into_ref[...] = dot(left, toep_ref[order].reshape(blocks * W, W))

    def anticausal(order, into_ref):
        left = jnp.concatenate(
            [back_ref[group * d : rows + group * d, :] for d in range(blocks)], axis=1
        )
        right = jnp.concatenate([toep_ref[order, d] for d in range(blocks)], axis=1)
        into_ref[...] = dot_nt(left, right)

    def put(slot, s, field, into_ref=None, at=0):
        low = field.astype(BF16)
        kept_ref[slot, chunks[s], :] = low
        if into_ref is not None:
            into_ref[at + s * each : at + (s + 1) * each, :] = low

    def short(kind, s):
        held = fields_ref[s, kind * each : (kind + 1) * each, :].astype(F32)
        if s:
            last = fields_ref[s - 1, (kind + 1) * each - group : (kind + 1) * each, :].astype(F32)
        else:
            last = jnp.zeros((group, W), F32)
        total = scaled(held, tap[kind][0])
        low, high = held[:, :TILE], held[:, TILE:]
        for j in (1, 2):
            low_j, high_j = pltpu.roll(low, j, 1), pltpu.roll(high, j, 1)
            above = jnp.concatenate([pltpu.roll(last[:, TILE:], j, 1), high_j[:-group]], axis=0)
            edge = lanes_of(low) < j
            moved = [jnp.where(edge, above, low_j), jnp.where(edge, low_j, high_j)]
            total = total + scaled(jnp.concatenate(moved, axis=1), tap[kind][j])
        return total

    edges = unfold(fields_ref[:, start:, :].astype(F32), group)
    none = jnp.zeros((1, group, W), F32)
    before = jnp.concatenate([none, edges[:-1]], axis=0)
    following = jnp.concatenate([edges[1:], none], axis=0)
    lane = lanes_of(edges)
    reach = tap[2][2] * turned(before, 128)
    reach = reach + jnp.where(lane < 1, tap[2][1] * turned(before, 127), 0.0)
    reach = jnp.where(lane < 2, turned(edges, 126) * reach, 0.0)
    for s in range(sources):
        held = fields_ref[s, 2 * each : 3 * each, :].astype(F32)
        held = jnp.concatenate([held[:group] + reach[s], held[group:]], axis=0)
        grad_ref[chunks[s], :] = held
        put(3, s, held, back_ref)
        value = short(0, s)
        value_ref[chunks[s], :] = value
        put(0, s, value, pad_ref, rows)
        gate_ref[chunks[s], :] = short(1, s)

    causal(0, first_ref)
    anticausal(1, second_ref)
    for s in range(sources):
        at = chunks[s]
        y_one = first_ref[at, :] + scaled(value_ref[at, :], skip_one)
        y_ref[at, :] = y_one
        mid = gate_ref[at, :] * y_one
        mid_ref[at, :] = mid
        put(1, s, mid, pad_ref, rows)
    causal(1, first_ref)
    for s in range(sources):
        at = chunks[s]
        d_mid = second_ref[at, :] + scaled(grad_ref[at, :], skip_two)
        grad_one = d_mid * gate_ref[at, :]
        grad_ref[at, :] = grad_one
        put(2, s, grad_one, back_ref)
        d_gate = d_mid * y_ref[at, :]
        y_ref[at, :] = d_gate
        put(5, s, d_gate)
    anticausal(0, second_ref)
    heads = []
    for s in range(sources):
        at = chunks[s]
        y_two = first_ref[at, :] + scaled(mid_ref[at, :], skip_two)
        out_ref[s, 2 * each : 3 * each, :] = y_two.astype(BF16)
        heads.append(y_two[:group])
    heads = jnp.stack(heads[1:] + [none[0]])
    edges = jnp.where(lane < 4, turned(following, 128) * turned(heads, 2), 0.0)
    edges = jnp.where(lane < 2, turned(before, 128), edges)
    out_ref[:, start:, :] = fold(edges).astype(BF16)
    for s in range(sources):
        at = chunks[s]
        d_value = second_ref[at, :] + scaled(grad_ref[at, :], skip_one)
        value_ref[at, :] = d_value
        put(4, s, d_value)

    for s in range(sources):
        for kind, ref in ((0, value_ref), (1, y_ref)):
            held = ref[chunks[s], :]
            if s + 1 < sources:
                first = ref[(s + 1) * each : (s + 1) * each + group, :]
            else:
                first = jnp.zeros((group, W), F32)
            total = scaled(held, tap[kind][0])
            low, high = held[:, :TILE], held[:, TILE:]
            for j in (1, 2):
                low_j, high_j = pltpu.roll(low, TILE - j, 1), pltpu.roll(high, TILE - j, 1)
                below = jnp.concatenate([low_j[group:], pltpu.roll(first[:, :TILE], TILE - j, 1)], axis=0)
                edge = lanes_of(low) >= TILE - j
                moved = [jnp.where(edge, high_j, low_j), jnp.where(edge, below, high_j)]
                total = total + scaled(jnp.concatenate(moved, axis=1), tap[kind][j])
            out_ref[s, kind * each : (kind + 1) * each, :] = total.astype(BF16)


def gradient_kernel(units, fields_ref, kept_ref, low_ref, pad_ref, corr_ref, out_ref):
    sources, _, _ = fields_ref.shape
    _, rows, _ = kept_ref.shape
    _, length = corr_ref.shape
    width = out_ref.shape[1]
    blocks = length // W
    group = rows // blocks
    each = rows // sources
    half = W // 2
    lines = length // width

    pad_ref[rows : 2 * rows, :] = jnp.zeros((rows, W), BF16)
    row8 = lax.broadcasted_iota(jnp.int32, (8, length), 0)
    b = lax.broadcasted_iota(jnp.int32, (W, W), 0)
    r = lax.broadcasted_iota(jnp.int32, (W, W), 1)
    for m in range(2):
        pad_ref[0:rows, :] = kept_ref[2 + m]
        right = jnp.concatenate(
            [pad_ref[group * d : rows + group * d, :] for d in range(blocks)], axis=1
        )
        held = kept_ref[m].astype(F32).T.astype(BF16)
        corr_ref[...] = dot(held, right)
        corr_ref[:, 0:W] = jnp.where(r >= b, corr_ref[:, 0:W], 0.0)
        total = None
        for q in range(half // 8):
            upper = corr_ref[half + 8 * q : half + 8 * q + 8, :]
            upper = jnp.concatenate([upper[:, half:], jnp.zeros((8, half), F32)], axis=1)
            both = corr_ref[8 * q : 8 * q + 8, :] + upper
            if q:
                both = pltpu.roll(both, length - 8 * q, 1)
            total = both if total is None else total + both
        for bit in (1, 2, 4):
            total = jnp.where((row8 & bit) != 0, pltpu.roll(total, length - bit, 1), total)
        line = jnp.sum(total, axis=0, keepdims=True)
        for q in range(lines):
            at = m * lines + q
            out_ref[at : at + 1, :] = line[:, q * width : (q + 1) * width]

    lane = lax.broadcasted_iota(jnp.int32, (group, width), 1)
    channel = lax.broadcasted_iota(jnp.int32, (group, width), 0)
    small = [jnp.zeros((1, width), F32)] * 16

    def put(n, products):
        by_channel = jnp.sum(products.reshape(blocks, group, W), axis=0)
        col = jnp.sum(by_channel, axis=1, keepdims=True)
        mine = lane == n % units * group + channel
        small[n // units] += jnp.sum(jnp.where(mine, col, 0.0), axis=0, keepdims=True)

    for j in range(3):
        for kind in range(2):
            field = pick(fields_ref, kind, each)
            put(2 * j + kind, kept_ref[4 + kind].astype(F32) * earlier(field, j, group))
    for m in range(2):
        put(6 + m, kept_ref[2 + m].astype(F32) * kept_ref[m].astype(F32))
    out_ref[2 * lines : 2 * lines + 16, :] = jnp.concatenate(small, axis=0)
    low_ref[...] = out_ref[...].astype(BF16)


def received_field(in_ref, units, group, parts, kind, part):
    at = (kind * parts + part) * group
    return in_ref[:, at : at + group, :].reshape(units * group, W)


def partial_kernel(units, copies, in_ref, held_ref, taps_ref, series_ref, cot_ref, *refs):
    own_refs, (part_ref, product_ref, grads_ref) = refs[:copies], refs[copies:]
    _, block, width = series_ref.shape
    group = width // units
    parts = block // W
    cols = gate_taps(taps_ref)
    edges = unfold(in_ref[:, 3 * parts * group :, :].astype(F32), group).reshape(width, W)
    lane = lanes_of(edges)
    second = [held_ref[0, p] for p in range(parts)]
    gate = [held_ref[1, p] for p in range(parts)]
    gate[0] += jnp.where(lane < 2, cols[2] * edges, 0.0)
    gate[0] += jnp.where(lane < 1, cols[1] * turned(edges, W - 1), 0.0)
    around = turned(edges, W - 2)
    y_two = [received_field(in_ref, units, group, parts, 2, p).astype(F32) for p in range(parts)]
    d_gate = [held_ref[2, p] * y_two[p] for p in range(parts)]
    grads = [cols[0] * held for held in d_gate]
    for j in (1, 2):
        grads = [
            have + cols[j] * held for have, held in zip(grads, later_parts(d_gate, j, around))
        ]
    w_in_part = 0.0
    w_out_part = 0.0
    for p in range(parts):
        rows = pl.ds(p * W, W)
        product = (gate[p] * y_two[p]).astype(BF16)
        product_ref[p] = product
        low = grads[p].astype(BF16)
        grads_ref[p] = low
        field = [received_field(in_ref, units, group, parts, k, p) for k in range(2)] + [low]
        w_in_part += dot(jnp.concatenate(field, axis=0), series_ref[0, rows, :])
        w_out_part += dot(product, cot_ref[0, rows, :])

    small = jnp.zeros((width, width), F32)
    for j in range(3):
        moved = earlier_parts(second, j, around) if j else second
        col = sum(jnp.sum(d * held, axis=1, keepdims=True) for d, held in zip(d_gate, moved))
        small = jnp.where(lanes_of(small) == j, col, small)
    small = small.T[0:3]

    weights = jnp.concatenate([w_in_part, w_out_part], axis=0)
    own = own_refs[0][...].astype(F32)
    for ref in own_refs[1:]:
        own = own + ref[...].astype(F32)
    targets, sent, _ = part_ref.shape
    each = weights.shape[0] // targets
    sources = in_ref.shape[0]
    lines = (own.shape[0] - 16) // 2
    slots = lines // sources
    share = 2 * slots // copies
    mine = lax.axis_index("dp")
    spare = sent - each - share - 4
    spare = [jnp.zeros((spare, width), F32)] if spare else []
    rests = []
    for s in range(sources):
        rows = [own[order * lines + s * slots + q][None] for order in range(2) for q in range(slots)]
        held = 0.0
        for k in range(copies):
            block = jnp.concatenate(rows[k * share : (k + 1) * share], axis=0)
            held += jnp.where(mine == k, block, 0.0)
        rows = [held, own[2 * lines : 2 * lines + 1], small]
        rests.append(jnp.concatenate(rows + spare, axis=0))
    for g in range(targets):
        block = [weights[g * each : (g + 1) * each], rests[g % sources]]
        part_ref[g] = jnp.concatenate(block, axis=0).astype(BF16)


def output_kernel(units, in_ref, product_ref, grads_ref, w_in_ref, w_out_ref, out_ref, d_series_ref):
    _, block, width = out_ref.shape
    group = width // units
    parts = block // W
    w_in = w_in_ref[...]
    w_out_t = w_out_ref[...].T
    for p in range(parts):
        rows = pl.ds(p * W, W)
        out_ref[0, rows, :] = dot(w_out_t, product_ref[p]).T.astype(BF16)
        field = [received_field(in_ref, units, group, parts, k, p) for k in range(2)]
        grads = jnp.concatenate(field + [grads_ref[p]], axis=0)
        d_series_ref[0, rows, :] = dot(w_in, grads).T.astype(BF16)


def sum_kernel(in_ref, out_ref):
    targets, each, _ = out_ref.shape
    total = in_ref[0, 0:each, :].astype(F32)
    for g in range(1, targets):
        total = total + in_ref[g, 0:each, :].astype(F32)
    total = total.astype(BF16)
    for g in range(targets):
        out_ref[g] = total


def small_kernel(units, each, scale, in_ref, one_ref, two_ref, taps_ref, skip_one_ref, skip_two_ref):
    targets, _, width = in_ref.shape
    filters, block = one_ref.shape
    slots = block // width
    group = width // units
    share = 2 * slots * units // targets
    by_unit = []
    gate = 0.0
    for u in range(units):
        rows = [in_ref[g, each:, :].astype(F32) * scale for g in range(u, targets, units)]
        for held in rows:
            gate += held[share + 1 : share + 4]
        shares = [held[:share] for held in rows]
        by_unit.append(jnp.concatenate(shares + [rows[0][share : share + 1]], axis=0))
    repeat = units // filters
    for f in range(filters):
        sums = by_unit[f * repeat]
        for u in range(f * repeat + 1, (f + 1) * repeat):
            sums = sums + by_unit[u]
        for q in range(slots):
            one_ref[f : f + 1, q * width : (q + 1) * width] = sums[q : q + 1]
            two_ref[f : f + 1, q * width : (q + 1) * width] = sums[slots + q : slots + q + 1]

    row = lax.broadcasted_iota(jnp.int32, (units, width), 0)
    lane = lax.broadcasted_iota(jnp.int32, (units, width), 1)
    held = jnp.concatenate([sums[2 * slots : 2 * slots + 1] for sums in by_unit], axis=0)
    small = 0.0
    for shift in range(units):
        moved = pltpu.roll(held, shift * group, 1) if shift else held
        moved = jnp.where(lane // group == row, moved, 0.0)
        small += pltpu.roll(moved, units - shift, 0) if shift else moved
    for j in range(3):
        for kind in range(2):
            n = 2 * j + kind
            taps_ref[j : j + 1, kind * width : (kind + 1) * width] = small[n : n + 1]
    taps_ref[:, 2 * width :] = gate
    skip_one_ref[...] = small[6:7]
    skip_two_ref[...] = small[7:8]


def weight_kernel(scale, in_ref, w_in_ref, w_out_ref):
    targets, each, width = in_ref.shape
    weights = jnp.concatenate([in_ref[g].astype(F32) for g in range(targets)], axis=0) * scale
    for kind in range(3):
        w_in_ref[:, kind * width : (kind + 1) * width] = weights[kind * width : (kind + 1) * width].T
    w_out_ref[...] = weights[3 * width :]


def all_to_all(blocks, axis):
    return lax.all_to_all(blocks, axis, split_axis=0, concat_axis=0, tiled=True)


def shards(series, cotangent, w_in, w_out, taps, skip_one, skip_two, filter_one, filter_two):
    count, block, width = series.shape
    filters = filter_one.shape[0]
    sources = lax.axis_size("seq")
    copies = lax.axis_size("dp")
    length = block * sources
    units = sources // count
    group = width // units
    assert count == 1 and units >= 8 and 2 * block // width <= 16 and units % filters == 0 and block % W == 0
    blocks = length // W
    rows = blocks * group
    scale = 1.0 / math.sqrt(count * copies * length)
    shape = jax.ShapeDtypeStruct

    devices = sources * copies
    assert 2 * block // width == 8 and group in (8, 16)
    packed = 3 * (block // W) * group + 8
    skips = (skip_one.reshape(1, width), skip_two.reshape(1, width))
    given = (series, cotangent, w_in, w_out, taps, *skips, filter_one, filter_two)
    fields, params = call(
        functools.partial(project_kernel, units),
        (shape((sources, packed, W), BF16), shape((8, 3 * width), F32)),
        [pltpu.VMEM(x.shape, x.dtype) for x in given] + [pltpu.SemaphoreType.DMA((len(given),))],
        flops=2 * block * width * 4 * width,
        moved=8 * block * width * 4,
        limit=VMEM_ALL,
        in_specs=[pl.BlockSpec(memory_space=pl.ANY)] * len(given),
    )(*given)
    fields = all_to_all(fields, "seq")
    held = call(
        gate_kernel,
        shape((3, block // W, width, W), F32),
        flops=2 * block * width * 2 * width,
        moved=4 * 4 * block * width,
    )(series, cotangent, w_in, w_out, params)

    sent, kept = call(
        functools.partial(operator_kernel, units),
        (shape((sources, packed, W), BF16), shape((7, rows, W), BF16)),
        [
            pltpu.VMEM((2 * rows, W), BF16),
            pltpu.VMEM((2 * rows, W), BF16),
            pltpu.VMEM((2, blocks, W, W), BF16),
            pltpu.VMEM((7, rows, W), F32),
        ],
        flops=4 * 2 * rows * length * W,
        moved=2 * W * length * 2 * 2,
    )(fields, params)

    back = all_to_all(sent, "seq")

    own = call(
        functools.partial(gradient_kernel, units),
        shape((2 * (length // width) + 16, width), BF16),
        [
            pltpu.VMEM((2 * rows, W), BF16),
            pltpu.VMEM((W, length), F32),
            pltpu.VMEM((2 * (length // width) + 16, width), F32),
        ],
        flops=2 * 2 * rows * length * W,
        moved=2 * length * width * 2,
    )(fields, kept)

    each = 4 * width // devices
    around = [[(i, (i + d) % copies) for i in range(copies)] for d in range(1, copies)]
    owns = [own] + [lax.ppermute(own, "dp", route) for route in around]
    assert 2 * (block // width) % copies == 0
    sent_rows = -(-(each + 2 * (block // width) // copies + 4) // 8) * 8
    partial, product, grads = call(
        functools.partial(partial_kernel, units, copies),
        (
            shape((devices, sent_rows, width), BF16),
            shape((block // W, width, W), BF16),
            shape((block // W, width, W), BF16),
        ),
        flops=2 * block * width * 4 * width,
        moved=2 * block * width * 6,
    )(back, held, params, series, cotangent, *owns)
    partial = all_to_all(partial, ("dp", "seq"))

    output, d_series = call(
        functools.partial(output_kernel, units),
        (shape(series.shape, BF16), shape(series.shape, BF16)),
        flops=2 * block * width * 4 * width,
        moved=2 * block * width * 6,
    )(back, product, grads, w_in, w_out)

    sums = call(
        sum_kernel,
        shape((devices, each, width), BF16),
        flops=devices * each * width,
        moved=4 * devices * each * width,
    )(partial)
    sums = all_to_all(sums, ("dp", "seq"))

    grad_one, grad_two, grad_taps, grad_skip_one, grad_skip_two = call(
        functools.partial(small_kernel, units, each, scale),
        (
            shape(filter_one.shape, F32),
            shape(filter_two.shape, F32),
            shape(taps.shape, F32),
            shape((1, width), F32),
            shape((1, width), F32),
        ),
        flops=devices * sent_rows * width,
        moved=4 * devices * sent_rows * width,
    )(partial)
    grad_w_in, grad_w_out = call(
        functools.partial(weight_kernel, scale),
        (shape(w_in.shape, F32), shape(w_out.shape, F32)),
        flops=devices * each * width,
        moved=2 * devices * each * width,
    )(sums)
    return (
        output,
        d_series,
        grad_w_in,
        grad_w_out,
        grad_taps,
        grad_skip_one.reshape(width),
        grad_skip_two.reshape(width),
        grad_one,
        grad_two,
    )


def solution(mesh):
    specs = (
        P("dp", "seq", None),
        P("dp", "seq", None),
        P(),
        P(),
        P(),
        P(),
        P(),
        P(None, "seq"),
        P(None, "seq"),
    )
    return jax.shard_map(shards, mesh=mesh, in_specs=specs, out_specs=specs, check_vma=False)
```
